32 devices in a mesh: dp: 4 (over z), tensor: 4 (over y, core), ctx: 2 (over x).
Axes of the slice: x: 2, y: 2, z: 4, core: 2. Of those that a mesh axis runs over, the one named last changes fastest.
Arguments:
- tokens: bfloat16 [2048, 2048], P('dp', ('tensor', 'ctx')), may hold values from -6 to 6
- targets: bfloat16 [2048, 2048], P('dp', ('tensor', 'ctx')), may hold values from -6 to 6
- ln_gain: bfloat16 [2048], P(('tensor', 'ctx')), may hold values from 0.5 to 1.5
- up_weight: bfloat16 [2048, 2, 4, 1024], P('dp', None, 'ctx', 'tensor'), may hold values from -0.125 to 0.125
- conv_weight: bfloat16 [4, 4, 1024], P(None, 'ctx', 'tensor'), may hold values from -3 to 3
- conv_bias: bfloat16 [4, 1024], P('ctx', 'tensor'), may hold values from -3 to 3
- qkv_weight: bfloat16 [3, 4, 4, 1024], P(None, None, 'ctx', 'tensor'), may hold values from -3 to 3
- gate_weight: bfloat16 [2, 4, 3, 4, 1024], P(None, None, None, 'ctx', 'tensor'), may hold values from -0.0546875 to 0.0546875
- gate_bias: bfloat16 [2, 4], replicated, may hold values from -3 to 5, as said below
- group_gain: bfloat16 [4, 1024], P('ctx', 'tensor'), may hold values from 0.099609375 to 1.8984375
- skip_gain: bfloat16 [4, 1024], P('ctx', 'tensor'), may hold values from 0.099609375 to 1.8984375
- down_weight: bfloat16 [4, 1024, 2048], P('ctx', 'tensor', 'dp'), may hold values from -0.1875 to 0.1875
- lengths: int32 [4, 3], replicated, may hold values from 64 to 256, as said below
- permutation: int32 [2048], replicated, may hold values from 0 to 2047, as said below
- valid: int32 [2048], P('dp'), may hold values from 0 to 1, as said below
Outputs:
- output: bfloat16 [2048, 2048], P('dp', ('tensor', 'ctx'))
- loss: float32 [], replicated
- grad_input: bfloat16 [2048, 2048], P('dp', ('tensor', 'ctx'))
- grad_ln_gain: float32 [2048], P(('tensor', 'ctx'))
- grad_up_weight: float32 [2048, 2, 4, 1024], P('dp', None, 'ctx', 'tensor')
- grad_conv_weight: float32 [4, 4, 1024], P(None, 'ctx', 'tensor')
- grad_conv_bias: float32 [4, 1024], P('ctx', 'tensor')
- grad_qkv_weight: float32 [3, 4, 4, 1024], P(None, None, 'ctx', 'tensor')
- grad_gate_weight: float32 [2, 4, 3, 4, 1024], P(None, None, None, 'ctx', 'tensor')
- grad_gate_bias: float32 [2, 4], replicated
- grad_group_gain: float32 [4, 1024], P('ctx', 'tensor')
- grad_skip_gain: float32 [4, 1024], P('ctx', 'tensor')
- grad_down_weight: float32 [4, 1024, 2048], P('ctx', 'tensor', 'dp')
The draws below stay inside these ranges and needn't reach their ends.
Inputs may be any that keep to these rules, and one draw needn't show every extreme that they name: `lengths`: in each pack one sequence has exactly 256 tokens and the others between one eighth and one quarter of 512. A permutation of the 2048 slots; the 512 tokens that one index of dp holds in the loader's order go to every pack, exactly 128 to each. `valid`: A 0 or 1 for each token. `gate_bias`: input gate biases (first index 0) lie from -3 to 0, forget gate biases from 1 to 5.
All inputs are finite; a program needn't handle non-finite values.
Results may differ from the reference program's by a relative error of at most 0.014.
The reference program's roundings to bfloat16 on the way count: a program that leaves them out, or rounds other values in their place, can miss the bound.
Values may be sent and summed in bfloat16 or wider, within the bound.
A program may use at most 192 MiB of HBM per device.

```python
import jax
import jax.numpy as jnp
from jax import lax

D = 2048
NH = 4
DH = 1024
CONV = 4
QKV_BLOCK = 4
SPAN = 256
SEQS = 3
TOK_GRP = 512
TOKENS = 2048
CAP = 128
LONGEST = 256
N_DP = 4


def draw_gate_bias(key, part):
    rolls = jax.random.uniform(jax.random.fold_in(key, 5), (2, NH), jnp.float32)
    low_end = jnp.array([-3.0, 1.0], jnp.float32)[:, None]
    widths = jnp.array([3.0, 4.0], jnp.float32)[:, None]
    return (low_end + widths * rolls).astype(jnp.bfloat16)


def draw_lengths(key, part):
    first, second = jax.random.split(jax.random.fold_in(key, 11))
    long_place = jax.random.randint(first, (N_DP,), 0, SEQS)
    others = jax.random.randint(second, (N_DP, SEQS), TOK_GRP // 8, TOK_GRP // 4 + 1)
    column = jnp.arange(SEQS, dtype=jnp.int32)
    return jnp.where(column[None, :] == long_place[:, None], LONGEST, others).astype(jnp.int32)


def shuffle_one(subkey):
    return jax.random.permutation(subkey, TOK_GRP).astype(jnp.int32)


def invert_one(order_row):
    return jnp.zeros((TOK_GRP,), jnp.int32).at[order_row].set(jnp.arange(TOK_GRP, dtype=jnp.int32))


def draw_permutation(key, part):
    first, second = jax.random.split(jax.random.fold_in(key, 23))
    outgoing = jax.vmap(shuffle_one)(jax.random.split(first, N_DP))
    incoming = jax.vmap(shuffle_one)(jax.random.split(second, N_DP))
    arrival = jax.vmap(invert_one)(incoming)
    source = jnp.arange(N_DP, dtype=jnp.int32)[:, None]
    target_pack = outgoing // CAP
    within = outgoing % CAP
    slot = arrival[target_pack, source * CAP + within]
    return (target_pack * TOK_GRP + slot).reshape(-1).astype(jnp.int32)


def draw_valid(key, part):
    rolls = jax.random.randint(jax.random.fold_in(key, 37), (TOKENS,), 0, 100)
    block = jnp.arange(TOKENS, dtype=jnp.int32) // TOK_GRP
    threshold = 20 + 75 * block // max(N_DP - 1, 1)
    return (rolls < threshold).astype(jnp.int32)


def block_levels(own_key, extent, cuts, smallest, top_value):
    loudness, own = 1.0, jax.random.fold_in(own_key, 6)
    for axis_at, shards_of in cuts:
        steps = jnp.exp(jax.random.uniform(jax.random.fold_in(own, axis_at), (shards_of,), jnp.float32, smallest / len(cuts), top_value / len(cuts)))
        loudness = loudness * jnp.repeat(steps, extent[axis_at] // shards_of).reshape([-1 if axis == axis_at else 1 for axis in range(len(extent))])
    return loudness


def gaussian(stream_key, shape, deviation, reach, cuts=(), held_as=jnp.bfloat16):
    loudness = block_levels(stream_key, shape, cuts, -0.22, 0.18) if cuts else 1.0
    values = jax.random.normal(stream_key, shape, jnp.float32) * deviation * loudness
    return jnp.minimum(jnp.maximum(values, -reach), reach).astype(held_as)


def setup_inputs(seed: int = 0) -> dict:
    key_list = jax.random.split(jax.random.key(seed), 16)
    return {
        "tokens": gaussian(key_list[0], (TOKENS, D), 1.0, 6.0, ((0, 4), (1, 8))),
        "targets": gaussian(key_list[1], (TOKENS, D), 1.0, 6.0, ((0, 4), (1, 8))),
        "ln_gain": jnp.clip(1.0 + 0.1 * jax.random.normal(key_list[2], (D,), jnp.float32), 0.5, 1.5).astype(jnp.bfloat16),
        "up_weight": gaussian(key_list[3], (D, 2, NH, DH), D ** -0.5, 0.125, ((0, 4), (2, 2), (3, 4))),
        "conv_weight": gaussian(key_list[4], (CONV, NH, DH), 0.5, 3.0, ((1, 2), (2, 4))),
        "conv_bias": gaussian(key_list[5], (NH, DH), 0.5, 3.0, ((0, 2), (1, 4))),
        "qkv_weight": gaussian(key_list[6], (3, QKV_BLOCK, NH, DH), QKV_BLOCK ** -0.5, 3.0, ((2, 2), (3, 4))),
        "gate_weight": gaussian(key_list[7], (2, NH, 3, NH, DH), (3 * NH * DH) ** -0.5, 0.0546875, ((3, 2), (4, 4))),
        "gate_bias": draw_gate_bias(jax.random.fold_in(key_list[15], 71), 0),
        "group_gain": jnp.clip(1.0 + 0.18 * jax.random.normal(key_list[9], (NH, DH), jnp.float32), 0.099609375, 1.8984375).astype(jnp.bfloat16),
        "skip_gain": jnp.clip(1.0 + 0.18 * jax.random.normal(key_list[10], (NH, DH), jnp.float32), 0.099609375, 1.8984375).astype(jnp.bfloat16),
        "down_weight": gaussian(key_list[11], (NH, DH, D), DH ** -0.5, 0.1875, ((0, 2), (1, 4), (2, 4))),
        "lengths": draw_lengths(jax.random.fold_in(key_list[15], 71), 0),
        "permutation": draw_permutation(jax.random.fold_in(key_list[15], 71), 0),
        "valid": draw_valid(jax.random.fold_in(key_list[15], 71), 0),
    }


@jax.custom_vjp
def low(v):
    return lax.optimization_barrier(v.astype(jnp.bfloat16)).astype(jnp.float32)

@jax.custom_vjp
def low_back(v):
    return v

def low_keep(v):
    return (low(v), None)

def low_pass(kept, grad):
    return (grad,)

def back_keep(v):
    return (v, None)

def back_low(kept, grad):
    return (low(grad),)
low.defvjp(low_keep, low_pass)
low_back.defvjp(back_keep, back_low)
NEG_FILL = -1e+30
EPSILON = 1e-05
HIGHEST = lax.Precision.HIGHEST

def segment_ids(row_lengths):
    ends = jnp.cumsum(row_lengths).astype(jnp.int32)
    places = jnp.arange(TOK_GRP, dtype=jnp.int32)
    return lax.optimization_barrier(jnp.sum((places[:, None] >= ends[None, :]).astype(jnp.int32), axis=1)).astype(jnp.int32)

def convolve(branch, conv_taps, conv_shift, segment):
    result = conv_shift[None] + conv_taps[0][None] * branch
    for offset in range(1, conv_taps.shape[0]):
        shifted = jnp.concatenate([jnp.zeros((offset,) + branch.shape[1:], branch.dtype), branch[:-offset]], axis=0)
        shifted_ids = jnp.concatenate([jnp.full((offset,), -1, jnp.int32), segment[:-offset]], axis=0)
        result = result + jnp.where((shifted_ids == segment)[:, None, None], conv_taps[offset][None] * shifted, 0.0)
    return result

def blockwise(values_in, block_map):
    row_count, head_count, channels = values_in.shape
    block_width = block_map.shape[0]
    split_values = values_in.reshape(row_count, head_count, channels // block_width, block_width)
    split_map = block_map.reshape(block_width, head_count, channels // block_width, block_width)
    return jnp.einsum('thbi,ihbj->thbj', split_values, split_map, precision=HIGHEST).reshape(row_count, head_count, channels)

def front(up_values, conv_taps, conv_shift, mix_maps, segment):
    branch = up_values[:, 0]
    gate_branch = up_values[:, 1]
    convolved = convolve(branch, conv_taps, conv_shift, segment)
    activated = convolved * jax.nn.sigmoid(convolved)
    queries = low(blockwise(activated, mix_maps[0]))
    keys_out = low(blockwise(activated, mix_maps[1]))
    values_out = low(blockwise(branch, mix_maps[2]))
    return (jnp.stack([queries, keys_out, values_out], axis=1), activated, gate_branch)

def cell_block(running, block):
    memory, normalizer, stabilizer, last_id = running
    queries, keys_in, values_in, in_gate, log_forget, segment = block
    length = queries.shape[0]
    score_scale = queries.shape[2] ** (-0.5)
    rising = jnp.cumsum(log_forget, axis=0).T
    gate_in = in_gate.T
    position = jnp.arange(length)
    allowed = (segment[:, None] == segment[None, :]) & (position[:, None] >= position[None, :])
    logits = jnp.where(allowed[None], rising[:, :, None] - rising[:, None, :] + gate_in[:, None, :], NEG_FILL)
    carried = jnp.where((segment == last_id)[None, :], rising + stabilizer[:, None], NEG_FILL)
    row_top = jnp.maximum(lax.optimization_barrier(jnp.max(logits, axis=2)), carried)
    scores = jnp.einsum('thd,shd->hts', queries, keys_in, precision=HIGHEST)
    weights = scores * score_scale * jnp.exp(logits - row_top[:, :, None])
    decay_in = jnp.exp(carried - row_top)
    through = jnp.einsum('thd,hdv->htv', queries, memory, precision=HIGHEST)
    inner_sum = jnp.einsum('hts,shv->htv', weights, values_in, precision=HIGHEST)
    numerator = inner_sum + score_scale * decay_in[:, :, None] * through
    denominator = lax.optimization_barrier(jnp.sum(weights, axis=2)) + score_scale * decay_in * jnp.einsum('thd,hd->ht', queries, normalizer, precision=HIGHEST)
    divisor = jnp.maximum(jnp.abs(denominator), jnp.exp(-row_top))
    hidden = numerator / divisor[:, :, None]
    end_id = segment[length - 1]
    block_total = rising[:, length - 1]
    kept_log = jnp.where(last_id == end_id, block_total + stabilizer, NEG_FILL)
    added_log = jnp.where((segment == end_id)[None, :], block_total[:, None] - rising + gate_in, NEG_FILL)
    new_stab = jnp.maximum(kept_log, lax.optimization_barrier(jnp.max(added_log, axis=1)))
    kept_weight = jnp.exp(kept_log - new_stab)
    added_weight = jnp.exp(added_log - new_stab[:, None])
    weighted_keys = keys_in * added_weight.T[:, :, None]
    memory = kept_weight[:, None, None] * memory + jnp.einsum('shd,shv->hdv', weighted_keys, values_in, precision=HIGHEST)
    normalizer = kept_weight[:, None] * normalizer + jnp.einsum('shd,hs->hd', keys_in, added_weight, precision=HIGHEST)
    return ((memory, normalizer, new_stab, end_id), jnp.transpose(hidden, (1, 0, 2)))

def run_cell(queries, keys_in, values_in, in_gate, log_forget, segment):
    row_count, head_count, key_depth = queries.shape
    value_depth = values_in.shape[2]
    block_count = row_count // SPAN
    blocks = (queries.reshape(block_count, SPAN, head_count, key_depth), keys_in.reshape(block_count, SPAN, head_count, key_depth), values_in.reshape(block_count, SPAN, head_count, value_depth), in_gate.reshape(block_count, SPAN, head_count), log_forget.reshape(block_count, SPAN, head_count), segment.reshape(block_count, SPAN))
    initial = (jnp.zeros((head_count, key_depth, value_depth), queries.dtype), jnp.zeros((head_count, key_depth), queries.dtype), jnp.full((head_count,), NEG_FILL, queries.dtype), jnp.int32(-1))
    final_state, hidden = lax.scan(jax.checkpoint(cell_block), initial, blocks)
    return hidden.reshape(row_count, head_count, value_depth)

def group_forward(params, row_block, segment):
    ln_g, up_w, conv_w, conv_b, mix_w, gate_w, gate_b, group_g, skip_g, down_w = params
    row_mean = lax.optimization_barrier(jnp.mean(row_block, axis=1, keepdims=True))
    row_var = lax.optimization_barrier(jnp.mean(row_block * row_block, axis=1, keepdims=True)) - row_mean * row_mean
    x_hat = (row_block - row_mean) * lax.rsqrt(row_var + EPSILON)
    normed = low(x_hat * ln_g[None])
    up_values = low(low_back(jnp.dot(normed, up_w.reshape(D, -1), precision=HIGHEST)))
    up_values = up_values.reshape(TOK_GRP, 2, NH, DH)
    projected, activated, gate_branch = front(up_values, conv_w, conv_b, mix_w, segment)
    gate_pre = jnp.einsum('tshd,goshd->tgo', projected, gate_w, precision=HIGHEST) + gate_b[None]
    hidden = run_cell(projected[:, 0], projected[:, 1], projected[:, 2], gate_pre[:, 0], jax.nn.log_sigmoid(gate_pre[:, 1]), segment)
    head_mean = lax.optimization_barrier(jnp.mean(hidden, axis=2, keepdims=True))
    head_var = lax.optimization_barrier(jnp.mean(hidden * hidden, axis=2, keepdims=True)) - head_mean * head_mean
    normal_h = (hidden - head_mean) * lax.rsqrt(head_var + EPSILON) * group_g[None]
    mixed = low((normal_h + skip_g[None] * activated) * (gate_branch * jax.nn.sigmoid(gate_branch)))
    down_out = jnp.dot(mixed.reshape(TOK_GRP, NH * DH), down_w.reshape(NH * DH, D), precision=HIGHEST)
    return low(low_back(row_block + down_out))

def reference(tokens, targets, ln_gain, up_weight, conv_weight, conv_bias, qkv_weight, gate_weight, gate_bias, group_gain, skip_gain, down_weight, lengths, permutation, valid):
    inverse = jnp.zeros((TOKENS,), jnp.int32).at[permutation].set(jnp.arange(TOKENS, dtype=jnp.int32))
    segment_all = jax.vmap(segment_ids)(lengths)
    open_slots = (segment_all < SEQS).reshape(TOKENS)
    keep_load = valid.astype(jnp.float32) * open_slots[permutation].astype(jnp.float32)
    count = jnp.sum(keep_load)
    work_rows = tokens.astype(jnp.float32)[inverse].reshape(N_DP, TOK_GRP, D)
    work_goal = targets.astype(jnp.float32)[inverse].reshape(N_DP, TOK_GRP, D)
    work_keep = keep_load[inverse].reshape(N_DP, TOK_GRP)
    params = tuple((item.astype(jnp.float32) for item in (ln_gain, up_weight, conv_weight, conv_bias, qkv_weight, gate_weight, gate_bias, group_gain, skip_gain, down_weight)))

    def step(running, item):
        row_block, target_rows, keep_rows, segment = item

        def objective(theta, inputs):
            result = group_forward(theta, inputs, segment)
            difference = result - target_rows
            return (jnp.sum(keep_rows * 0.5 * lax.optimization_barrier(jnp.sum(difference * difference, axis=1))) / count, result)
        loss_part, pullback, result = jax.vjp(objective, params, row_block, has_aux=True)
        grad_params, grad_rows = pullback(jnp.asarray(TOKENS, jnp.float32))
        return ((running[0] + loss_part, jax.tree.map(jnp.add, running[1], grad_params)), (result, grad_rows))
    initial = (jnp.zeros((), jnp.float32), jax.tree.map(jnp.zeros_like, params))
    (loss, grads), (results, grad_rows) = lax.scan(step, initial, (work_rows, work_goal, work_keep, segment_all))
    output = results.reshape(TOKENS, D)[permutation].astype(jnp.bfloat16)
    grad_input = grad_rows.reshape(TOKENS, D)[permutation].astype(jnp.bfloat16)
    return (output, loss, grad_input, grads[0], grads[1], grads[2], grads[3], grads[4], grads[5], grads[6], grads[7], grads[8], grads[9])
```

```python
import jax
import jax.numpy as jnp
from jax import lax
from jax.sharding import PartitionSpec as P

NEG_FILL = -1e30
EPSILON = 1e-05
PLANE = ("tensor", "ctx")
BF = jnp.bfloat16
F32 = jnp.float32


def mm(a, b):
    return jnp.dot(a, b, preferred_element_type=F32)


def mm_nt(a, b):
    return lax.dot_general(a, b, (((1,), (1,)), ((), ())), preferred_element_type=F32)


def mm_tn(a, b):
    return lax.dot_general(a, b, (((0,), (0,)), ((), ())), preferred_element_type=F32)


def split(v):
    high = lax.reduce_precision(v, 8, 7)
    return high.astype(BF), (v - high).astype(BF)


def two(v, b, product):
    high, rest = split(v)
    return product(high, b) + product(rest, b)


def shift_down(v, offset):
    return jnp.concatenate([jnp.zeros((offset,) + v.shape[1:], v.dtype), v[:-offset]], axis=0)


def shift_up(v, offset):
    return jnp.concatenate([v[offset:], jnp.zeros((offset,) + v.shape[1:], v.dtype)], axis=0)


def shards(
    tokens,
    targets,
    ln_gain,
    up_weight,
    conv_weight,
    conv_bias,
    qkv_weight,
    gate_weight,
    gate_bias,
    group_gain,
    skip_gain,
    down_weight,
    lengths,
    permutation,
    valid,
):
    rows, own_width = tokens.shape
    dp_count = lax.axis_size("dp")
    tensor_count = lax.axis_size("tensor")
    ctx_count = lax.axis_size("ctx")
    spread = tensor_count * ctx_count
    width = own_width * spread
    dp = lax.axis_index("dp")
    ctx = lax.axis_index("ctx")
    plane = lax.axis_index("tensor") * ctx_count + ctx
    heads, chan = up_weight.shape[2], up_weight.shape[3]
    local = heads * chan
    all_heads = gate_weight.shape[1]
    head_width = chan * tensor_count
    all_rows = rows * dp_count
    cap = rows // dp_count
    block = up_weight.shape[0]

    up_cell = lax.all_gather(up_weight[:, 0].reshape(block, local), "dp", axis=0, tiled=True)
    up_gate = lax.all_gather(up_weight[:, 1].reshape(block, local), "dp", axis=0, tiled=True)
    down_all = lax.all_gather(down_weight.reshape(local, -1), "dp", axis=0, tiled=False)

    place = jnp.arange(rows, dtype=jnp.int32)
    own_perm = lax.dynamic_slice_in_dim(permutation, dp * rows, rows)
    dest = own_perm // rows
    earlier = (dest[:, None] == dest[None, :]) & (place[:, None] > place[None, :])
    code = dest * cap + jnp.sum(earlier.astype(jnp.int32), axis=1)
    send_map = (place[:, None] == code[None, :]).astype(BF)
    by_source = permutation.reshape(dp_count, rows)
    mine = by_source // rows == dp
    before = (place[:, None] < place[None, :]).astype(BF)
    rank = mm(mine.astype(BF), before).astype(jnp.int32)
    hit = mine[:, None, :] & (rank[:, None, :] == jnp.arange(cap, dtype=jnp.int32)[None, :, None])
    slot_of = jnp.sum(jnp.where(hit, (by_source - dp * rows)[:, None, :], 0), axis=2).reshape(-1)
    recv_map = (place[:, None] == slot_of[None, :]).astype(BF)

    ends_all = jnp.cumsum(lengths, axis=1)
    ends = lax.dynamic_index_in_dim(ends_all, dp, 0, keepdims=False)
    segment = jnp.sum((place[:, None] >= ends[None, :]).astype(jnp.int32), axis=1)
    seg_col = segment[:, None]
    valid_all = lax.all_gather(valid, "dp", axis=0, tiled=True)
    total_of = jnp.sum(
        jnp.where(
            (permutation // rows)[:, None] == jnp.arange(dp_count, dtype=jnp.int32)[None, :],
            ends_all[:, -1][None, :],
            0,
        ),
        axis=1,
    )
    count = jnp.sum(jnp.where(permutation % rows < total_of, valid_all, 0)).astype(F32)

    payload = jnp.concatenate(
        [tokens, targets, jnp.broadcast_to(valid[:, None], (rows, 128)).astype(BF)], axis=1
    )
    sent = mm(send_map, payload).astype(BF)
    arrived = lax.all_to_all(sent, "dp", split_axis=0, concat_axis=0, tiled=True)
    placed = mm(recv_map, arrived).astype(BF)
    work = placed[:, :own_width]
    goal = placed[:, own_width : 2 * own_width].astype(F32)
    keep = placed[:, 2 * own_width : 2 * own_width + 1].astype(F32) * (
        seg_col < lengths.shape[1]
    ).astype(F32)

    work_full = lax.all_gather(work, PLANE, axis=1, tiled=True).astype(F32)
    gain_full = lax.all_gather(ln_gain, PLANE, axis=0, tiled=True).astype(F32)
    row_mean = jnp.mean(work_full, axis=1, keepdims=True)
    row_var = jnp.mean(work_full * work_full, axis=1, keepdims=True) - row_mean * row_mean
    row_rstd = lax.rsqrt(row_var + EPSILON)
    normed = ((work_full - row_mean) * row_rstd * gain_full[None]).astype(BF)
    own_x = work.astype(F32)
    x_hat = (own_x - row_mean) * row_rstd

    branch_low = mm(normed, up_cell).astype(BF)
    branch = branch_low.astype(F32)
    taps = conv_weight.astype(F32).reshape(-1, local)
    tap_count = taps.shape[0]
    linked = [None] + [
        jnp.concatenate([jnp.full((j,), -1, jnp.int32), segment[:-j]])[:, None] == seg_col
        for j in range(1, tap_count)
    ]
    conv = conv_bias.astype(F32).reshape(1, local) + taps[0][None] * branch
    for j in range(1, tap_count):
        conv = conv + jnp.where(linked[j], taps[j][None] * shift_down(branch, j), 0.0)
    sig = jax.nn.sigmoid(conv)
    act = conv * sig
    width_of_map = qkv_weight.shape[1]
    cin = jnp.arange(chan, dtype=jnp.int32)
    same_map = cin[:, None] // width_of_map == cin[None, :] // width_of_map
    maps = [
        [
            jnp.where(same_map, jnp.tile(qkv_weight[s, :, h], (chan // width_of_map, 1)), 0).astype(BF)
            for h in range(heads)
        ]
        for s in range(3)
    ]

    def head_of(v, h):
        return v[:, h * chan : (h + 1) * chan]

    def per_head(parts):
        return jnp.concatenate(parts, axis=1)

    q = per_head([two(head_of(act, h), maps[0][h], mm) for h in range(heads)]).astype(BF)
    k = per_head([two(head_of(act, h), maps[1][h], mm) for h in range(heads)]).astype(BF)
    v = per_head([mm(head_of(branch_low, h), maps[2][h]) for h in range(heads)]).astype(BF)
    qkv = jnp.concatenate([q, k, v], axis=1)
    gates_w = gate_weight.reshape(2 * all_heads, -1)
    pre_part = mm_nt(gates_w, qkv)
    pre = lax.psum(pre_part, PLANE) + gate_bias.astype(F32).reshape(-1, 1)
    own_pre = lax.dynamic_slice_in_dim(
        pre.reshape(2, all_heads, rows), ctx * heads, heads, 1
    )
    in_gate, forget = own_pre[0], own_pre[1]
    log_forget = jax.nn.log_sigmoid(forget)
    rising = jnp.cumsum(log_forget, axis=1)
    score_part = jnp.stack([mm_nt(head_of(q, h), head_of(k, h)) for h in range(heads)])
    scores = lax.psum(score_part, "tensor")
    allowed = (seg_col == segment[None, :]) & (place[:, None] >= place[None, :])
    scale = head_width**-0.5
    hidden, weights, decays, inv_r, dens, live = [], [], [], [], [], []
    for h in range(heads):
        logit = jnp.where(
            allowed, rising[h][:, None] + (in_gate[h] - rising[h])[None, :], NEG_FILL
        )
        top = jnp.max(logit, axis=1, keepdims=True)
        decay = jnp.where(allowed, jnp.exp(logit - top), 0.0) * scale
        weight = scores[h] * decay
        den = jnp.sum(weight, axis=1, keepdims=True)
        floor = jnp.exp(-top)
        inv = 1.0 / jnp.maximum(jnp.abs(den), floor)
        weight_low = weight.astype(BF)
        hidden.append(mm(weight_low, head_of(v, h)) * inv)
        weights.append(weight)
        decays.append(decay)
        inv_r.append(inv)
        dens.append(den)
        live.append(jnp.abs(den) > floor)
    hidden_all = per_head(hidden)
    moments = lax.psum(
        jnp.stack(
            [jnp.stack([jnp.sum(hh, axis=1), jnp.sum(hh * hh, axis=1)]) for hh in hidden]
        ),
        "tensor",
    ) / head_width
    h_mean = [moments[h, 0][:, None] for h in range(heads)]
    h_rstd = [
        lax.rsqrt(moments[h, 1][:, None] - h_mean[h] * h_mean[h] + EPSILON) for h in range(heads)
    ]
    h_hat = per_head([(hidden[h] - h_mean[h]) * h_rstd[h] for h in range(heads)])

    gate_branch = mm(normed, up_gate).astype(BF).astype(F32)
    group = group_gain.astype(F32).reshape(1, local)
    skip = skip_gain.astype(F32).reshape(1, local)
    gate_sig = jax.nn.sigmoid(gate_branch)
    silu = gate_branch * gate_sig
    inner = h_hat * group + skip * act
    mixed = (inner * silu).astype(BF)
    down_part = jnp.concatenate([mm(mixed, down_all[z]) for z in range(dp_count)], axis=1)
    down_out = lax.psum_scatter(down_part.astype(BF), PLANE, scatter_dimension=1, tiled=True)
    result = (own_x + down_out.astype(F32)).astype(BF)
    difference = result.astype(F32) - goal
    loss_part = jnp.sum(keep * 0.5 * jnp.sum(difference * difference, axis=1, keepdims=True))
    loss = lax.psum(loss_part, ("dp", "tensor", "ctx")) / count
    grad_work = (all_rows / count * keep * difference).astype(BF)
    grad_full = lax.all_gather(grad_work, PLANE, axis=1, tiled=True)

    grad_down = jnp.concatenate(
        [mm_tn(mixed, grad_full[:, z * block : (z + 1) * block]) for z in range(dp_count)], axis=0
    )
    down_owned = lax.psum_scatter(grad_down.astype(BF), "dp", scatter_dimension=0, tiled=True)
    grad_mixed = sum(
        mm_nt(grad_full[:, z * block : (z + 1) * block], down_all[z]) for z in range(dp_count)
    )
    grad_inner = grad_mixed * silu
    grad_gate_branch = grad_mixed * inner * (gate_sig + silu * (1.0 - gate_sig))
    g_gate_low = grad_gate_branch.astype(BF)
    grad_up_gate = mm_tn(normed, g_gate_low)
    up_gate_owned = lax.psum_scatter(grad_up_gate.astype(BF), "dp", scatter_dimension=0, tiled=True)
    grad_skip = jnp.sum(grad_inner * act, axis=0)
    grad_group = jnp.sum(grad_inner * h_hat, axis=0)
    grad_act = grad_inner * skip
    u = grad_inner * group
    u_moments = lax.psum(
        jnp.stack(
            [
                jnp.stack(
                    [
                        jnp.sum(head_of(u, h), axis=1),
                        jnp.sum(head_of(u, h) * head_of(h_hat, h), axis=1),
                    ]
                )
                for h in range(heads)
            ]
        ),
        "tensor",
    )
    d_num, d_den, radial = [], [], []
    for h in range(heads):
        mean_u = u_moments[h, 0][:, None] / head_width
        sum_ux = u_moments[h, 1][:, None]
        d_hidden = h_rstd[h] * (head_of(u, h) - mean_u - head_of(h_hat, h) * (sum_ux / head_width))
        rho = sum_ux * (EPSILON * h_rstd[h] * h_rstd[h])
        d_num.append((d_hidden * inv_r[h]).astype(BF))
        d_den.append(jnp.where(live[h], jnp.where(dens[h] > 0.0, -rho, rho) * inv_r[h], 0.0))
        radial.append(rho)
    dw_part = jnp.stack([mm_nt(d_num[h], head_of(v, h)) for h in range(heads)])
    dw = lax.psum(dw_part, "tensor")
    grad_q, grad_k, grad_v, pre_grads = [], [], [], []
    for h in range(heads):
        full = dw[h] + d_den[h]
        exact = jnp.where(live[h], 0.0, radial[h])
        noisy = jnp.sum(full * weights[h], axis=1, keepdims=True)
        square = jnp.sum(weights[h] * weights[h], axis=1, keepdims=True)
        full = full - weights[h] * ((noisy - exact) / jnp.where(square > 0.0, square, 1.0))
        d_score = (full * decays[h]).astype(BF)
        d_logit = full * weights[h]
        over_rows = jnp.sum(d_logit, axis=1)
        over_cols = jnp.sum(d_logit, axis=0)
        grad_q.append(mm(d_score, head_of(k, h)))
        grad_k.append(mm_tn(d_score, head_of(q, h)))
        grad_v.append(mm_tn(weights[h].astype(BF), d_num[h]))
        delta = over_rows - over_cols
        d_forget = jnp.sum(delta) - jnp.cumsum(delta) + delta
        pre_grads.append(
            jnp.stack([over_cols, d_forget * (1.0 - jax.nn.sigmoid(forget[h]))])
        )
    own_grads = jnp.stack(pre_grads, axis=1)
    pre_grad = (
        lax.all_gather(own_grads, "ctx", axis=1, tiled=True).reshape(2 * all_heads, rows)
    )
    grad_gate_bias = jnp.sum(pre_grad, axis=1).reshape(2, all_heads)
    grad_proj = jnp.concatenate(grad_q + grad_k + grad_v, axis=1) + two(
        pre_grad.T, gates_w, mm
    )
    grad_gate_weight = two(pre_grad, qkv, mm).reshape(gate_weight.shape)
    gq, gk, gv = (grad_proj[:, s * local : (s + 1) * local] for s in range(3))

    grad_maps = []
    act_low = act.astype(BF)
    gq_low, gk_low, gv_low = gq.astype(BF), gk.astype(BF), gv.astype(BF)
    for left, right in ((act_low, gq_low), (act_low, gk_low), (branch_low, gv_low)):
        per = []
        for h in range(heads):
            dense = jnp.where(same_map, mm_tn(head_of(left, h), head_of(right, h)), 0.0)
            per.append(jnp.sum(dense.reshape(chan // width_of_map, width_of_map, chan), axis=0))
        grad_maps.append(jnp.stack(per, axis=1))
    grad_qkv = jnp.stack(grad_maps)
    grad_act = grad_act + per_head(
        [
            mm_nt(head_of(gq_low, h), maps[0][h]) + mm_nt(head_of(gk_low, h), maps[1][h])
            for h in range(heads)
        ]
    )
    grad_conv = grad_act * (sig + act * (1.0 - sig))
    grad_branch = per_head([mm_nt(head_of(gv_low, h), maps[2][h]) for h in range(heads)])
    grad_branch = grad_branch + taps[0][None] * grad_conv
    grad_taps = [jnp.sum(grad_conv * branch, axis=0)]
    for j in range(1, tap_count):
        kept = jnp.where(linked[j], grad_conv, 0.0)
        grad_branch = grad_branch + taps[j][None] * shift_up(kept, j)
        grad_taps.append(jnp.sum(kept * shift_down(branch, j), axis=0))
    g_cell_low = grad_branch.astype(BF)
    grad_up_cell = mm_tn(normed, g_cell_low)
    up_cell_owned = lax.psum_scatter(grad_up_cell.astype(BF), "dp", scatter_dimension=0, tiled=True)
    grad_normed_part = mm_nt(g_cell_low, up_cell) + mm_nt(g_gate_low, up_gate)
    grad_normed = lax.psum_scatter(
        grad_normed_part.astype(BF), PLANE, scatter_dimension=1, tiled=True
    ).astype(F32)
    ln_float = ln_gain.astype(F32)[None]
    grad_scaled = grad_normed * ln_float
    grad_ln = jnp.sum(grad_normed * x_hat, axis=0)
    lines = lax.psum(
        jnp.stack([jnp.sum(grad_scaled, axis=1), jnp.sum(grad_scaled * x_hat, axis=1)]), PLANE
    )
    grad_x = row_rstd * (
        grad_scaled - lines[0][:, None] / width - x_hat * (lines[1][:, None] / width)
    )
    grad_slot = (grad_work.astype(F32) + grad_x).astype(BF)
    back = mm_tn(recv_map, jnp.concatenate([result, grad_slot], axis=1)).astype(BF)
    home = lax.all_to_all(back, "dp", split_axis=0, concat_axis=0, tiled=True)
    out_rows = mm_tn(send_map, home).astype(BF)

    small = [
        grad_ln,
        jnp.stack(grad_taps).reshape(-1),
        jnp.sum(grad_conv, axis=0),
        grad_qkv.reshape(-1),
        grad_gate_weight.reshape(-1),
        grad_gate_bias.reshape(-1),
        grad_group,
        grad_skip,
    ]
    sizes = [s.shape[0] for s in small]
    summed = lax.psum(jnp.concatenate(small), "dp")
    pieces, at = [], 0
    for size in sizes:
        pieces.append(summed[at : at + size])
        at += size
    grad_up = jnp.stack(
        [
            up_cell_owned.astype(F32).reshape(block, heads, chan),
            up_gate_owned.astype(F32).reshape(block, heads, chan),
        ],
        axis=1,
    )
    return (
        out_rows[:, :own_width],
        loss,
        out_rows[:, own_width:],
        pieces[0],
        grad_up,
        pieces[1].reshape(conv_weight.shape),
        pieces[2].reshape(conv_bias.shape),
        pieces[3].reshape(qkv_weight.shape),
        pieces[4].reshape(gate_weight.shape),
        pieces[5].reshape(gate_bias.shape),
        pieces[6].reshape(group_gain.shape),
        pieces[7].reshape(skip_gain.shape),
        down_owned.astype(F32).reshape(down_weight.shape),
    )


def solution(mesh):
    return jax.shard_map(
        shards,
        mesh=mesh,
        in_specs=(
            P("dp", ("tensor", "ctx")),
            P("dp", ("tensor", "ctx")),
            P(("tensor", "ctx")),
            P("dp", None, "ctx", "tensor"),
            P(None, "ctx", "tensor"),
            P("ctx", "tensor"),
            P(None, None, "ctx", "tensor"),
            P(None, None, None, "ctx", "tensor"),
            P(),
            P("ctx", "tensor"),
            P("ctx", "tensor"),
            P("ctx", "tensor", "dp"),
            P(),
            P(),
            P("dp"),
        ),
        out_specs=(
            P("dp", ("tensor", "ctx")),
            P(),
            P("dp", ("tensor", "ctx")),
            P(("tensor", "ctx")),
            P("dp", None, "ctx", "tensor"),
            P(None, "ctx", "tensor"),
            P("ctx", "tensor"),
            P(None, None, "ctx", "tensor"),
            P(None, None, None, "ctx", "tensor"),
            P(),
            P("ctx", "tensor"),
            P("ctx", "tensor"),
            P("ctx", "tensor", "dp"),
        ),
        check_vma=False,
    )
```

```python
import itertools
import types

import jax
import jax.numpy as jnp
from jax import lax
from jax.experimental import pallas as pl
from jax.experimental.pallas import tpu as pltpu
from jax.sharding import PartitionSpec as P

NEG_FILL = -1e30
EPSILON = 1e-05
BF = jnp.bfloat16
F32 = jnp.float32
MESH = pl.DeviceIdType.MESH
VMEM_LIMIT = 60 * 1024 * 1024
LINE = 128
BAND = 2


def mm(a, b):
    return jnp.dot(a, b, preferred_element_type=F32)


def mm_nt(a, b):
    return lax.dot_general(a, b, (((1,), (1,)), ((), ())), preferred_element_type=F32)


def mm_tn(a, b):
    return lax.dot_general(a, b, (((0,), (0,)), ((), ())), preferred_element_type=F32)


def split(v):
    high = v.astype(BF)
    return high, (v - high.astype(F32)).astype(BF)


def sigmoid(v):
    return 1.0 / (1.0 + jnp.exp(-v))


class Links:
    def __init__(self, send, recv, limit):
        self.send, self.recv, self.limit, self.all = send, recv, limit, []
        self.closed = 0

    def go(self, src, dst, peer):
        k = len(self.all)
        assert k < self.limit
        copy = pltpu.make_async_remote_copy(
            src_ref=src,
            dst_ref=dst,
            send_sem=self.send.at[k],
            recv_sem=self.recv.at[k],
            device_id=peer,
            device_id_type=MESH,
        )
        copy.start()
        self.all.append(copy)
        return copy

    def close(self):
        for copy in self.all[self.closed :]:
            copy.wait_send()
        self.closed = len(self.all)


class Ring:
    def __init__(self, links, own, hold, next_peer, owners):
        self.links, self.own, self.hold = links, own, hold
        self.peer, self.owners = next_peer, owners
        self.flying, self.at = None, 0

    def start(self):
        source = self.own if self.at == 0 else self.hold.at[self.owners[self.at]]
        self.flying = self.links.go(source, self.hold.at[self.owners[self.at]], self.peer)

    def step(self):
        if self.at >= len(self.owners) - 1:
            return False
        if self.flying is None:
            self.start()
        self.flying.wait_recv()
        self.at += 1
        self.flying = None
        if self.at < len(self.owners) - 1:
            self.start()
            return True
        return False

    def finish(self):
        while self.step():
            pass


def coordinates(dp_count):
    z, t, c = lax.axis_index("dp"), lax.axis_index("tensor"), lax.axis_index("ctx")
    core = lax.rem(t, 2)
    m = types.SimpleNamespace(z=z, t=t, c=c, core=core, y=lax.div(t, 2))
    m.sib_t, m.far_t, m.other_c = t + 1 - 2 * core, lax.rem(t + 2, 4), 1 - c
    m.sib, m.yn, m.xn = (z, m.sib_t, c), (z, m.far_t, c), (z, t, m.other_c)
    m.slot = t * 2 + c
    m.slot_x, m.slot_y, m.slot_d = t * 2 + m.other_c, m.far_t * 2 + c, m.far_t * 2 + m.other_c
    m.to_sib = 2 - 4 * core
    if dp_count == 4:
        def after(v):
            return lax.rem(2 * v + 1, 5)

        def before(v):
            return lax.rem(3 * v + 2, 5)
    else:
        def after(v):
            return lax.rem(v + 1, dp_count)

        def before(v):
            return lax.rem(v + dp_count - 1, dp_count)

    m.ring_next = (after(z), t, c)
    m.owners = [z]
    for _ in range(dp_count - 1):
        m.owners.append(before(m.owners[-1]))
    m.dp_peers = [(lax.rem(z + d, dp_count), t, c) for d in range(1, dp_count)]
    m.plane_peers = [
        (z, lax.rem(t + dt, 4), lax.rem(c + dc, 2))
        for dt in range(4)
        for dc in range(2)
        if dt or dc
    ]
    m.tensor_peers = [(z, lax.rem(t + dt, 4), c) for dt in range(1, 4)]
    return m


def plane_gather(links, m, full, rows):
    half = rows // 2
    first, second = pl.ds(0, half), pl.ds(half, half)

    def send(slot, part, peer):
        return links.go(full.at[slot, part], full.at[slot, part], peer)

    x_first = send(m.slot, first, m.xn)
    y_second = send(m.slot, second, m.yn)
    to_sib = links.go(full.at[m.slot], full.at[m.slot], m.sib)
    x_second = send(m.slot, second, m.xn)
    y_first = send(m.slot, first, m.yn)
    yield m.slot
    to_sib.wait_recv()
    yield m.slot + m.to_sib
    x_first.wait_recv()
    d_first = send(m.slot_x, first, m.yn)
    y_second.wait_recv()
    d_second = send(m.slot_y, second, m.xn)
    x_second.wait_recv()
    sib_x = links.go(full.at[m.slot_x], full.at[m.slot_x], m.sib)
    yield m.slot_x
    y_first.wait_recv()
    sib_y = links.go(full.at[m.slot_y], full.at[m.slot_y], m.sib)
    yield m.slot_y
    sib_x.wait_recv()
    yield m.slot_x + m.to_sib
    d_first.wait_recv()
    d_second.wait_recv()
    sib_d = links.go(full.at[m.slot_d], full.at[m.slot_d], m.sib)
    yield m.slot_d
    sib_y.wait_recv()
    yield m.slot_y + m.to_sib
    sib_d.wait_recv()
    yield m.slot_d + m.to_sib


def to_lanes(columns, rows):
    lane = lax.broadcasted_iota(jnp.int32, (rows, 128), 1)
    out = jnp.zeros((rows, 128), F32)
    for j, column in enumerate(columns):
        out = jnp.where(lane == j, column, out)
    return out.T[:8]


def to_columns(lines):
    rows = lines.shape[1]
    return jnp.concatenate([lines, jnp.zeros((120, rows), F32)], axis=0).T


def push_sum(links, m, lines, box, peers, own_place, count):
    box[own_place] = lines
    copies = [links.go(box.at[own_place], box.at[own_place], peer) for peer in peers]

    def finish():
        for copy in copies:
            copy.wait_recv()
        total = box[0]
        for k in range(1, count):
            total = total + box[k]
        return total

    return finish


def prefix_lanes(v):
    width = v.shape[1]
    lane = lax.broadcasted_iota(jnp.int32, v.shape, 1)
    step = 1
    while step < width:
        v = v + jnp.where(lane >= step, pltpu.roll(v, step, 1), 0.0)
        step *= 2
    return v


def band(rows):
    out, at = [], 0
    for i in range(rows // LINE):
        low = max(0, i - BAND)
        out.append((i, low, at, i - low + 1))
        at += i - low + 1
    return out, at


def wide(ref, h, at, width):
    return jnp.concatenate([ref[h, at + k] for k in range(width)], axis=1)


def plane_scatter(links, m, part, b, rows):
    half = rows // 2
    first, second = pl.ds(0, half), pl.ds(half, half)
    own_k = m.y * 2 + m.c
    far_y = 1 - m.y
    copies = []
    for k in range(4):
        b.out[k] = part(k // 2, 1 - m.core, k % 2).astype(BF)
        copies.append(links.go(b.out.at[k], b.into.at[k], m.sib))
    for k in range(4):
        b.acc[k] = part(k // 2, m.core, k % 2)
    for k in range(4):
        copies[k].wait_recv()
        b.acc[k] += b.into[k].astype(F32)
    copies = []
    for y in range(2):
        b.small_out[y] = b.acc[y * 2 + m.other_c, first].astype(BF)
        copies.append(links.go(b.small_out.at[y], b.small_in.at[y], m.xn))
    for x in range(2):
        b.small_out[2 + x] = b.acc[far_y * 2 + x, second].astype(BF)
        copies.append(links.go(b.small_out.at[2 + x], b.small_in.at[2 + x], m.yn))
    for k in range(4):
        copies[k].wait_recv()
    for y in range(2):
        b.acc[y * 2 + m.c, first] += b.small_in[y].astype(F32)
    for x in range(2):
        b.acc[m.y * 2 + x, second] += b.small_in[2 + x].astype(F32)
    b.small_out[4] = b.acc[far_y * 2 + m.c, first].astype(BF)
    to_y = links.go(b.small_out.at[4], b.small_in.at[4], m.yn)
    b.small_out[5] = b.acc[m.y * 2 + m.other_c, second].astype(BF)
    to_x = links.go(b.small_out.at[5], b.small_in.at[5], m.xn)
    to_y.wait_recv()
    to_x.wait_recv()
    b.acc[own_k, first] += b.small_in[4].astype(F32)
    b.acc[own_k, second] += b.small_in[5].astype(F32)
    return own_k


def forward(b, m, links, shape):
    rows, local, chan, n_dp, block, wide_d = shape
    cap, heads = rows // n_dp, local // chan
    width = 8 * wide_d
    scale = (4 * chan) ** -0.5
    blocks, n_blocks = band(rows)
    low_rows = pl.ds(0, rows)

    partners = m.plane_peers + m.dp_peers
    barrier = pltpu.get_barrier_semaphore()
    for peer in partners:
        pl.semaphore_signal(barrier, inc=1, device_id=peer, device_id_type=MESH)
    sent = mm(b.send_map[...], b.payload[...]).astype(BF)
    b.sent_tokens[...] = sent[:, :wide_d]
    b.sent_rest[...] = sent[:, wide_d:]
    own_place = pl.ds(pl.multiple_of(m.z * cap, 16), cap)
    b.full[m.slot, own_place] = b.sent_tokens[own_place]
    b.rest[own_place] = b.sent_rest[own_place]
    b.gains[m.slot] = b.ln8[...]
    b.up_cell[m.z] = b.own_cell[...]
    b.up_gate[m.z] = b.own_gate[...]
    b.down[m.z] = b.own_down[...]
    pl.semaphore_wait(barrier, len(partners))

    cell = Ring(links, b.own_cell, b.up_cell, m.ring_next, m.owners)
    gate = Ring(links, b.own_gate, b.up_gate, m.ring_next, m.owners)
    down = Ring(links, b.own_down, b.down, m.ring_next, m.owners)
    a2a, a2a_rest = [], []
    for d, peer in enumerate(m.dp_peers):
        place = pl.ds(pl.multiple_of(lax.rem(m.z + d + 1, n_dp) * cap, 16), cap)
        a2a.append(links.go(b.sent_tokens.at[place], b.full.at[m.slot, own_place], peer))
    cell.start()
    gain_copies = [
        links.go(b.gains.at[m.slot], b.gains.at[m.slot], peer) for peer in m.plane_peers
    ]
    for d, peer in enumerate(m.dp_peers):
        place = pl.ds(pl.multiple_of(lax.rem(m.z + d + 1, n_dp) * cap, 16), cap)
        a2a_rest.append(links.go(b.sent_rest.at[place], b.rest.at[own_place], peer))
    for copy in a2a:
        copy.wait_recv()

    b.sums[...] = jnp.zeros((rows, 128), F32)
    b.squares[...] = jnp.zeros((rows, 128), F32)
    arrivals = 0
    for slot in plane_gather(links, m, b.full, rows):
        columns = pl.ds(pl.multiple_of(slot * wide_d, 128), wide_d)

        def place_rows(r, carry, slot=slot, columns=columns):
            at = pl.ds(pl.multiple_of(r * LINE, LINE), LINE)
            x = mm(b.recv_map[at], b.full[slot])
            b.x_full[at, columns] = x.astype(BF)
            b.sums[at] += jnp.sum(x, axis=1, keepdims=True)
            b.squares[at] += jnp.sum(x * x, axis=1, keepdims=True)
            return carry

        lax.fori_loop(0, rows // LINE, place_rows, 0)
        arrivals += 1
        if arrivals in (3, 6):
            cell.step()
    for copy in gain_copies:
        copy.wait_recv()

    def normalise(r, carry):
        at = pl.ds(pl.multiple_of(r * 64, 64), 64)
        mean = b.sums[at][:, :1] / width
        var = b.squares[at][:, :1] / width - mean * mean
        rstd = lax.rsqrt(var + EPSILON)
        b.mean[at] = jnp.broadcast_to(mean, (64, 128))
        b.rstd[at] = jnp.broadcast_to(rstd, (64, 128))
        for i in range(8):
            x = b.x_full[at, i * wide_d : (i + 1) * wide_d].astype(F32)
            x = (x - mean) * rstd * b.gains[i, :1]
            b.normed[at, i * wide_d : (i + 1) * wide_d] = x.astype(BF)
        return carry

    lax.fori_loop(0, rows // 64, normalise, 0)

    def project(hold, ring, target):
        for s in range(n_dp):
            if s:
                while ring.at < s:
                    ring.step()
            owner = m.owners[s]
            columns = pl.ds(pl.multiple_of(owner * block, 128), block)
            product = mm(b.normed[:, columns], hold[owner])
            target[...] = product if s == 0 else target[...] + product

    project(b.up_cell, cell, b.wide_f)
    links.close()
    gate.start()
    down.start()

    place = lax.broadcasted_iota(jnp.int32, (rows, 1), 0)
    ends, total = [], 0
    for k in range(b.lengths.shape[1]):
        total = total + b.lengths[m.z, k]
        ends.append(total)
    begin = jnp.zeros((rows, 1), jnp.int32)
    for end in ends:
        begin = jnp.where(place >= end, end, begin)
    b.begin[...] = jnp.broadcast_to(begin, (rows, 128))

    def convolve(i, carry):
        at = pl.ds(pl.multiple_of(i * 128, 128), 128)
        low = b.wide_f[:, at].astype(BF)
        b.branch[:, at] = low
        x = low.astype(F32)
        since = lax.broadcasted_iota(jnp.int32, (rows, 128), 0) - b.begin[...]
        conv = b.chan_params[4:5, at] + b.chan_params[0:1, at] * x
        for j in range(1, 4):
            back = b.chan_params[j : j + 1, at] * pltpu.roll(x, j, 0)
            conv = conv + jnp.where(since >= j, back, 0.0)
        sig = sigmoid(conv)
        act = conv * sig
        b.act[:, at] = act
        b.slope[:, at] = sig + act * (1.0 - sig)
        return carry

    lax.fori_loop(0, local // 128, convolve, 0)
    r_map = lax.broadcasted_iota(jnp.int32, (chan, chan), 0) // 4
    c_map = lax.broadcasted_iota(jnp.int32, (chan, chan), 1) // 4
    same = r_map == c_map
    for s in range(3):
        for h in range(heads):
            base = b.maps8[s, h]
            dense = jnp.broadcast_to(base[None], (chan // 8, 8, chan)).reshape(chan, chan)
            b.maps[s, h] = jnp.where(same, dense, 0.0).astype(BF)
    for h in range(heads):
        at = slice(h * chan, (h + 1) * chan)
        high, rest = split(b.act[:, at])
        for s in range(2):
            b.qkv[:, s * local + h * chan : s * local + (h + 1) * chan] = (
                mm(high, b.maps[s, h]) + mm(rest, b.maps[s, h])
            ).astype(BF)
        b.qkv[:, 2 * local + h * chan : 2 * local + (h + 1) * chan] = mm(
            b.branch[:, at], b.maps[2, h]
        ).astype(BF)

    pre_part = mm_nt(b.gates_w[...], b.qkv[...])[:8]
    pre_sum = push_sum(links, m, pre_part, b.pre_box, m.plane_peers, m.slot, 8)

    def q_of(h, i):
        return b.qkv[i * LINE : (i + 1) * LINE, h * chan : (h + 1) * chan]

    def k_of(h, low, n):
        return b.qkv[
            low * LINE : (low + n) * LINE, local + h * chan : local + (h + 1) * chan
        ]

    def v_of(h, low, n):
        return b.qkv[
            low * LINE : (low + n) * LINE, 2 * local + h * chan : 2 * local + (h + 1) * chan
        ]

    b.of = (q_of, k_of, v_of)
    for h in range(heads):
        for i, low, at, n in blocks:
            tile = mm_nt(q_of(h, i), k_of(h, low, n))
            for k in range(n):
                b.score_part[h, at + k] = tile[:, k * LINE : (k + 1) * LINE]
    other = links.go(b.score_part.at[1 - m.core], b.score_in.at[0], m.sib)
    other.wait_recv()
    b.score_sum[0] = b.score_part[m.core] + b.score_in[0]
    far = links.go(b.score_sum.at[0], b.score_in.at[1], m.yn)

    pre = pre_sum() + b.gate_bias[:, :1]
    b.pre[...] = pre
    line8 = lax.broadcasted_iota(jnp.int32, (8, rows), 0)
    head = m.c * heads + m.core
    in_gate = jnp.sum(jnp.where(line8 == head, pre, 0.0), axis=0, keepdims=True)
    forget = jnp.sum(jnp.where(line8 == head + 4, pre, 0.0), axis=0, keepdims=True)
    log_forget = jnp.minimum(forget, 0.0) - jnp.log(1.0 + jnp.exp(-jnp.abs(forget)))
    rising = prefix_lanes(jnp.broadcast_to(log_forget, (8, rows)))
    rise_col = to_columns(rising)
    gate_line = in_gate - rising[:1]
    gate.step()
    far.wait_recv()
    b.score_sum[1] = b.score_sum[0] + b.score_in[1]
    for i, low, at, n in blocks:
        lines = slice(i * LINE, (i + 1) * LINE)
        t_at = i * LINE + lax.broadcasted_iota(jnp.int32, (LINE, n * LINE), 0)
        s_at = low * LINE + lax.broadcasted_iota(jnp.int32, (LINE, n * LINE), 1)
        allowed = (s_at <= t_at) & (s_at >= b.begin[lines][:, :1])
        logit = jnp.where(
            allowed, rise_col[lines][:, :1] + gate_line[:, low * LINE : (low + n) * LINE], NEG_FILL
        )
        top = jnp.max(logit, axis=1, keepdims=True)
        decay = jnp.where(allowed, jnp.exp(logit - top), 0.0) * scale
        weight = wide(b.score_sum, 1, at, n) * decay
        den = jnp.sum(weight, axis=1, keepdims=True)
        floor = jnp.exp(-top)
        inv = 1.0 / jnp.maximum(jnp.abs(den), floor)
        shares = (weight * inv).astype(BF)
        b.inv[lines] = jnp.broadcast_to(inv, (LINE, 128))
        sign = jnp.where(jnp.abs(den) > floor, jnp.where(den > 0.0, 1.0, -1.0), 0.0)
        b.sign[lines] = jnp.broadcast_to(sign, (LINE, 128))
        for k in range(n):
            b.decay[at + k] = decay[:, k * LINE : (k + 1) * LINE]
            b.weight[at + k] = weight[:, k * LINE : (k + 1) * LINE]
            b.share[m.core, at + k] = shares[:, k * LINE : (k + 1) * LINE]
    shared = links.go(b.share.at[m.core], b.share.at[m.core], m.sib)
    gate.step()
    shared.wait_recv()
    columns = []
    for h in range(heads):
        for i, low, at, n in blocks:
            lines = slice(i * LINE, (i + 1) * LINE)
            b.hidden[lines, h * chan : (h + 1) * chan] = mm(
                wide(b.share, h, at, n), v_of(h, low, n)
            )
        hid = b.hidden[:, h * chan : (h + 1) * chan]
        columns.append(jnp.sum(hid, axis=1, keepdims=True))
        columns.append(jnp.sum(hid * hid, axis=1, keepdims=True))
    moment_sum = push_sum(
        links, m, to_lanes(columns, rows), b.moment_box, m.tensor_peers, m.t, 4
    )
    gate.finish()
    down.step()
    project(b.up_gate, gate, b.wide_f)
    moments = to_columns(moment_sum()) / (4 * chan)
    for h in range(heads):
        mean = moments[:, 2 * h : 2 * h + 1]
        rstd = lax.rsqrt(moments[:, 2 * h + 1 : 2 * h + 2] - mean * mean + EPSILON)
        b.head_rstd[h] = jnp.broadcast_to(rstd, (rows, 128))
        b.head_mean[h] = jnp.broadcast_to(mean, (rows, 128))
    down.step()

    def mix(i, carry):
        at = pl.ds(pl.multiple_of(i * 128, 128), 128)
        h = lax.div(i, chan // 128)
        hat = (b.hidden[:, at] - b.head_mean[h]) * b.head_rstd[h]
        b.hidden[:, at] = hat
        low = b.wide_f[:, at].astype(BF)
        b.gate_low[:, at] = low
        g = low.astype(F32)
        inner = hat * b.chan_params[5:6, at] + b.chan_params[6:7, at] * b.act[:, at]
        b.mixed[:, at] = (inner * (g * sigmoid(g))).astype(BF)
        return carry

    lax.fori_loop(0, local // 128, mix, 0)
    down.finish()
    piece = min(block, wide_d)

    def down_part(y, core, x):
        slot = (y * 2 + core) * 2 + x
        parts = []
        for k in range(wide_d // piece):
            if block >= 2 * wide_d:
                owner = lax.div((y * 2 + core) * 2 * wide_d, block)
                parts.append(mm(b.mixed[...], b.down[owner, :, x * wide_d : (x + 1) * wide_d]))
            else:
                owner = lax.div(slot * wide_d, block) + k
                parts.append(mm(b.mixed[...], b.down[owner]))
        return jnp.concatenate(parts, axis=1)

    for copy in a2a_rest:
        copy.wait_recv()
    placed = mm(b.recv_map[...], b.rest[...])
    b.goal[...] = placed[:, :wide_d].astype(BF)
    keep = placed[:, wide_d : wide_d + 1] * (place < ends[-1]).astype(F32)
    count_part = jnp.broadcast_to(jnp.sum(keep, axis=0, keepdims=True), (8, 128))
    count_sum = push_sum(links, m, count_part, b.count_box, m.dp_peers, m.z, n_dp)
    own_k = plane_scatter(links, m, down_part, b, rows)
    count = count_sum()[:1, :1]
    own_columns = pl.ds(pl.multiple_of(m.slot * wide_d, 128), wide_d)
    result = (b.x_full[:, own_columns].astype(F32) + b.acc[own_k]).astype(BF)
    difference = result.astype(F32) - b.goal[...].astype(F32)
    per_row = jnp.sum(difference * difference, axis=1, keepdims=True)
    loss_part = jnp.sum(keep * 0.5 * per_row, axis=0, keepdims=True) / count
    b.loss_part[...] = jnp.broadcast_to(loss_part, (8, 128))
    own_gradient = ((rows * n_dp) / count * keep * difference).astype(BF)
    b.own_gradient[...] = own_gradient
    links.close()
    b.full[m.slot] = own_gradient
    b.arriving = plane_gather(links, m, b.full, rows)
    next_slot = next(b.arriving)

    b.sent_out[...] = mm_tn(b.recv_map[...], result).astype(BF)
    b.home_out[own_place] = b.sent_out[own_place]
    b.home_copies = []
    for d, peer in enumerate(m.dp_peers):
        place = pl.ds(pl.multiple_of(lax.rem(m.z + d + 1, n_dp) * cap, 16), cap)
        b.home_copies.append(links.go(b.sent_out.at[place], b.home_out.at[own_place], peer))
    b.arriving = itertools.chain([next_slot], b.arriving)


class RingSum:
    def __init__(self, links, part, hold, target, peer, owners):
        self.links, self.part, self.hold, self.target = links, part, hold, target
        self.peer, self.owners, self.at = peer, owners, 0
        self.flying = None

    def start(self):
        self.hold[0] = self.part(self.owners[1]).astype(BF)
        self.flying = self.links.go(self.hold.at[0], self.hold.at[1], self.peer)

    def step(self):
        if self.at >= len(self.owners) - 1:
            return False
        if self.flying is None:
            self.start()
        own = self.part(self.owners[(self.at + 2) % len(self.owners)])
        self.flying.wait_recv()
        self.at += 1
        total = own + self.hold[self.at].astype(F32)
        if self.at == len(self.owners) - 1:
            self.target(total)
            return False
        self.hold[self.at] = total.astype(BF)
        self.flying = self.links.go(
            self.hold.at[self.at], self.hold.at[self.at + 1], self.peer
        )
        return True

    def finish(self):
        while self.step():
            pass


def backward(b, m, links, shape):
    rows, local, chan, n_dp, block, wide_d = shape
    cap, heads = rows // n_dp, local // chan
    all_heads = 2 * heads
    width, head_width = 8 * wide_d, 4 * chan
    blocks, n_blocks = band(rows)
    q_of, k_of, v_of = b.of
    line8 = lax.broadcasted_iota(jnp.int32, (8, rows), 0)
    head = m.c * heads + m.core

    seen = 0
    for slot in b.arriving:
        g = b.full[slot]
        if block >= wide_d:
            ratio = block // wide_d
            at = pl.ds(pl.multiple_of(lax.rem(slot, ratio) * wide_d, 128), wide_d)
            product = mm_nt(g, b.down[lax.div(slot, ratio), :, at])
        else:
            ratio = wide_d // block
            product = sum(
                mm_nt(g[:, k * block : (k + 1) * block], b.down[slot * ratio + k])
                for k in range(ratio)
            )
        b.wide_f[...] = product if seen == 0 else b.wide_f[...] + product
        seen += 1

    def down_grad(owner):
        if block >= wide_d:
            ratio = block // wide_d
            return jnp.concatenate(
                [mm_tn(b.mixed[...], b.full[owner * ratio + k]) for k in range(ratio)], axis=1
            )
        ratio = wide_d // block
        at = pl.ds(pl.multiple_of(lax.rem(owner, ratio) * block, 128), block)
        return mm_tn(b.mixed[...], b.full[lax.div(owner, ratio), :, at])

    def up_grad(grads):
        def part(owner):
            at = pl.ds(pl.multiple_of(owner * block, 128), block)
            return mm_tn(b.normed[:, at], grads[...])

        return part

    def keep_down(total):
        b.grad_down[...] = total

    def keep_gate(total):
        b.grad_up[:, local:] = total

    def keep_cell(total):
        b.grad_up[:, :local] = total

    ring_down = RingSum(links, down_grad, b.ring_down, keep_down, m.ring_next, m.owners)
    ring_gate = RingSum(links, up_grad(b.g_gate), b.ring_gate, keep_gate, m.ring_next, m.owners)
    ring_cell = RingSum(links, up_grad(b.g_cell), b.ring_cell, keep_cell, m.ring_next, m.owners)
    ring_down.start()

    def unmix(i, carry):
        at = pl.ds(pl.multiple_of(i * 128, 128), 128)
        gm = b.wide_f[:, at]
        g = b.gate_low[:, at].astype(F32)
        sig = sigmoid(g)
        silu = g * sig
        hat, act = b.hidden[:, at], b.act[:, at]
        group, skip = b.chan_params[5:6, at], b.chan_params[6:7, at]
        inner = hat * group + skip * act
        b.g_gate[:, at] = (gm * inner * (sig + silu * (1.0 - sig))).astype(BF)
        gi = gm * silu
        b.small[5:6, at] = jnp.sum(gi * hat, axis=0, keepdims=True)
        b.small[6:7, at] = jnp.sum(gi * act, axis=0, keepdims=True)
        b.g_act[:, at] = gi * skip
        b.wide_f[:, at] = gi * group
        return carry

    lax.fori_loop(0, local // 128, unmix, 0)
    columns = []
    for h in range(heads):
        u = b.wide_f[:, h * chan : (h + 1) * chan]
        columns.append(jnp.sum(u, axis=1, keepdims=True))
        columns.append(
            jnp.sum(u * b.hidden[:, h * chan : (h + 1) * chan], axis=1, keepdims=True)
        )
    u_sum = push_sum(links, m, to_lanes(columns, rows), b.u_box, m.tensor_peers, m.t, 4)
    u_moments = to_columns(u_sum())
    rhos = []
    for h in range(heads):
        at = slice(h * chan, (h + 1) * chan)
        rstd = b.head_rstd[h][:, :1]
        mean_u = u_moments[:, 2 * h : 2 * h + 1] / head_width
        sum_ux = u_moments[:, 2 * h + 1 : 2 * h + 2]
        d_hidden = rstd * (b.wide_f[:, at] - mean_u - b.hidden[:, at] * (sum_ux / head_width))
        b.d_hidden[:, at] = d_hidden.astype(BF)
        rhos.append(sum_ux * (EPSILON * rstd * rstd))
    rho = jnp.where(m.core == 0, rhos[0], rhos[1])
    for h in range(heads):
        for i, low, at, n in blocks:
            tile = mm_nt(
                b.d_hidden[i * LINE : (i + 1) * LINE, h * chan : (h + 1) * chan], v_of(h, low, n)
            )
            for k in range(n):
                b.score_part[h, at + k] = tile[:, k * LINE : (k + 1) * LINE]
    other = links.go(b.score_part.at[1 - m.core], b.score_in.at[0], m.sib)
    other.wait_recv()
    b.share_out[...] = (b.score_part[m.core] + b.score_in[0]).astype(BF)
    far = links.go(b.share_out, b.share_in, m.yn)
    ring_down.step()
    ring_gate.start()
    far.wait_recv()
    b.lines[...] = jnp.zeros((8, rows), F32)
    for i, low, at, n in blocks:
        lines = slice(i * LINE, (i + 1) * LINE)
        across = slice(low * LINE, (low + n) * LINE)

        def spread(ref):
            return jnp.concatenate([ref[at + k].astype(F32) for k in range(n)], axis=1)

        inv, sign, radial = b.inv[lines][:, :1], b.sign[lines][:, :1], rho[lines]
        weight = spread(b.weight)
        full = (spread(b.share_out) + spread(b.share_in)) * inv - sign * radial * inv
        exact = jnp.where(sign == 0.0, radial, 0.0)
        noisy = jnp.sum(full * weight, axis=1, keepdims=True)
        square = jnp.sum(weight * weight, axis=1, keepdims=True)
        full = full - weight * ((noisy - exact) / jnp.where(square > 0.0, square, 1.0))
        d_score = (full * spread(b.decay)).astype(BF)
        for k in range(n):
            b.d_score[m.core, at + k] = d_score[:, k * LINE : (k + 1) * LINE]
        b.lines[0:1, across] += jnp.sum(full * weight, axis=0, keepdims=True)
        b.exact[lines] = jnp.broadcast_to(exact, (LINE, 128))
    scored = links.go(b.d_score.at[m.core], b.d_score.at[m.core], m.sib)
    over_cols = b.lines[0:1]
    over_rows = b.exact[...].T[0:1]
    delta = jnp.broadcast_to(over_rows - over_cols, (8, rows))
    after = jnp.sum(delta, axis=1, keepdims=True) - prefix_lanes(delta) + delta
    forget = jnp.sum(jnp.where(line8 == head + all_heads, b.pre[...], 0.0), axis=0, keepdims=True)
    d_forget = after[:1] / (1.0 + jnp.exp(forget))
    own_lines = jnp.where(line8 == head, over_cols, 0.0) + jnp.where(
        line8 == head + all_heads, d_forget, 0.0
    )
    head_peers = [
        m.sib,
        m.xn,
        (m.z, m.sib_t, m.other_c),
    ]
    pre_sum = push_sum(links, m, own_lines, b.grad_box, head_peers, m.c * 2 + m.core, 4)

    for h in range(heads):
        at = slice(2 * local + h * chan, 2 * local + (h + 1) * chan)
        b.g_proj[:, at] = jnp.zeros((rows, chan), F32)
        for i, low, place, n in blocks:
            d_hid = b.d_hidden[i * LINE : (i + 1) * LINE, h * chan : (h + 1) * chan]
            b.g_proj[low * LINE : (low + n) * LINE, at] += mm_tn(wide(b.share, h, place, n), d_hid)
    ring_down.step()
    scored.wait_recv()
    for h in range(heads):
        at = slice(h * chan, (h + 1) * chan)
        k_at = slice(local + h * chan, local + (h + 1) * chan)
        b.g_proj[:, k_at] = jnp.zeros((rows, chan), F32)
        for i, low, place, n in blocks:
            tile = wide(b.d_score, h, place, n)
            b.g_proj[i * LINE : (i + 1) * LINE, at] = mm(tile, k_of(h, low, n))
            b.g_proj[low * LINE : (low + n) * LINE, k_at] += mm_tn(tile, q_of(h, i))
    pre_grad = pre_sum()
    pre16 = jnp.concatenate([pre_grad, jnp.zeros((8, rows), F32)], axis=0)
    high, rest = split(pre16)
    b.g_proj[...] += mm_tn(high, b.gates_w[...]) + mm_tn(rest, b.gates_w[...])
    gate_grad = (mm(high, b.qkv[...]) + mm(rest, b.qkv[...]))[:8]
    for s in range(3):
        b.small[8 * (s + 1) : 8 * (s + 2)] = gate_grad[:, s * local : (s + 1) * local]
    b.small[32:40] = jnp.broadcast_to(jnp.sum(pre_grad, axis=1, keepdims=True), (8, local))
    ring_down.finish()
    ring_gate.step()

    r_map = lax.broadcasted_iota(jnp.int32, (chan, chan), 0) // 4
    c_map = lax.broadcasted_iota(jnp.int32, (chan, chan), 1) // 4
    same = r_map == c_map
    for h in range(heads):
        at = slice(h * chan, (h + 1) * chan)
        act_low = b.act[:, at].astype(BF)
        extra = None
        for s in range(3):
            low = b.g_proj[:, s * local + h * chan : s * local + (h + 1) * chan].astype(BF)
            left = act_low if s < 2 else b.branch[:, at]
            dense = jnp.where(same, mm_tn(left, low), 0.0)
            folded = jnp.sum(dense.reshape(chan // 8, 8, chan), axis=0)
            b.small[40 + 8 * s : 48 + 8 * s, at] = folded
            back = mm_nt(low, b.maps[s, h])
            if s == 0:
                extra = back
            elif s == 1:
                b.g_act[:, at] += extra + back
            else:
                b.wide_f[:, at] = back

    def unconvolve(i, carry):
        at = pl.ds(pl.multiple_of(i * 128, 128), 128)
        since = lax.broadcasted_iota(jnp.int32, (rows, 128), 0) - b.begin[...]
        x = b.branch[:, at].astype(F32)
        gc = b.g_act[:, at] * b.slope[:, at]
        gb = b.wide_f[:, at] + b.chan_params[0:1, at] * gc
        b.small[0:1, at] = jnp.sum(gc * x, axis=0, keepdims=True)
        b.small[4:5, at] = jnp.sum(gc, axis=0, keepdims=True)
        for j in range(1, 4):
            kept = jnp.where(since >= j, gc, 0.0)
            gb = gb + b.chan_params[j : j + 1, at] * pltpu.roll(kept, rows - j, 0)
            b.small[j : j + 1, at] = jnp.sum(kept * pltpu.roll(x, j, 0), axis=0, keepdims=True)
        b.g_cell[:, at] = gb.astype(BF)
        return carry

    lax.fori_loop(0, local // 128, unconvolve, 0)
    ring_gate.step()
    ring_cell.start()

    def up_part(y, core, x):
        slot = (y * 2 + core) * 2 + x
        if block >= wide_d:
            ratio = block // wide_d
            at = pl.ds(pl.multiple_of(lax.rem(slot, ratio) * wide_d, 16), wide_d)
            owner = lax.div(slot, ratio)
            return mm_nt(b.g_cell[...], b.up_cell[owner, at]) + mm_nt(
                b.g_gate[...], b.up_gate[owner, at]
            )
        ratio = wide_d // block
        return jnp.concatenate(
            [
                mm_nt(b.g_cell[...], b.up_cell[slot * ratio + k])
                + mm_nt(b.g_gate[...], b.up_gate[slot * ratio + k])
                for k in range(ratio)
            ],
            axis=1,
        )

    own_k = plane_scatter(links, m, up_part, b, rows)
    ring_gate.finish()
    grad_normed = b.acc[own_k]
    own_columns = pl.ds(pl.multiple_of(m.slot * wide_d, 128), wide_d)
    x_hat = (b.x_full[:, own_columns].astype(F32) - b.mean[:, :1]) * b.rstd[:, :1]
    grad_scaled = grad_normed * b.ln8[:1]
    line_sum = push_sum(
        links,
        m,
        to_lanes(
            [
                jnp.sum(grad_scaled, axis=1, keepdims=True),
                jnp.sum(grad_scaled * x_hat, axis=1, keepdims=True),
            ],
            rows,
        ),
        b.line_box,
        m.plane_peers,
        m.slot,
        8,
    )
    loss_sum = push_sum(links, m, b.loss_part[...], b.loss_box, m.plane_peers, m.slot, 8)
    b.small[7:8] = jnp.zeros((1, local), F32)
    b.small[64:72] = jnp.zeros((8, local), F32)
    b.small[7:8, :wide_d] = jnp.sum(grad_normed * x_hat, axis=0, keepdims=True)
    b.small[64:65, :128] = loss_sum()[:1]
    b.small_box[m.z] = b.small[...]
    small_copies = [
        links.go(b.small_box.at[m.z], b.small_box.at[m.z], peer) for peer in m.dp_peers
    ]
    ring_cell.step()
    lines = to_columns(line_sum()) / width
    grad_x = b.rstd[:, :1] * (grad_scaled - lines[:, :1] - x_hat * lines[:, 1:2])
    own_grad = b.own_gradient[...].astype(F32)
    grad_slot = (own_grad + grad_x).astype(BF)
    b.sent_tokens[...] = mm_tn(b.recv_map[...], grad_slot).astype(BF)
    own_place = pl.ds(pl.multiple_of(m.z * cap, 16), cap)
    b.home_grad[own_place] = b.sent_tokens[own_place]
    copies = []
    for d, peer in enumerate(m.dp_peers):
        place = pl.ds(pl.multiple_of(lax.rem(m.z + d + 1, n_dp) * cap, 16), cap)
        copies.append(links.go(b.sent_tokens.at[place], b.home_grad.at[own_place], peer))
    for copy in b.home_copies:
        copy.wait_recv()
    b.output[...] = mm_tn(b.send_map[...], b.home_out[...]).astype(BF)
    for copy in small_copies:
        copy.wait_recv()
    total = b.small_box[0]
    for k in range(1, n_dp):
        total = total + b.small_box[k]
    b.small_sum[...] = total
    for copy in copies:
        copy.wait_recv()
    b.grad_input[...] = mm_tn(b.send_map[...], b.home_grad[...]).astype(BF)
    ring_cell.finish()


def kernel(names, shape, limit, *refs):
    b = types.SimpleNamespace(**dict(zip(names, refs)))
    m = coordinates(shape[3])
    links = Links(b.send_sem, b.recv_sem, limit)
    forward(b, m, links, shape)
    backward(b, m, links, shape)
    links.close()


def shards(
    tokens,
    targets,
    ln_gain,
    up_weight,
    conv_weight,
    conv_bias,
    qkv_weight,
    gate_weight,
    gate_bias,
    group_gain,
    skip_gain,
    down_weight,
    lengths,
    permutation,
    valid,
):
    rows, wide_d = tokens.shape
    n_dp = lax.axis_size("dp")
    dp = lax.axis_index("dp")
    heads, chan = up_weight.shape[2], up_weight.shape[3]
    local = heads * chan
    cap = rows // n_dp
    block = up_weight.shape[0]
    width = 8 * wide_d

    place = jnp.arange(rows, dtype=jnp.int32)
    own_perm = lax.dynamic_slice_in_dim(permutation, dp * rows, rows)
    dest = own_perm // rows
    earlier = (dest[:, None] == dest[None, :]) & (place[:, None] > place[None, :])
    code = dest * cap + jnp.sum(earlier.astype(jnp.int32), axis=1)
    send_map = (place[:, None] == code[None, :]).astype(BF)
    by_source = permutation.reshape(n_dp, rows)
    mine = by_source // rows == dp
    before = (place[:, None] < place[None, :]).astype(BF)
    rank = mm(mine.astype(BF), before).astype(jnp.int32)
    hit = mine[:, None, :] & (rank[:, None, :] == jnp.arange(cap, dtype=jnp.int32)[None, :, None])
    slot_of = jnp.sum(jnp.where(hit, (by_source - dp * rows)[:, None, :], 0), axis=2).reshape(-1)
    recv_map = (place[:, None] == slot_of[None, :]).astype(BF)
    payload = jnp.concatenate(
        [tokens, targets, jnp.broadcast_to(valid[:, None], (rows, 128)).astype(BF)], axis=1
    )
    chan_params = jnp.concatenate(
        [
            conv_weight.reshape(4, local),
            conv_bias.reshape(1, local),
            group_gain.reshape(1, local),
            skip_gain.reshape(1, local),
            jnp.zeros((1, local), BF),
        ],
        axis=0,
    ).astype(F32)
    inputs = {
        "send_map": send_map,
        "recv_map": recv_map,
        "payload": payload,
        "ln8": jnp.broadcast_to(ln_gain[None], (8, wide_d)).astype(F32),
        "own_cell": up_weight[:, 0].reshape(block, local),
        "own_gate": up_weight[:, 1].reshape(block, local),
        "own_down": down_weight.reshape(local, block),
        "chan_params": chan_params,
        "maps8": jnp.tile(qkv_weight.transpose(0, 2, 1, 3), (1, 1, 2, 1)).astype(F32),
        "gates_w": jnp.pad(gate_weight.reshape(8, 3 * local), ((0, 8), (0, 0))),
        "gate_bias": jnp.broadcast_to(gate_bias.reshape(8, 1), (8, 128)).astype(F32),
        "lengths": lengths,
    }
    outputs = {
        "output": ((rows, wide_d), BF),
        "grad_input": ((rows, wide_d), BF),
        "small_sum": ((72, local), F32),
        "grad_up": ((block, 2 * local), F32),
        "grad_down": ((local, block), F32),
    }
    n_blocks = band(rows)[1]
    half = rows // 2
    limit = 120 + 12 * n_dp
    scratch = {
        "sent_tokens": ((rows, wide_d), BF),
        "sent_rest": ((rows, wide_d + 128), BF),
        "rest": ((rows, wide_d + 128), BF),
        "full": ((8, rows, wide_d), BF),
        "gains": ((8, 8, wide_d), F32),
        "up_cell": ((n_dp, block, local), BF),
        "up_gate": ((n_dp, block, local), BF),
        "down": ((n_dp, local, block), BF),
        "sums": ((rows, 128), F32),
        "squares": ((rows, 128), F32),
        "mean": ((rows, 128), F32),
        "rstd": ((rows, 128), F32),
        "x_full": ((rows, width), BF),
        "normed": ((rows, width), BF),
        "wide_f": ((rows, local), F32),
        "begin": ((rows, 128), jnp.int32),
        "branch": ((rows, local), BF),
        "act": ((rows, local), F32),
        "slope": ((rows, local), F32),
        "maps": ((3, heads, chan, chan), BF),
        "qkv": ((rows, 3 * local), BF),
        "pre_box": ((8, 8, rows), F32),
        "pre": ((8, rows), F32),
        "score_part": ((heads, n_blocks, LINE, LINE), F32),
        "score_in": ((2, n_blocks, LINE, LINE), F32),
        "score_sum": ((2, n_blocks, LINE, LINE), F32),
        "decay": ((n_blocks, LINE, LINE), F32),
        "weight": ((n_blocks, LINE, LINE), F32),
        "share": ((heads, n_blocks, LINE, LINE), BF),
        "inv": ((rows, 128), F32),
        "sign": ((rows, 128), F32),
        "hidden": ((rows, local), F32),
        "moment_box": ((4, 8, rows), F32),
        "head_rstd": ((heads, rows, 128), F32),
        "head_mean": ((heads, rows, 128), F32),
        "gate_low": ((rows, local), BF),
        "mixed": ((rows, local), BF),
        "goal": ((rows, wide_d), BF),
        "count_box": ((n_dp, 8, 128), F32),
        "out": ((4, rows, wide_d), BF),
        "into": ((4, rows, wide_d), BF),
        "acc": ((4, rows, wide_d), F32),
        "small_out": ((6, half, wide_d), BF),
        "small_in": ((6, half, wide_d), BF),
        "loss_part": ((8, 128), F32),
        "own_gradient": ((rows, wide_d), BF),
        "sent_out": ((rows, wide_d), BF),
        "home_out": ((rows, wide_d), BF),
        "home_grad": ((rows, wide_d), BF),
        "ring_down": ((n_dp, local, block), BF),
        "ring_gate": ((n_dp, block, local), BF),
        "ring_cell": ((n_dp, block, local), BF),
        "g_gate": ((rows, local), BF),
        "g_cell": ((rows, local), BF),
        "small": ((72, local), F32),
        "small_box": ((n_dp, 72, local), F32),
        "g_act": ((rows, local), F32),
        "u_box": ((4, 8, rows), F32),
        "d_hidden": ((rows, local), BF),
        "share_out": ((n_blocks, LINE, LINE), BF),
        "share_in": ((n_blocks, LINE, LINE), BF),
        "lines": ((8, rows), F32),
        "d_score": ((heads, n_blocks, LINE, LINE), BF),
        "exact": ((rows, 128), F32),
        "grad_box": ((4, 8, rows), F32),
        "g_proj": ((rows, 3 * local), F32),
        "line_box": ((8, 8, rows), F32),
        "loss_box": ((8, 8, 128), F32),
    }
    vmem = pl.BlockSpec(memory_space=pltpu.VMEM)
    smem = pl.BlockSpec(memory_space=pltpu.SMEM)
    names = list(inputs) + list(outputs) + list(scratch) + ["send_sem", "recv_sem"]
    results = pl.pallas_call(
        lambda *refs: kernel(names, (rows, local, chan, n_dp, block, wide_d), limit, *refs),
        out_shape=[jax.ShapeDtypeStruct(*spec) for spec in outputs.values()],
        in_specs=[smem if name == "lengths" else vmem for name in inputs],
        out_specs=[vmem] * len(outputs),
        scratch_shapes=[pltpu.VMEM(*spec) for spec in scratch.values()]
        + [pltpu.SemaphoreType.DMA((limit,)), pltpu.SemaphoreType.DMA((limit,))],
        compiler_params=pltpu.CompilerParams(
            collective_id=0, has_side_effects=True, vmem_limit_bytes=VMEM_LIMIT
        ),
    )(*inputs.values())
    o = types.SimpleNamespace(**dict(zip(outputs, results)))
    small = o.small_sum
    maps = small[40:64].reshape(3, 2, 4, heads, chan).sum(axis=1)
    return (
        o.output,
        small[64, 0],
        o.grad_input,
        small[7, :wide_d],
        o.grad_up.reshape(up_weight.shape),
        small[0:4].reshape(conv_weight.shape),
        small[4].reshape(conv_bias.shape),
        maps,
        small[8:32].reshape(3, 8, local).transpose(1, 0, 2).reshape(gate_weight.shape),
        small[32:40, 0].reshape(gate_bias.shape),
        small[5].reshape(group_gain.shape),
        small[6].reshape(skip_gain.shape),
        o.grad_down.reshape(down_weight.shape),
    )


def solution(mesh):
    return jax.shard_map(
        shards,
        mesh=mesh,
        in_specs=(
            P("dp", ("tensor", "ctx")),
            P("dp", ("tensor", "ctx")),
            P(("tensor", "ctx")),
            P("dp", None, "ctx", "tensor"),
            P(None, "ctx", "tensor"),
            P("ctx", "tensor"),
            P(None, None, "ctx", "tensor"),
            P(None, None, None, "ctx", "tensor"),
            P(),
            P("ctx", "tensor"),
            P("ctx", "tensor"),
            P("ctx", "tensor", "dp"),
            P(),
            P(),
            P("dp"),
        ),
        out_specs=(
            P("dp", ("tensor", "ctx")),
            P(),
            P("dp", ("tensor", "ctx")),
            P(("tensor", "ctx")),
            P("dp", None, "ctx", "tensor"),
            P(None, "ctx", "tensor"),
            P("ctx", "tensor"),
            P(None, None, "ctx", "tensor"),
            P(None, None, None, "ctx", "tensor"),
            P(),
            P("ctx", "tensor"),
            P("ctx", "tensor"),
            P("ctx", "tensor", "dp"),
        ),
        check_vma=False,
    )
```

```python
import itertools
import types

import jax
import jax.numpy as jnp
from jax import lax
from jax.experimental import pallas as pl
from jax.experimental.pallas import tpu as pltpu
from jax.sharding import PartitionSpec as P

NEG_FILL = -1e30
EPSILON = 1e-05
BF = jnp.bfloat16
F32 = jnp.float32
MESH = pl.DeviceIdType.MESH
VMEM_LIMIT = 62 * 1024 * 1024
LINE = 128
BAND = 2


def mm(a, b):
    return jnp.dot(a, b, preferred_element_type=F32)


def mm_nt(a, b):
    return lax.dot_general(a, b, (((1,), (1,)), ((), ())), preferred_element_type=F32)


def mm_tn(a, b):
    return lax.dot_general(a, b, (((0,), (0,)), ((), ())), preferred_element_type=F32)


def split(v):
    high = v.astype(BF)
    return high, (v - high.astype(F32)).astype(BF)


def sigmoid(v):
    return 1.0 / (1.0 + jnp.exp(-v))


class Links:
    def __init__(self, send, recv, limit):
        self.send, self.recv, self.limit = send, recv, limit
        self.used, self.open = 0, []

    def make(self, src, dst, peer):
        k = self.used
        self.used += 1
        assert k < self.limit
        copy = pltpu.make_async_remote_copy(
            src_ref=src,
            dst_ref=dst,
            send_sem=self.send.at[k],
            recv_sem=self.recv.at[k],
            device_id=peer,
            device_id_type=MESH,
        )
        return copy

    def go(self, src, dst, peer):
        copy = self.make(src, dst, peer)
        copy.start()
        self.open.append(copy)
        return copy

    def settle(self, copies):
        for copy in copies:
            copy.wait_send()
        self.open = [c for c in self.open if all(c is not done for done in copies)]

    def close(self):
        self.settle(list(self.open))


class Ring:
    def __init__(self, links, hold, part, next_peer, owners):
        self.links, self.hold, self.part = links, hold, part
        self.peer, self.owners = next_peer, owners
        self.flying, self.at = None, 0

    def start(self):
        block = self.hold.at[self.owners[self.at], self.part]
        self.flying = self.links.go(block, block, self.peer)

    def step(self):
        if self.at >= len(self.owners) - 1:
            return False
        if self.flying is None:
            self.start()
        self.flying.wait_recv()
        self.at += 1
        self.flying = None
        if self.at < len(self.owners) - 1:
            self.start()
            return True
        return False

    def last_leg(self):
        while self.at < len(self.owners) - 2:
            self.step()

    def finish(self):
        while self.step():
            pass

    def settle(self):
        self.links.close()


def when(condition, *actions):
    @pl.when(condition)
    def _():
        for action in actions:
            action()


class LineGather:
    def __init__(self, links, hold, m, count):
        self.z, self.count, self.at = m.z, count, 0
        z, last = m.z, count - 1
        self.ways = []
        for d in range(1, count):
            to_right = jnp.maximum(z - (d - 1), 0)
            to_left = jnp.minimum(z + (d - 1), last)
            self.ways.append(
                (
                    (
                        links.make(hold.at[to_right], hold.at[to_right], m.right),
                        (z < last) & (z >= d - 1),
                        z >= d,
                    ),
                    (
                        links.make(hold.at[to_left], hold.at[to_left], m.left),
                        (z > 0) & (z + d - 1 <= last),
                        z + d <= last,
                    ),
                )
            )

    def start(self):
        for copy, sends, _ in self.ways[self.at]:
            when(sends, copy.start)

    def step(self):
        if self.at >= self.count - 1:
            return
        for copy, _, receives in self.ways[self.at]:
            when(receives, copy.wait_recv)
        self.at += 1
        if self.at < self.count - 1:
            self.start()

    def last_leg(self):
        while self.at < self.count - 2:
            self.step()

    def finish(self):
        while self.at < self.count - 1:
            self.step()

    def settle(self):
        for pair in self.ways:
            for copy, sends, _ in pair:
                when(sends, copy.wait_send)


class LineSum:
    def __init__(self, links, part, hold, target, m, count):
        self.part, self.hold, self.target = part, hold, target
        self.z, self.count, self.at = m.z, count, 0
        places = (m.z, count - 1 - m.z)
        self.ways = [
            (
                places[way],
                [
                    links.make(hold.at[way, t], hold.at[way, t + 1], peer)
                    for t in range(count - 1)
                ],
            )
            for way, peer in enumerate((m.right, m.left))
        ]

    def step(self):
        t, count = self.at, self.count
        if t > count - 1:
            return
        self.at += 1
        if t == count - 1:
            total = self.part(self.z)
        for way, (place, copies) in enumerate(self.ways):
            behind = place > 0
            if t:
                when(behind & (place <= t), copies[t - 1].wait_recv)
            if t == count - 1:
                total = total + jnp.where(behind, self.hold[way, t].astype(F32), 0.0)
                continue

            def send(way=way, place=place, copies=copies, behind=behind):
                ahead = count - 1 - t
                own = self.part(self.z + ahead if way == 0 else self.z - ahead)
                if t:
                    own = own + jnp.where(behind, self.hold[way, t].astype(F32), 0.0)
                self.hold[way, t] = own.astype(BF)
                copies[t].start()

            when(place <= t, send)
        if t == count - 1:
            self.target(total)

    def settle(self):
        for place, copies in self.ways:
            for t, copy in enumerate(copies):
                when(place <= t, copy.wait_send)


class RingSum:
    def __init__(self, links, part, hold, target, m, count):
        self.links, self.part, self.hold, self.target = links, part, hold, target
        self.m, self.count, self.at = m, count, -1
        self.sent = []

    def step(self):
        if self.at >= self.count - 1:
            return
        self.at += 1
        own = self.part(self.m.owners[(self.at + 1) % self.count])
        if self.at:
            self.sent[-1].wait_recv()
            own = own + self.hold[0, self.at].astype(F32)
        if self.at == self.count - 1:
            self.target(own)
            return
        self.hold[0, self.at] = own.astype(BF)
        self.sent.append(
            self.links.go(
                self.hold.at[0, self.at], self.hold.at[0, self.at + 1], self.m.ring_next
            )
        )

    def settle(self):
        self.links.settle(self.sent)


def coordinates(dp_count):
    z, t, c = lax.axis_index("dp"), lax.axis_index("tensor"), lax.axis_index("ctx")
    core = lax.rem(t, 2)
    m = types.SimpleNamespace(z=z, t=t, c=c, core=core, y=lax.div(t, 2))
    m.sib_t, m.far_t, m.other_c = t + 1 - 2 * core, lax.rem(t + 2, 4), 1 - c
    m.sib, m.yn, m.xn = (z, m.sib_t, c), (z, m.far_t, c), (z, t, m.other_c)
    m.slot = t * 2 + c
    m.slot_x, m.slot_y, m.slot_d = t * 2 + m.other_c, m.far_t * 2 + c, m.far_t * 2 + m.other_c
    m.to_sib = 2 - 4 * core
    if dp_count == 4:
        def after(v):
            return lax.rem(2 * v + 1, 5)

        def before(v):
            return lax.rem(3 * v + 2, 5)
    else:
        def after(v):
            return lax.rem(v + 1, dp_count)

        def before(v):
            return lax.rem(v + dp_count - 1, dp_count)

    m.ring_next = (after(z), t, c)
    m.owners = [z]
    for _ in range(dp_count - 1):
        m.owners.append(before(m.owners[-1]))
    m.right = (lax.rem(z + 1, dp_count), t, c)
    m.left = (lax.rem(z + dp_count - 1, dp_count), t, c)
    m.dp_peers = [(lax.rem(z + d, dp_count), t, c) for d in range(1, dp_count)]
    m.plane_peers = [
        (z, lax.rem(t + dt, 4), lax.rem(c + dc, 2))
        for dt in range(4)
        for dc in range(2)
        if dt or dc
    ]
    m.tensor_peers = [(z, lax.rem(t + dt, 4), c) for dt in range(1, 4)]
    return m


def plane_gather(links, m, full, rows):
    half = rows // 2
    first, second = pl.ds(0, half), pl.ds(half, half)

    sent = []

    def send(slot, part, peer):
        sent.append(links.go(full.at[slot, part], full.at[slot, part], peer))
        return sent[-1]

    x_first = send(m.slot, first, m.xn)
    y_second = send(m.slot, second, m.yn)
    to_sib = send(m.slot, pl.ds(0, rows), m.sib)
    x_second = send(m.slot, second, m.xn)
    y_first = send(m.slot, first, m.yn)
    yield m.slot
    to_sib.wait_recv()
    yield m.slot + m.to_sib
    x_first.wait_recv()
    d_first = send(m.slot_x, first, m.yn)
    y_second.wait_recv()
    d_second = send(m.slot_y, second, m.xn)
    x_second.wait_recv()
    sib_x = send(m.slot_x, pl.ds(0, rows), m.sib)
    yield m.slot_x
    y_first.wait_recv()
    sib_y = send(m.slot_y, pl.ds(0, rows), m.sib)
    yield m.slot_y
    sib_x.wait_recv()
    yield m.slot_x + m.to_sib
    d_first.wait_recv()
    d_second.wait_recv()
    sib_d = send(m.slot_d, pl.ds(0, rows), m.sib)
    yield m.slot_d
    sib_y.wait_recv()
    yield m.slot_y + m.to_sib
    sib_d.wait_recv()
    yield m.slot_d + m.to_sib
    links.settle(sent)


def idle():
    pass


def to_lanes(columns, rows):
    lane = lax.broadcasted_iota(jnp.int32, (rows, 128), 1)
    out = jnp.zeros((rows, 128), F32)
    for j, column in enumerate(columns):
        out = jnp.where(lane == j, column, out)
    return out.T[:8]


def to_lanes_one(column):
    line = lax.broadcasted_iota(jnp.int32, (8, 128), 0)
    lane = lax.broadcasted_iota(jnp.int32, (8, 128), 1)
    return jnp.sum(jnp.where(line == lane, column, 0.0), axis=0, keepdims=True)


def to_columns(lines):
    rows = lines.shape[1]
    return jnp.concatenate([lines, jnp.zeros((120, rows), F32)], axis=0).T


def push_sum(links, m, lines, box, peers, own_place, count):
    box[own_place] = lines
    copies = [links.go(box.at[own_place], box.at[own_place], peer) for peer in peers]

    def finish():
        for copy in copies:
            copy.wait_recv()
        total = box[0]
        for k in range(1, count):
            total = total + box[k]
        return total

    return finish


def prefix_lanes(v):
    width = v.shape[1]
    lane = lax.broadcasted_iota(jnp.int32, v.shape, 1)
    step = 1
    while step < width:
        v = v + jnp.where(lane >= step, pltpu.roll(v, step, 1), 0.0)
        step *= 2
    return v


def band(rows):
    out, at = [], 0
    for i in range(rows // LINE):
        low = max(0, i - BAND)
        out.append((i, low, at, i - low + 1))
        at += i - low + 1
    return out, at


def wide(ref, h, at, width):
    return jnp.concatenate([ref[h, at + k] for k in range(width)], axis=1)


def plane_scatter(links, m, part, b, rows, services):
    half = rows // 2
    first, second = pl.ds(0, half), pl.ds(half, half)
    own_k = m.y * 2 + m.c
    far_y = 1 - m.y
    links.settle(b.scatter_copies)
    copies = []
    for k in range(4):
        b.out[k] = part(k // 2, 1 - m.core, k % 2).astype(BF)
        copies.append(links.go(b.out.at[k], b.into.at[k], m.sib))
    for k in range(4):
        b.acc[k] = part(k // 2, m.core, k % 2)
    b.scatter_copies = copies
    services[0]()
    for k in range(4):
        copies[k].wait_recv()
        b.acc[k] += b.into[k].astype(F32)
    copies = []
    for y in range(2):
        b.small_out[y] = b.acc[y * 2 + m.other_c, first].astype(BF)
        copies.append(links.go(b.small_out.at[y], b.small_in.at[y], m.xn))
    for x in range(2):
        b.small_out[2 + x] = b.acc[far_y * 2 + x, second].astype(BF)
        copies.append(links.go(b.small_out.at[2 + x], b.small_in.at[2 + x], m.yn))
    b.scatter_copies += copies
    services[1]()
    for k in range(4):
        copies[k].wait_recv()
    for y in range(2):
        b.acc[y * 2 + m.c, first] += b.small_in[y].astype(F32)
    for x in range(2):
        b.acc[m.y * 2 + x, second] += b.small_in[2 + x].astype(F32)
    b.small_out[4] = b.acc[far_y * 2 + m.c, first].astype(BF)
    to_y = links.go(b.small_out.at[4], b.small_in.at[4], m.yn)
    b.small_out[5] = b.acc[m.y * 2 + m.other_c, second].astype(BF)
    to_x = links.go(b.small_out.at[5], b.small_in.at[5], m.xn)
    b.scatter_copies += [to_y, to_x]
    services[2]()
    to_y.wait_recv()
    to_x.wait_recv()
    b.acc[own_k, first] += b.small_in[4].astype(F32)
    b.acc[own_k, second] += b.small_in[5].astype(F32)
    return own_k


def forward(b, m, links, shape):
    rows, local, chan, n_dp, block, wide_d = shape
    cap, heads = rows // n_dp, local // chan
    width, all_heads = 8 * wide_d, 2 * heads
    scale = (4 * chan) ** -0.5
    blocks, n_blocks = band(rows)
    low_rows = pl.ds(0, rows)

    b.scatter_copies = []
    partners = m.plane_peers + m.dp_peers
    barrier = pltpu.get_barrier_semaphore()
    for peer in partners:
        pl.semaphore_signal(barrier, inc=1, device_id=peer, device_id_type=MESH)
    own_copies = [
        pltpu.make_async_copy(own, hold.at[m.z], b.local_sem.at[k])
        for k, (own, hold) in enumerate(
            ((b.own_cell, b.up_cell), (b.own_gate, b.up_gate), (b.own_down, b.down))
        )
    ]
    for copy in own_copies:
        copy.start()
    own_place = pl.ds(pl.multiple_of(m.z * cap, 16), cap)
    b.gains[m.slot] = jnp.broadcast_to(b.ln_gain[...].astype(F32), (8, wide_d))
    b.valids[m.z] = jnp.broadcast_to(b.index[n_dp : n_dp + 1].astype(F32), (8, rows))
    count = block // 2 if block % 256 == 0 else block
    cells = [
        Ring(links, b.up_cell, pl.ds(at, count), m.ring_next, m.owners)
        for at in range(0, block, count)
    ]
    gate = Ring(links, b.up_gate, pl.ds(0, block), m.ring_next, m.owners)
    down = Ring(links, b.down, pl.ds(0, local), m.ring_next, m.owners)
    if n_dp <= 4:
        mixed_ring = LineGather(links, b.mixed_all, m, n_dp)
    else:
        mixed_ring = Ring(links, b.mixed_all, pl.ds(0, rows), m.ring_next, m.owners)
    own_copies[0].wait()
    pl.semaphore_wait(barrier, len(partners))
    cells[0].start()

    digits = rows.bit_length() - 1
    packs = max(8, n_dp)
    own = b.index[pl.ds(m.z, 1)]
    dest = lax.shift_right_logical(own, digits)
    to_pack = lax.broadcasted_iota(jnp.int32, (packs, rows), 0) == dest
    ahead = prefix_lanes(jnp.where(to_pack, 1.0, 0.0))
    rank = jnp.sum(jnp.where(to_pack, ahead, 0.0), axis=0, keepdims=True).astype(jnp.int32) - 1
    line = lax.broadcasted_iota(jnp.int32, (rows, rows), 0)
    b.send_map[...] = jnp.where(line == dest * cap + rank, 1.0, 0.0).astype(BF)
    b.sent_tokens[...] = mm(b.send_map[...], b.tokens[...]).astype(BF)
    b.full[m.slot, own_place] = b.sent_tokens[own_place]

    def exchange(out, into):
        copies = []
        for d, peer in enumerate(m.dp_peers):
            place = pl.ds(pl.multiple_of(lax.rem(m.z + d + 1, n_dp) * cap, 16), cap)
            copies.append(links.go(out.at[place], into.at[own_place], peer))
        return copies

    b.exchange = exchange
    a2a = exchange(b.sent_tokens, b.full.at[m.slot])
    b.token_copies = a2a
    for ring in cells[1:]:
        ring.start()
    one = pl.ds(0, 1)
    gain_copies = [
        links.go(b.gains.at[m.slot], b.gains.at[m.slot], peer) for peer in m.plane_peers
    ]
    valid_copies = [
        links.go(b.valids.at[m.z, one], b.valids.at[m.z, one], peer) for peer in m.dp_peers
    ]
    for copy in own_copies[1:]:
        copy.wait()

    b.wide_f[...] = jnp.zeros((rows, rows), F32)

    def place_source(s, carry):
        perm = b.index[pl.ds(s, 1)]
        mine = lax.shift_right_logical(perm, digits) == m.z
        ahead = prefix_lanes(jnp.broadcast_to(jnp.where(mine, 1.0, 0.0), (8, rows)))[:1]
        at = jnp.where(mine, s * cap + ahead.astype(jnp.int32) - 1, -1)
        slot = perm - m.z * rows
        slots = jnp.where(line == slot, 1.0, 0.0).astype(BF)
        places = jnp.where(line == at, 1.0, 0.0).astype(BF)
        b.wide_f[...] += mm_nt(slots, places)
        return carry

    lax.fori_loop(0, n_dp, place_source, 0)
    b.recv_map[...] = b.wide_f[...].astype(BF)
    for copy in a2a:
        copy.wait_recv()
    cells[0].step()

    b.sums[...] = jnp.zeros((rows, 128), F32)
    b.squares[...] = jnp.zeros((rows, 128), F32)
    arrivals = 0
    for slot in plane_gather(links, m, b.full, rows):
        columns = pl.ds(pl.multiple_of(slot * wide_d, 128), wide_d)

        def place_rows(r, carry, slot=slot, columns=columns):
            at = pl.ds(pl.multiple_of(r * LINE, LINE), LINE)
            x = mm(b.recv_map[at], b.full[slot])
            b.normed[at, columns] = x.astype(BF)
            b.sums[at] += jnp.sum(x, axis=1, keepdims=True)
            b.squares[at] += jnp.sum(x * x, axis=1, keepdims=True)
            return carry

        lax.fori_loop(0, rows // LINE, place_rows, 0)
        arrivals += 1
        if arrivals in (3, 8):
            cells[-1].step()
        if arrivals == 6:
            cells[0].step()
    own_columns = pl.ds(pl.multiple_of(m.slot * wide_d, 128), wide_d)
    b.x_own[...] = b.normed[:, own_columns]
    b.sent_goal[...] = mm(b.send_map[...], b.targets[...]).astype(BF)
    b.goal_places[own_place] = b.sent_goal[own_place]
    for copy in gain_copies:
        copy.wait_recv()

    def normalise(r, carry):
        at = pl.ds(pl.multiple_of(r * 64, 64), 64)
        mean = b.sums[at][:, :1] / width
        var = b.squares[at][:, :1] / width - mean * mean
        rstd = lax.rsqrt(var + EPSILON)
        b.sums[at] = jnp.broadcast_to(mean, (64, 128))
        b.squares[at] = jnp.broadcast_to(rstd, (64, 128))
        for i in range(8):
            x = b.normed[at, i * wide_d : (i + 1) * wide_d].astype(F32)
            x = (x - mean) * rstd * b.gains[i, :1]
            b.normed[at, i * wide_d : (i + 1) * wide_d] = x.astype(BF)
        return carry

    lax.fori_loop(0, rows // 64, normalise, 0)

    def project(hold, rings, target):
        count = block // len(rings)
        for s in range(n_dp):
            owner = m.owners[s]
            for r, ring in enumerate(rings):
                while ring.at < s:
                    ring.step()
                columns = pl.ds(pl.multiple_of(owner * block + r * count, 128), count)
                product = mm(b.normed[:, columns], hold[owner, r * count : (r + 1) * count])
                target[...] = product if s + r == 0 else target[...] + product

    for ring in cells:
        ring.last_leg()
    gate.start()
    down.start()
    project(b.up_cell, cells, b.wide_f)

    for h in range(heads):
        at = slice(h * chan, (h + 1) * chan)
        for j in range(4):
            b.chan_params[j : j + 1, at] = b.conv_weight[j].astype(F32)[h : h + 1]
        for j, ref in ((4, b.conv_bias), (5, b.group_gain), (6, b.skip_gain)):
            b.chan_params[j : j + 1, at] = ref[...].astype(F32)[h : h + 1]
        for s in range(3):
            for i in range(4):
                tap = b.qkv_weight[s, i].astype(F32)[h : h + 1]
                b.maps8[s, h, i : i + 1] = tap
                b.maps8[s, h, i + 4 : i + 5] = tap
            for g in range(2 * all_heads):
                row = b.gate_weight[g // all_heads, g % all_heads, s].astype(F32)[h : h + 1]
                b.gates_f[g : g + 1, s * local + h * chan : s * local + (h + 1) * chan] = row
    b.gates_f[8:] = jnp.zeros((8, 3 * local), F32)
    b.gates_w[...] = b.gates_f[...].astype(BF)
    place = lax.broadcasted_iota(jnp.int32, (rows, 1), 0)
    ends, total = [], 0
    for k in range(b.lengths.shape[1]):
        total = total + b.lengths[m.z, k]
        ends.append(total)
    begin = jnp.zeros((rows, 1), jnp.int32)
    for end in ends:
        begin = jnp.where(place >= end, end, begin)
    b.begin[...] = jnp.broadcast_to(begin, (rows, 128))

    def convolve(i, carry):
        at = pl.ds(pl.multiple_of(i * 128, 128), 128)
        low = b.wide_f[:, at].astype(BF)
        b.branch[:, at] = low
        x = low.astype(F32)
        since = lax.broadcasted_iota(jnp.int32, (rows, 128), 0) - b.begin[...]
        conv = b.chan_params[4:5, at] + b.chan_params[0:1, at] * x
        for j in range(1, 4):
            back = b.chan_params[j : j + 1, at] * pltpu.roll(x, j, 0)
            conv = conv + jnp.where(since >= j, back, 0.0)
        sig = sigmoid(conv)
        act = conv * sig
        b.act[:, at] = act
        b.slope[:, at] = sig + act * (1.0 - sig)
        return carry

    lax.fori_loop(0, local // 128, convolve, 0)
    r_map = lax.broadcasted_iota(jnp.int32, (chan, chan), 0) // 4
    c_map = lax.broadcasted_iota(jnp.int32, (chan, chan), 1) // 4
    same = r_map == c_map
    for s in range(3):
        for h in range(heads):
            base = b.maps8[s, h]
            dense = jnp.broadcast_to(base[None], (chan // 8, 8, chan)).reshape(chan, chan)
            b.maps[s, h] = jnp.where(same, dense, 0.0).astype(BF)
    for h in range(heads):
        at = slice(h * chan, (h + 1) * chan)
        high, rest = split(b.act[:, at])
        for s in range(2):
            b.qkv[:, s * local + h * chan : s * local + (h + 1) * chan] = (
                mm(high, b.maps[s, h]) + mm(rest, b.maps[s, h])
            ).astype(BF)
        b.qkv[:, 2 * local + h * chan : 2 * local + (h + 1) * chan] = mm(
            b.branch[:, at], b.maps[2, h]
        ).astype(BF)

    pre_part = mm_nt(b.gates_w[...], b.qkv[...])[:8]
    pre_sum = push_sum(links, m, pre_part, b.pre_box, m.plane_peers, m.slot, 8)

    def q_of(h, i):
        return b.qkv[i * LINE : (i + 1) * LINE, h * chan : (h + 1) * chan]

    def k_of(h, low, n):
        return b.qkv[
            low * LINE : (low + n) * LINE, local + h * chan : local + (h + 1) * chan
        ]

    def v_of(h, low, n):
        return b.qkv[
            low * LINE : (low + n) * LINE, 2 * local + h * chan : 2 * local + (h + 1) * chan
        ]

    b.of = (q_of, k_of, v_of)
    for h in range(heads):
        for i, low, at, n in blocks:
            tile = mm_nt(q_of(h, i), k_of(h, low, n))
            for k in range(n):
                b.score_part[h, at + k] = tile[:, k * LINE : (k + 1) * LINE]
    other = links.go(b.score_part.at[1 - m.core], b.score_in.at[0], m.sib)
    b.score_copy = other
    other.wait_recv()
    b.score_sum[...] = b.score_part[m.core] + b.score_in[0]
    far = links.go(b.score_sum, b.score_in.at[1], m.yn)

    line81 = lax.broadcasted_iota(jnp.int32, (8, 1), 0)
    given = b.gate_bias[...].astype(F32)
    bias = jnp.zeros((8, 1), F32)
    for g in range(2):
        for o in range(all_heads):
            bias = jnp.where(line81 == g * all_heads + o, given[g : g + 1, o : o + 1], bias)
    pre = pre_sum() + bias
    b.pre[...] = pre
    line8 = lax.broadcasted_iota(jnp.int32, (8, rows), 0)
    head = m.c * heads + m.core
    in_gate = jnp.sum(jnp.where(line8 == head, pre, 0.0), axis=0, keepdims=True)
    forget = jnp.sum(jnp.where(line8 == head + all_heads, pre, 0.0), axis=0, keepdims=True)
    log_forget = jnp.minimum(forget, 0.0) - jnp.log(1.0 + jnp.exp(-jnp.abs(forget)))
    rising = prefix_lanes(jnp.broadcast_to(log_forget, (8, rows)))
    rise_col = to_columns(rising)
    gate_line = in_gate - rising[:1]
    gate.step()
    for copy in valid_copies:
        copy.wait_recv()
    b.keep[...] = jnp.zeros((rows, 128), F32)

    def take_source(s, carry):
        perm = b.index[pl.ds(s, 1)]
        valid = b.valids[s][:1]
        pack = lax.shift_right_logical(perm, digits)
        lasts = jnp.zeros((1, rows), jnp.int32)
        for p in range(n_dp):
            last = sum(b.lengths[p, k] for k in range(b.lengths.shape[1]))
            lasts = jnp.where(pack == p, last, lasts)
        counted = jnp.where(perm - pack * rows < lasts, valid, 0.0)
        hits = jnp.where(line == perm - m.z * rows, counted, 0.0)
        b.keep[...] += jnp.sum(hits, axis=1, keepdims=True)
        return carry + jnp.sum(counted, axis=1, keepdims=True)

    valid_count = lax.fori_loop(0, n_dp, take_source, jnp.zeros((1, 1), F32))
    keep = b.keep[:, :1]
    far.wait_recv()
    b.score_part[m.core] = b.score_sum[...] + b.score_in[1]
    for i, low, at, n in blocks:
        lines = slice(i * LINE, (i + 1) * LINE)
        t_at = i * LINE + lax.broadcasted_iota(jnp.int32, (LINE, n * LINE), 0)
        s_at = low * LINE + lax.broadcasted_iota(jnp.int32, (LINE, n * LINE), 1)
        allowed = (s_at <= t_at) & (s_at >= b.begin[lines][:, :1])
        logit = jnp.where(
            allowed, rise_col[lines][:, :1] + gate_line[:, low * LINE : (low + n) * LINE], NEG_FILL
        )
        top = jnp.max(logit, axis=1, keepdims=True)
        decay = jnp.where(allowed, jnp.exp(logit - top), 0.0) * scale
        weight = wide(b.score_part, m.core, at, n) * decay
        den = jnp.sum(weight, axis=1, keepdims=True)
        floor = jnp.exp(-top)
        inv = 1.0 / jnp.maximum(jnp.abs(den), floor)
        shares = (weight * inv).astype(BF)
        b.inv[lines] = jnp.broadcast_to(inv, (LINE, 128))
        sign = jnp.where(jnp.abs(den) > floor, jnp.where(den > 0.0, 1.0, -1.0), 0.0)
        b.sign[lines] = jnp.broadcast_to(sign, (LINE, 128))
        for k in range(n):
            b.decay[at + k] = decay[:, k * LINE : (k + 1) * LINE]
            b.weight[at + k] = weight[:, k * LINE : (k + 1) * LINE]
            b.share[m.core, at + k] = shares[:, k * LINE : (k + 1) * LINE]
    shared = links.go(b.share.at[m.core], b.share.at[m.core], m.sib)
    gate.step()
    shared.wait_recv()
    columns = []
    for h in range(heads):
        for i, low, at, n in blocks:
            lines = slice(i * LINE, (i + 1) * LINE)
            b.hidden[lines, h * chan : (h + 1) * chan] = mm(
                wide(b.share, h, at, n), v_of(h, low, n)
            )
        hid = b.hidden[:, h * chan : (h + 1) * chan]
        columns.append(jnp.sum(hid, axis=1, keepdims=True))
        columns.append(jnp.sum(hid * hid, axis=1, keepdims=True))
    moment_sum = push_sum(
        links, m, to_lanes(columns, rows), b.moment_box, m.tensor_peers, m.t, 4
    )
    gate.finish()
    down.step()
    project(b.up_gate, (gate,), b.wide_f)
    moments = to_columns(moment_sum()) / (4 * chan)
    for h in range(heads):
        mean = moments[:, 2 * h : 2 * h + 1]
        rstd = lax.rsqrt(moments[:, 2 * h + 1 : 2 * h + 2] - mean * mean + EPSILON)
        b.head_rstd[h] = jnp.broadcast_to(rstd, (rows, 128))
        b.head_mean[h] = jnp.broadcast_to(mean, (rows, 128))
    down.step()

    def mix(i, carry):
        at = pl.ds(pl.multiple_of(i * 128, 128), 128)
        h = lax.div(i, chan // 128)
        hat = (b.hidden[:, at] - b.head_mean[h]) * b.head_rstd[h]
        b.hidden[:, at] = hat
        low = b.wide_f[:, at].astype(BF)
        b.gate_low[:, at] = low
        g = low.astype(F32)
        inner = hat * b.chan_params[5:6, at] + b.chan_params[6:7, at] * b.act[:, at]
        b.mixed_all[m.z, :, at] = (inner * (g * sigmoid(g))).astype(BF)
        return carry

    lax.fori_loop(0, local // 128, mix, 0)
    down.last_leg()
    goal_copies = exchange(b.sent_goal, b.goal_places)
    mixed_ring.start()
    down.finish()
    piece = min(block, wide_d)

    def down_part(y, core, x):
        slot = (y * 2 + core) * 2 + x
        parts = []
        for k in range(wide_d // piece):
            if block >= 2 * wide_d:
                owner = lax.div((y * 2 + core) * 2 * wide_d, block)
                parts.append(mm(b.mixed_all[m.z], b.down[owner, :, x * wide_d : (x + 1) * wide_d]))
            else:
                owner = lax.div(slot * wide_d, block) + k
                parts.append(mm(b.mixed_all[m.z], b.down[owner]))
        return jnp.concatenate(parts, axis=1)

    own_k = plane_scatter(links, m, down_part, b, rows, (idle, mixed_ring.step, idle))
    for copy in goal_copies:
        copy.wait_recv()
    goal = mm(b.recv_map[...], b.goal_places[...])
    result = (b.x_own[...].astype(F32) + b.acc[own_k]).astype(BF)
    difference = result.astype(F32) - goal
    per_row = jnp.sum(difference * difference, axis=1, keepdims=True)
    loss_part = jnp.sum(keep * 0.5 * per_row, axis=0, keepdims=True) / valid_count
    b.loss_part[...] = jnp.broadcast_to(loss_part, (8, 128))
    own_gradient = ((rows * n_dp) / valid_count * keep * difference).astype(BF)
    b.own_gradient[...] = own_gradient
    b.mixed_ring = mixed_ring
    b.full[m.slot] = own_gradient
    b.arriving = plane_gather(links, m, b.full, rows)
    next_slot = next(b.arriving)

    b.sent_out[...] = mm_tn(b.recv_map[...], result).astype(BF)
    b.home_out[own_place] = b.sent_out[own_place]
    b.home_copies = exchange(b.sent_out, b.home_out)
    b.arriving = itertools.chain([next_slot], b.arriving)


def backward(b, m, links, shape):
    rows, local, chan, n_dp, block, wide_d = shape
    cap, heads = rows // n_dp, local // chan
    all_heads = 2 * heads
    width, head_width = 8 * wide_d, 4 * chan
    blocks, n_blocks = band(rows)
    q_of, k_of, v_of = b.of
    line8 = lax.broadcasted_iota(jnp.int32, (8, rows), 0)
    head = m.c * heads + m.core

    seen = 0
    for slot in b.arriving:
        g = b.full[slot]
        if block >= wide_d:
            ratio = block // wide_d
            at = pl.ds(pl.multiple_of(lax.rem(slot, ratio) * wide_d, 128), wide_d)
            product = mm_nt(g, b.down[lax.div(slot, ratio), :, at])
        else:
            ratio = wide_d // block
            product = sum(
                mm_nt(g[:, k * block : (k + 1) * block], b.down[slot * ratio + k])
                for k in range(ratio)
            )
        b.wide_f[...] = product if seen == 0 else b.wide_f[...] + product
        seen += 1
        if seen == 6:
            b.mixed_ring.step()

    per = rows // 8
    own_rows = pl.ds(pl.multiple_of(m.slot * per, 16), per)
    for d in range(n_dp):
        to = m.z if d == 0 else m.dp_peers[d - 1][0]
        if block >= wide_d:
            ratio = block // wide_d
            for k in range(ratio):
                b.cols_out[to, :, k * wide_d : (k + 1) * wide_d] = b.full[to * ratio + k, own_rows]
        else:
            ratio = wide_d // block
            at = pl.ds(pl.multiple_of(lax.rem(to, ratio) * block, 128), block)
            b.cols_out[to] = b.full[lax.div(to, ratio), own_rows, at]
    from_here = pl.ds(pl.multiple_of(m.z * per, 16), per)
    b.cols[m.slot, from_here] = b.cols_out[m.z]
    cols_copies = [
        links.go(b.cols_out.at[peer[0]], b.cols.at[m.slot, from_here], peer)
        for peer in m.dp_peers
    ]

    def sum_down():
        for copy in cols_copies:
            copy.wait_recv()
        b.mixed_ring.finish()
        b.grad_down[...] = jnp.zeros((local, block), F32)
        for slot in plane_gather(links, m, b.cols, n_dp * per):
            at = pl.ds(pl.multiple_of(slot * per, 16), per)
            for p in range(0, n_dp, 4):
                left = jnp.concatenate([b.mixed_all[p + k, at] for k in range(4)], axis=0)
                b.grad_down[...] += mm_tn(left, b.cols[slot, p * per : (p + 4) * per])
            yield

    down_sum = sum_down()

    def advance(steps):
        for _ in range(steps):
            next(down_sum, None)

    def up_ring(grads, hold, g, h):
        at_h = slice(h * chan, (h + 1) * chan)

        def part(owner):
            at = pl.ds(pl.multiple_of(owner * block, 128), block)
            return mm_tn(b.normed[:, at], grads[:, at_h])

        def keep(total):
            b.grad_up[:, g, h] = total

        return (LineSum if n_dp <= 4 else RingSum)(links, part, hold.at[h], keep, m, n_dp)

    gates = [up_ring(b.g_gate, b.ring_gate, 1, h) for h in range(heads)]
    cells = [up_ring(b.g_cell, b.ring_cell, 0, h) for h in range(heads)]

    def ticks(rings):
        for _ in range(n_dp):
            for ring in rings:
                yield ring.step()

    gate_ticks, cell_ticks = ticks(gates), ticks(cells)

    def tick(source):
        return lambda: next(source, None)

    def unmix(i, carry):
        at = pl.ds(pl.multiple_of(i * 128, 128), 128)
        gm = b.wide_f[:, at]
        g = b.gate_low[:, at].astype(F32)
        sig = sigmoid(g)
        silu = g * sig
        hat, act = b.hidden[:, at], b.act[:, at]
        group, skip = b.chan_params[5:6, at], b.chan_params[6:7, at]
        inner = hat * group + skip * act
        b.g_gate[:, at] = (gm * inner * (sig + silu * (1.0 - sig))).astype(BF)
        gi = gm * silu
        b.small[5:6, at] = jnp.sum(gi * hat, axis=0, keepdims=True)
        b.small[6:7, at] = jnp.sum(gi * act, axis=0, keepdims=True)
        b.g_act[:, at] = gi * skip
        b.wide_f[:, at] = gi * group
        return carry

    lax.fori_loop(0, local // 128, unmix, 0)
    b.mixed_ring.last_leg()
    next(gate_ticks)
    next(gate_ticks)
    columns = []
    for h in range(heads):
        u = b.wide_f[:, h * chan : (h + 1) * chan]
        columns.append(jnp.sum(u, axis=1, keepdims=True))
        columns.append(
            jnp.sum(u * b.hidden[:, h * chan : (h + 1) * chan], axis=1, keepdims=True)
        )
    u_sum = push_sum(links, m, to_lanes(columns, rows), b.u_box, m.tensor_peers, m.t, 4)
    u_moments = to_columns(u_sum())
    rhos = []
    for h in range(heads):
        at = slice(h * chan, (h + 1) * chan)
        rstd = b.head_rstd[h][:, :1]
        mean_u = u_moments[:, 2 * h : 2 * h + 1] / head_width
        sum_ux = u_moments[:, 2 * h + 1 : 2 * h + 2]
        d_hidden = rstd * (b.wide_f[:, at] - mean_u - b.hidden[:, at] * (sum_ux / head_width))
        b.d_hidden[:, at] = d_hidden.astype(BF)
        rhos.append(sum_ux * (EPSILON * rstd * rstd))
    rho = jnp.where(m.core == 0, rhos[0], rhos[1])
    links.settle([b.score_copy])
    for h in range(heads):
        for i, low, at, n in blocks:
            tile = mm_nt(
                b.d_hidden[i * LINE : (i + 1) * LINE, h * chan : (h + 1) * chan], v_of(h, low, n)
            )
            for k in range(n):
                b.score_part[h, at + k] = tile[:, k * LINE : (k + 1) * LINE]
    other = links.go(b.score_part.at[1 - m.core], b.score_in.at[0], m.sib)
    other.wait_recv()
    b.share_out[...] = (b.score_part[m.core] + b.score_in[0]).astype(BF)
    far = links.go(b.share_out, b.share_in, m.yn)
    far.wait_recv()
    b.lines[...] = jnp.zeros((8, rows), F32)
    for i, low, at, n in blocks:
        lines = slice(i * LINE, (i + 1) * LINE)
        across = slice(low * LINE, (low + n) * LINE)

        def spread(ref):
            return jnp.concatenate([ref[at + k].astype(F32) for k in range(n)], axis=1)

        inv, sign, radial = b.inv[lines][:, :1], b.sign[lines][:, :1], rho[lines]
        weight = spread(b.weight)
        full = (spread(b.share_out) + spread(b.share_in)) * inv - sign * radial * inv
        exact = jnp.where(sign == 0.0, radial, 0.0)
        noisy = jnp.sum(full * weight, axis=1, keepdims=True)
        square = jnp.sum(weight * weight, axis=1, keepdims=True)
        full = full - weight * ((noisy - exact) / jnp.where(square > 0.0, square, 1.0))
        d_score = (full * spread(b.decay)).astype(BF)
        for k in range(n):
            b.d_score[m.core, at + k] = d_score[:, k * LINE : (k + 1) * LINE]
        b.lines[0:1, across] += jnp.sum(full * weight, axis=0, keepdims=True)
        b.keep[lines] = jnp.broadcast_to(exact, (LINE, 128))
    next(gate_ticks)
    scored = links.go(b.d_score.at[m.core], b.d_score.at[m.core], m.sib)
    over_cols = b.lines[0:1]
    over_rows = b.keep[...].T[0:1]
    delta = jnp.broadcast_to(over_rows - over_cols, (8, rows))
    after = jnp.sum(delta, axis=1, keepdims=True) - prefix_lanes(delta) + delta
    forget = jnp.sum(jnp.where(line8 == head + all_heads, b.pre[...], 0.0), axis=0, keepdims=True)
    d_forget = after[:1] / (1.0 + jnp.exp(forget))
    own_lines = jnp.where(line8 == head, over_cols, 0.0) + jnp.where(
        line8 == head + all_heads, d_forget, 0.0
    )
    head_peers = [
        m.sib,
        m.xn,
        (m.z, m.sib_t, m.other_c),
    ]
    pre_sum = push_sum(links, m, own_lines, b.grad_box, head_peers, m.c * 2 + m.core, 4)

    for h in range(heads):
        at = slice(2 * local + h * chan, 2 * local + (h + 1) * chan)
        b.g_proj[:, at] = jnp.zeros((rows, chan), F32)
        for i, low, place, n in blocks:
            d_hid = b.d_hidden[i * LINE : (i + 1) * LINE, h * chan : (h + 1) * chan]
            b.g_proj[low * LINE : (low + n) * LINE, at] += mm_tn(wide(b.share, h, place, n), d_hid)
    next(gate_ticks)
    scored.wait_recv()
    for h in range(heads):
        at = slice(h * chan, (h + 1) * chan)
        k_at = slice(local + h * chan, local + (h + 1) * chan)
        b.g_proj[:, k_at] = jnp.zeros((rows, chan), F32)
        for i, low, place, n in blocks:
            tile = wide(b.d_score, h, place, n)
            b.g_proj[i * LINE : (i + 1) * LINE, at] = mm(tile, k_of(h, low, n))
            b.g_proj[low * LINE : (low + n) * LINE, k_at] += mm_tn(tile, q_of(h, i))
    pre_grad = pre_sum()
    next(gate_ticks)
    advance(1)
    pre16 = jnp.concatenate([pre_grad, jnp.zeros((8, rows), F32)], axis=0)
    high, rest = split(pre16)
    b.g_proj[...] += mm_tn(high, b.gates_w[...]) + mm_tn(rest, b.gates_w[...])
    gate_grad = (mm(high, b.qkv[...]) + mm(rest, b.qkv[...]))[:8]
    for s in range(3):
        b.low_sum[8 * s : 8 * (s + 1)] = gate_grad[:, s * local : (s + 1) * local]
    bias_grad = jnp.sum(pre_grad, axis=1, keepdims=True)
    b.small[8:16] = jnp.zeros((8, local), F32)
    b.small[8:9, :128] = to_lanes_one(bias_grad)
    advance(2)

    r_map = lax.broadcasted_iota(jnp.int32, (chan, chan), 0) // 4
    c_map = lax.broadcasted_iota(jnp.int32, (chan, chan), 1) // 4
    same = r_map == c_map
    for h in range(heads):
        at = slice(h * chan, (h + 1) * chan)
        act_low = b.act[:, at].astype(BF)
        extra = None
        for s in range(3):
            low = b.g_proj[:, s * local + h * chan : s * local + (h + 1) * chan].astype(BF)
            left = act_low if s < 2 else b.branch[:, at]
            dense = jnp.where(same, mm_tn(left, low), 0.0)
            folded = jnp.sum(dense.reshape(chan // 8, 8, chan), axis=0)
            b.low_sum[24 + 4 * s : 28 + 4 * s, at] = folded[:4] + folded[4:]
            back = mm_nt(low, b.maps[s, h])
            if s == 0:
                extra = back
            elif s == 1:
                b.g_act[:, at] += extra + back
            else:
                b.wide_f[:, at] = back

    def unconvolve(i, carry):
        at = pl.ds(pl.multiple_of(i * 128, 128), 128)
        since = lax.broadcasted_iota(jnp.int32, (rows, 128), 0) - b.begin[...]
        x = b.branch[:, at].astype(F32)
        gc = b.g_act[:, at] * b.slope[:, at]
        gb = b.wide_f[:, at] + b.chan_params[0:1, at] * gc
        b.small[0:1, at] = jnp.sum(gc * x, axis=0, keepdims=True)
        b.small[4:5, at] = jnp.sum(gc, axis=0, keepdims=True)
        for j in range(1, 4):
            kept = jnp.where(since >= j, gc, 0.0)
            gb = gb + b.chan_params[j : j + 1, at] * pltpu.roll(kept, rows - j, 0)
            b.small[j : j + 1, at] = jnp.sum(kept * pltpu.roll(x, j, 0), axis=0, keepdims=True)
        b.g_cell[:, at] = gb.astype(BF)
        return carry

    lax.fori_loop(0, local // 128, unconvolve, 0)
    next(gate_ticks)
    next(cell_ticks)
    next(cell_ticks)
    b.low_sum[36:] = jnp.zeros((12, local), F32)
    b.low_box[m.z] = b.low_sum[...].astype(BF)
    low_copies = [links.go(b.low_box.at[m.z], b.low_box.at[m.z], peer) for peer in m.dp_peers]
    advance(4)

    def up_part(y, core, x):
        slot = (y * 2 + core) * 2 + x
        if block >= wide_d:
            ratio = block // wide_d
            at = pl.ds(pl.multiple_of(lax.rem(slot, ratio) * wide_d, 16), wide_d)
            owner = lax.div(slot, ratio)
            return mm_nt(b.g_cell[...], b.up_cell[owner, at]) + mm_nt(
                b.g_gate[...], b.up_gate[owner, at]
            )
        ratio = wide_d // block
        return jnp.concatenate(
            [
                mm_nt(b.g_cell[...], b.up_cell[slot * ratio + k])
                + mm_nt(b.g_gate[...], b.up_gate[slot * ratio + k])
                for k in range(ratio)
            ],
            axis=1,
        )

    own_k = plane_scatter(
        links, m, up_part, b, rows, (lambda: advance(2), tick(gate_ticks), tick(gate_ticks))
    )
    for _ in gate_ticks:
        pass
    grad_normed = b.acc[own_k]
    x_hat = (b.x_own[...].astype(F32) - b.sums[:, :1]) * b.squares[:, :1]
    grad_scaled = grad_normed * b.gains[m.slot, :1]
    line_sum = push_sum(
        links,
        m,
        to_lanes(
            [
                jnp.sum(grad_scaled, axis=1, keepdims=True),
                jnp.sum(grad_scaled * x_hat, axis=1, keepdims=True),
            ],
            rows,
        ),
        b.line_box,
        m.plane_peers,
        m.slot,
        8,
    )
    loss_sum = push_sum(links, m, b.loss_part[...], b.loss_box, m.plane_peers, m.slot, 8)
    b.small[7:8] = jnp.zeros((1, local), F32)
    b.small[7:8, :wide_d] = jnp.sum(grad_normed * x_hat, axis=0, keepdims=True)
    b.small[9:10, :128] = loss_sum()[:1]
    b.small_box[m.z] = b.small[...]
    small_copies = [
        links.go(b.small_box.at[m.z], b.small_box.at[m.z], peer) for peer in m.dp_peers
    ]
    next(cell_ticks)
    lines = to_columns(line_sum()) / width
    grad_x = b.squares[:, :1] * (grad_scaled - lines[:, :1] - x_hat * lines[:, 1:2])
    own_grad = b.own_gradient[...].astype(F32)
    grad_slot = (own_grad + grad_x).astype(BF)
    links.settle(b.token_copies)
    b.sent_tokens[...] = mm_tn(b.recv_map[...], grad_slot).astype(BF)
    own_place = pl.ds(pl.multiple_of(m.z * cap, 16), cap)
    b.home_grad[own_place] = b.sent_tokens[own_place]
    copies = b.exchange(b.sent_tokens, b.home_grad)
    next(cell_ticks)
    for copy in b.home_copies:
        copy.wait_recv()
    b.output[...] = mm_tn(b.send_map[...], b.home_out[...]).astype(BF)
    next(cell_ticks)
    advance(3)
    for copy in small_copies + low_copies:
        copy.wait_recv()
    lows = b.low_box[0].astype(F32)
    for k in range(1, n_dp):
        lows = lows + b.low_box[k].astype(F32)
    b.low_sum[...] = lows
    total = b.small_box[0]
    for k in range(1, n_dp):
        total = total + b.small_box[k]
    b.small[...] = total
    b.loss[...] = total[9:10, :1]
    b.grad_ln[...] = total[7:8, :wide_d]
    for h in range(heads):
        at = slice(h * chan, (h + 1) * chan)
        for j in range(4):
            b.grad_conv_weight[j, h : h + 1] = b.small[j : j + 1, at]
        for j, ref in ((4, b.grad_conv_bias), (5, b.grad_group), (6, b.grad_skip)):
            ref[h : h + 1] = b.small[j : j + 1, at]
        for s in range(3):
            for i in range(4):
                k = 24 + 4 * s + i
                b.grad_qkv[s, i, h : h + 1] = b.low_sum[k : k + 1, at]
            for g in range(2 * all_heads):
                k = 8 * s + g
                b.grad_gate_weight[g // all_heads, g % all_heads, s, h : h + 1] = b.low_sum[
                    k : k + 1, at
                ]
    for g in range(2):
        b.grad_gate_bias[g : g + 1] = total[8:9, g * all_heads : (g + 1) * all_heads]
    for _ in cell_ticks:
        pass
    for copy in copies:
        copy.wait_recv()
    b.grad_input[...] = mm_tn(b.send_map[...], b.home_grad[...]).astype(BF)
    for line in [b.mixed_ring] + gates + cells:
        line.settle()


def kernel(names, shape, limit, *refs):
    b = types.SimpleNamespace(**dict(zip(names, refs)))
    m = coordinates(shape[3])
    links = Links(b.send_sem, b.recv_sem, limit)
    forward(b, m, links, shape)
    backward(b, m, links, shape)
    links.close()


def carry_out(*refs):
    *ends, sems = refs
    half = len(ends) // 2
    copies = [
        pltpu.make_async_copy(ends[k], ends[half + k], sems.at[k]) for k in range(half)
    ]
    for copy in copies:
        copy.start()
    for copy in copies:
        copy.wait()


def shards(
    tokens,
    targets,
    ln_gain,
    up_weight,
    conv_weight,
    conv_bias,
    qkv_weight,
    gate_weight,
    gate_bias,
    group_gain,
    skip_gain,
    down_weight,
    lengths,
    permutation,
    valid,
):
    rows, wide_d = tokens.shape
    n_dp = lax.axis_size("dp")
    heads, chan = up_weight.shape[2], up_weight.shape[3]
    local = heads * chan
    block = up_weight.shape[0]
    width = 8 * wide_d
    up_halves = up_weight.transpose(1, 0, 2, 3).reshape(2, block, local)
    inputs = dict(
        tokens=tokens,
        targets=targets,
        index=jnp.concatenate([permutation.reshape(n_dp, rows), valid.reshape(1, rows)]),
        own_cell=up_halves[0],
        own_gate=up_halves[1],
        own_down=down_weight.reshape(local, block),
        ln_gain=ln_gain.reshape(1, wide_d),
        conv_weight=conv_weight,
        conv_bias=conv_bias,
        qkv_weight=qkv_weight,
        gate_weight=gate_weight,
        gate_bias=gate_bias,
        group_gain=group_gain,
        skip_gain=skip_gain,
        lengths=lengths,
    )
    outputs = dict(
        output=((rows, wide_d), BF),
        loss=((1, 1), F32),
        grad_input=((rows, wide_d), BF),
        grad_ln=((1, wide_d), F32),
        grad_up=(up_weight.shape, F32),
        grad_conv_weight=(conv_weight.shape, F32),
        grad_conv_bias=(conv_bias.shape, F32),
        grad_qkv=(qkv_weight.shape, F32),
        grad_gate_weight=(gate_weight.shape, F32),
        grad_gate_bias=(gate_bias.shape, F32),
        grad_group=(group_gain.shape, F32),
        grad_skip=(skip_gain.shape, F32),
        grad_down=((local, block), F32),
    )
    n_blocks = band(rows)[1]
    half = rows // 2
    limit = 130 + 18 * n_dp
    turns = (2 if n_dp <= 4 else 1, n_dp)
    scratch = dict(
        send_map=((rows, rows), BF),
        recv_map=((rows, rows), BF),
        chan_params=((8, local), F32),
        maps8=((3, heads, 8, chan), F32),
        gates_f=((16, 3 * local), F32),
        gates_w=((16, 3 * local), BF),
        sent_tokens=((rows, wide_d), BF),
        sent_goal=((rows, wide_d), BF),
        goal_places=((rows, wide_d), BF),
        valids=((n_dp, 8, rows), F32),
        keep=((rows, 128), F32),
        full=((8, rows, wide_d), BF),
        gains=((8, 8, wide_d), F32),
        up_cell=((n_dp, block, local), BF),
        up_gate=((n_dp, block, local), BF),
        down=((n_dp, local, block), BF),
        sums=((rows, 128), F32),
        squares=((rows, 128), F32),
        x_own=((rows, wide_d), BF),
        normed=((rows, width), BF),
        wide_f=((rows, local), F32),
        begin=((rows, 128), jnp.int32),
        branch=((rows, local), BF),
        act=((rows, local), F32),
        slope=((rows, local), F32),
        maps=((3, heads, chan, chan), BF),
        qkv=((rows, 3 * local), BF),
        pre_box=((8, 8, rows), F32),
        pre=((8, rows), F32),
        score_part=((heads, n_blocks, LINE, LINE), F32),
        score_in=((2, n_blocks, LINE, LINE), F32),
        score_sum=((n_blocks, LINE, LINE), F32),
        decay=((n_blocks, LINE, LINE), F32),
        weight=((n_blocks, LINE, LINE), F32),
        share=((heads, n_blocks, LINE, LINE), BF),
        inv=((rows, 128), F32),
        sign=((rows, 128), F32),
        hidden=((rows, local), F32),
        moment_box=((4, 8, rows), F32),
        head_rstd=((heads, rows, 128), F32),
        head_mean=((heads, rows, 128), F32),
        gate_low=((rows, local), BF),
        out=((4, rows, wide_d), BF),
        into=((4, rows, wide_d), BF),
        acc=((4, rows, wide_d), F32),
        small_out=((6, half, wide_d), BF),
        small_in=((6, half, wide_d), BF),
        loss_part=((8, 128), F32),
        own_gradient=((rows, wide_d), BF),
        sent_out=((rows, wide_d), BF),
        home_out=((rows, wide_d), BF),
        home_grad=((rows, wide_d), BF),
        mixed_all=((n_dp, rows, local), BF),
        cols_out=((n_dp, rows // 8, block), BF),
        cols=((8, n_dp * rows // 8, block), BF),
        low_sum=((48, local), F32),
        low_box=((n_dp, 48, local), BF),
        ring_gate=((heads,) + turns + (block, chan), BF),
        ring_cell=((heads,) + turns + (block, chan), BF),
        g_gate=((rows, local), BF),
        g_cell=((rows, local), BF),
        small=((16, local), F32),
        small_box=((n_dp, 16, local), F32),
        g_act=((rows, local), F32),
        u_box=((4, 8, rows), F32),
        d_hidden=((rows, local), BF),
        share_out=((n_blocks, LINE, LINE), BF),
        share_in=((n_blocks, LINE, LINE), BF),
        lines=((8, rows), F32),
        d_score=((heads, n_blocks, LINE, LINE), BF),
        grad_box=((4, 8, rows), F32),
        g_proj=((rows, 3 * local), F32),
        line_box=((8, 8, rows), F32),
        loss_box=((8, 8, 128), F32),
    )
    vmem = pl.BlockSpec(memory_space=pltpu.VMEM)
    spaces = {name: pl.BlockSpec(memory_space=pl.ANY) for name in inputs if name[:4] == "own_"}
    spaces["lengths"] = pl.BlockSpec(memory_space=pltpu.SMEM)
    names = list(inputs) + list(outputs) + list(scratch) + ["send_sem", "recv_sem", "local_sem"]
    results = pl.pallas_call(
        lambda *refs: kernel(names, (rows, local, chan, n_dp, block, wide_d), limit, *refs),
        out_shape=[jax.ShapeDtypeStruct(*spec) for spec in outputs.values()],
        in_specs=[spaces.get(name, vmem) for name in inputs],
        out_specs=[vmem] * len(outputs),
        scratch_shapes=[pltpu.VMEM(*spec) for spec in scratch.values()]
        + [pltpu.SemaphoreType.DMA((limit,)), pltpu.SemaphoreType.DMA((limit,))]
        + [pltpu.SemaphoreType.DMA((3,))],
        compiler_params=pltpu.CompilerParams(
            collective_id=0, has_side_effects=True, vmem_limit_bytes=VMEM_LIMIT
        ),
    )(*inputs.values())
    results = pl.pallas_call(
        carry_out,
        out_shape=[jax.ShapeDtypeStruct(*spec) for spec in outputs.values()],
        in_specs=[pl.BlockSpec(memory_space=pl.ANY)] * len(outputs),
        out_specs=[vmem] * len(outputs),
        scratch_shapes=[pltpu.SemaphoreType.DMA((len(outputs),))],
    )(*results)
    o = types.SimpleNamespace(**dict(zip(outputs, results)))
    return (
        o.output,
        o.loss.reshape(()),
        o.grad_input,
        o.grad_ln.reshape(-1),
        o.grad_up,
        o.grad_conv_weight,
        o.grad_conv_bias,
        o.grad_qkv,
        o.grad_gate_weight,
        o.grad_gate_bias,
        o.grad_group,
        o.grad_skip,
        o.grad_down.reshape(down_weight.shape),
    )


def solution(mesh):
    return jax.shard_map(
        shards,
        mesh=mesh,
        in_specs=(
            P("dp", ("tensor", "ctx")),
            P("dp", ("tensor", "ctx")),
            P(("tensor", "ctx")),
            P("dp", None, "ctx", "tensor"),
            P(None, "ctx", "tensor"),
            P("ctx", "tensor"),
            P(None, None, "ctx", "tensor"),
            P(None, None, None, "ctx", "tensor"),
            P(),
            P("ctx", "tensor"),
            P("ctx", "tensor"),
            P("ctx", "tensor", "dp"),
            P(),
            P(),
            P("dp"),
        ),
        out_specs=(
            P("dp", ("tensor", "ctx")),
            P(),
            P("dp", ("tensor", "ctx")),
            P(("tensor", "ctx")),
            P("dp", None, "ctx", "tensor"),
            P(None, "ctx", "tensor"),
            P("ctx", "tensor"),
            P(None, None, "ctx", "tensor"),
            P(None, None, None, "ctx", "tensor"),
            P(),
            P("ctx", "tensor"),
            P("ctx", "tensor"),
            P("ctx", "tensor", "dp"),
        ),
        check_vma=False,
    )
```

```python
import itertools
import types

import jax
import jax.numpy as jnp
from jax import lax
from jax.experimental import pallas as pl
from jax.experimental.pallas import tpu as pltpu
from jax.sharding import PartitionSpec as P

NEG_FILL = -1e30
EPSILON = 1e-05
BF = jnp.bfloat16
F32 = jnp.float32
MESH = pl.DeviceIdType.MESH
VMEM_LIMIT = 62 * 1024 * 1024
LINE = 128
GROUPS = 2
BAND = 2


def mm(a, b):
    return jnp.dot(a, b, preferred_element_type=F32)


def mm_nt(a, b):
    return lax.dot_general(a, b, (((1,), (1,)), ((), ())), preferred_element_type=F32)


def mm_tn(a, b):
    return lax.dot_general(a, b, (((0,), (0,)), ((), ())), preferred_element_type=F32)


def split(v):
    high = v.astype(BF)
    return high, (v - high.astype(F32)).astype(BF)


def root_inverse(v):
    guess = lax.rsqrt(v)
    return guess * (1.5 - 0.5 * v * guess * guess)


def sigmoid(v):
    return 1.0 / (1.0 + jnp.exp(-v))


class Links:
    def __init__(self, send, recv, limit):
        self.send, self.recv, self.limit = send, recv, limit
        self.used, self.open = 0, []

    def make(self, src, dst, peer):
        k = self.used
        self.used += 1
        assert k < self.limit
        copy = pltpu.make_async_remote_copy(
            src_ref=src,
            dst_ref=dst,
            send_sem=self.send.at[k],
            recv_sem=self.recv.at[k],
            device_id=peer,
            device_id_type=MESH,
        )
        return copy

    def go(self, src, dst, peer):
        copy = self.make(src, dst, peer)
        copy.start()
        self.open.append(copy)
        return copy

    def settle(self, copies):
        for copy in copies:
            copy.wait_send()
        self.open = [c for c in self.open if all(c is not done for done in copies)]

    def close(self):
        self.settle(list(self.open))


class Ring:
    def __init__(self, links, hold, part, next_peer, owners):
        self.links, self.hold, self.part = links, hold, part
        self.peer, self.owners = next_peer, owners
        self.flying, self.at = None, 0

    def start(self):
        block = self.hold.at[self.owners[self.at], self.part]
        self.flying = self.links.go(block, block, self.peer)

    def step(self):
        if self.at >= len(self.owners) - 1:
            return False
        if self.flying is None:
            self.start()
        self.flying.wait_recv()
        self.at += 1
        self.flying = None
        if self.at < len(self.owners) - 1:
            self.start()
            return True
        return False

    def last_leg(self):
        while self.at < len(self.owners) - 2:
            self.step()

    def finish(self):
        while self.step():
            pass

    def settle(self):
        self.links.close()


def when(condition, *actions):
    @pl.when(condition)
    def _():
        for action in actions:
            action()


class LineGather:
    def __init__(self, links, hold, m, count):
        self.z, self.count, self.at = m.z, count, 0
        z, last = m.z, count - 1
        self.ways = []
        for d in range(1, count):
            to_right = jnp.maximum(z - (d - 1), 0)
            to_left = jnp.minimum(z + (d - 1), last)
            self.ways.append(
                (
                    (
                        links.make(hold.at[to_right], hold.at[to_right], m.right),
                        (z < last) & (z >= d - 1),
                        z >= d,
                    ),
                    (
                        links.make(hold.at[to_left], hold.at[to_left], m.left),
                        (z > 0) & (z + d - 1 <= last),
                        z + d <= last,
                    ),
                )
            )

    def start(self):
        for copy, sends, _ in self.ways[self.at]:
            when(sends, copy.start)

    def step(self):
        if self.at >= self.count - 1:
            return
        for copy, _, receives in self.ways[self.at]:
            when(receives, copy.wait_recv)
        self.at += 1
        if self.at < self.count - 1:
            self.start()

    def last_leg(self):
        while self.at < self.count - 2:
            self.step()

    def finish(self):
        while self.at < self.count - 1:
            self.step()

    def settle(self):
        for pair in self.ways:
            for copy, sends, _ in pair:
                when(sends, copy.wait_send)


class LineSum:
    def __init__(self, links, part, hold, target, m, count):
        self.part, self.hold, self.target = part, hold, target
        self.z, self.count, self.at = m.z, count, 0
        places = (m.z, count - 1 - m.z)
        self.ways = [
            (
                places[way],
                [
                    links.make(hold.at[way, t], hold.at[way, t + 1], peer)
                    for t in range(count - 1)
                ],
            )
            for way, peer in enumerate((m.right, m.left))
        ]

    def step(self):
        t, count = self.at, self.count
        if t > count - 1:
            return
        self.at += 1
        if t == count - 1:
            total = self.part(self.z)
        for way, (place, copies) in enumerate(self.ways):
            behind = place > 0
            if t:
                when(behind & (place <= t), copies[t - 1].wait_recv)
            if t == count - 1:
                total = total + jnp.where(behind, self.hold[way, t].astype(F32), 0.0)
                continue

            def send(way=way, place=place, copies=copies, behind=behind):
                ahead = count - 1 - t
                own = self.part(self.z + ahead if way == 0 else self.z - ahead)
                if t:
                    own = own + jnp.where(behind, self.hold[way, t].astype(F32), 0.0)
                self.hold[way, t] = own.astype(BF)
                copies[t].start()

            when(place <= t, send)
        if t == count - 1:
            self.target(total)

    def settle(self):
        for place, copies in self.ways:
            for t, copy in enumerate(copies):
                when(place <= t, copy.wait_send)


class RingSum:
    def __init__(self, links, part, hold, target, m, count):
        self.links, self.part, self.hold, self.target = links, part, hold, target
        self.m, self.count, self.at = m, count, -1
        self.sent = []

    def step(self):
        if self.at >= self.count - 1:
            return
        self.at += 1
        own = self.part(self.m.owners[(self.at + 1) % self.count])
        if self.at:
            self.sent[-1].wait_recv()
            own = own + self.hold[0, self.at].astype(F32)
        if self.at == self.count - 1:
            self.target(own)
            return
        self.hold[0, self.at] = own.astype(BF)
        self.sent.append(
            self.links.go(
                self.hold.at[0, self.at], self.hold.at[0, self.at + 1], self.m.ring_next
            )
        )

    def settle(self):
        self.links.settle(self.sent)


def coordinates(dp_count):
    z, t, c = lax.axis_index("dp"), lax.axis_index("tensor"), lax.axis_index("ctx")
    core = lax.rem(t, 2)
    m = types.SimpleNamespace(z=z, t=t, c=c, core=core, y=lax.div(t, 2))
    m.sib_t, m.far_t, m.other_c = t + 1 - 2 * core, lax.rem(t + 2, 4), 1 - c
    m.sib, m.yn, m.xn = (z, m.sib_t, c), (z, m.far_t, c), (z, t, m.other_c)
    m.slot = t * 2 + c
    m.slot_x, m.slot_y, m.slot_d = t * 2 + m.other_c, m.far_t * 2 + c, m.far_t * 2 + m.other_c
    m.to_sib = 2 - 4 * core
    if dp_count == 4:
        def after(v):
            return lax.rem(2 * v + 1, 5)

        def before(v):
            return lax.rem(3 * v + 2, 5)
    else:
        def after(v):
            return lax.rem(v + 1, dp_count)

        def before(v):
            return lax.rem(v + dp_count - 1, dp_count)

    m.ring_next = (after(z), t, c)
    m.owners = [z]
    for _ in range(dp_count - 1):
        m.owners.append(before(m.owners[-1]))
    m.right = (lax.rem(z + 1, dp_count), t, c)
    m.left = (lax.rem(z + dp_count - 1, dp_count), t, c)
    m.dp_peers = [(lax.rem(z + d, dp_count), t, c) for d in range(1, dp_count)]
    m.plane_peers = [
        (z, lax.rem(t + dt, 4), lax.rem(c + dc, 2))
        for dt in range(4)
        for dc in range(2)
        if dt or dc
    ]
    m.tensor_peers = [(z, lax.rem(t + dt, 4), c) for dt in range(1, 4)]
    return m


def plane_gather(links, m, full, rows, base=0):
    half = rows // 2
    first, second, whole = pl.ds(base, half), pl.ds(base + half, half), pl.ds(base, rows)
    sent = []

    def send(slot, part, peer):
        sent.append(links.go(full.at[slot, part], full.at[slot, part], peer))
        return sent[-1]

    x_first = send(m.slot, first, m.xn)
    y_second = send(m.slot, second, m.yn)
    to_sib = send(m.slot, whole, m.sib)
    x_second = send(m.slot, second, m.xn)
    y_first = send(m.slot, first, m.yn)
    yield m.slot
    to_sib.wait_recv()
    yield m.slot + m.to_sib
    x_first.wait_recv()
    d_first = send(m.slot_x, first, m.yn)
    y_second.wait_recv()
    d_second = send(m.slot_y, second, m.xn)
    x_second.wait_recv()
    sib_x = send(m.slot_x, whole, m.sib)
    yield m.slot_x
    y_first.wait_recv()
    sib_y = send(m.slot_y, whole, m.sib)
    yield m.slot_y
    sib_x.wait_recv()
    yield m.slot_x + m.to_sib
    d_first.wait_recv()
    d_second.wait_recv()
    sib_d = send(m.slot_d, whole, m.sib)
    yield m.slot_d
    sib_y.wait_recv()
    yield m.slot_y + m.to_sib
    sib_d.wait_recv()
    yield m.slot_d + m.to_sib
    links.settle(sent)


def idle():
    pass


def to_lanes(columns, rows):
    lane = lax.broadcasted_iota(jnp.int32, (rows, 128), 1)
    out = jnp.zeros((rows, 128), F32)
    for j, column in enumerate(columns):
        out = jnp.where(lane == j, column, out)
    return out.T[:8]


def to_lanes_one(column):
    line = lax.broadcasted_iota(jnp.int32, (8, 128), 0)
    lane = lax.broadcasted_iota(jnp.int32, (8, 128), 1)
    return jnp.sum(jnp.where(line == lane, column, 0.0), axis=0, keepdims=True)


def to_columns(lines):
    rows = lines.shape[1]
    return jnp.concatenate([lines, jnp.zeros((120, rows), F32)], axis=0).T


def push_sum(links, m, lines, box, peers, own_place, count):
    box[own_place] = lines
    copies = [links.go(box.at[own_place], box.at[own_place], peer) for peer in peers]

    def finish():
        for copy in copies:
            copy.wait_recv()
        total = box[0]
        for k in range(1, count):
            total = total + box[k]
        return total

    return finish


def prefix_lanes(v):
    width = v.shape[1]
    lane = lax.broadcasted_iota(jnp.int32, v.shape, 1)
    step = 1
    while step < width:
        v = v + jnp.where(lane >= step, pltpu.roll(v, step, 1), 0.0)
        step *= 2
    return v


def band(rows):
    out, at = [], 0
    for i in range(rows // LINE):
        low = max(0, i - BAND)
        out.append((i, low, at, i - low + 1))
        at += i - low + 1
    return out, at


def wide(ref, h, at, width):
    return jnp.concatenate([ref[h, at + k] for k in range(width)], axis=1)


def plane_scatter(links, m, part, b, rows, services):
    size = rows // GROUPS
    half = size // 2
    own_k = m.y * 2 + m.c
    far_y = 1 - m.y
    links.settle(b.scatter_copies)
    copies = []
    for k in range(4):
        b.out[k] = part(k // 2, 1 - m.core, k % 2).astype(BF)
        for g in range(GROUPS):
            at = pl.ds(g * size, size)
            copies.append(links.go(b.out.at[k, at], b.into.at[k, at], m.sib))
    for k in range(4):
        b.acc[k] = part(k // 2, m.core, k % 2)
    b.scatter_copies = list(copies)
    services[0]()

    def send(g, place, k, at, peer):
        place += 6 * g
        b.small_out[place] = b.acc[k, at].astype(BF)
        copy = links.go(b.small_out.at[place], b.small_in.at[place], peer)
        b.scatter_copies.append(copy)
        return copy

    def receive(g, place, k, at, copy):
        copy.wait_recv()
        b.acc[k, at] += b.small_in[place + 6 * g].astype(F32)

    parts = [(pl.ds(g * size, half), pl.ds(g * size + half, half)) for g in range(GROUPS)]
    second_phase, third_phase = [], []
    for g, (first, second) in enumerate(parts):
        at = pl.ds(g * size, size)
        for k in range(4):
            copies[k * GROUPS + g].wait_recv()
            b.acc[k, at] += b.into[k, at].astype(F32)
        second_phase.append(
            [send(g, y, y * 2 + m.other_c, first, m.xn) for y in range(2)]
            + [send(g, 2 + x, far_y * 2 + x, second, m.yn) for x in range(2)]
        )
    services[1]()
    for g, (first, second) in enumerate(parts):
        flying = second_phase[g]
        for y in range(2):
            receive(g, y, y * 2 + m.c, first, flying[y])
        for x in range(2):
            receive(g, 2 + x, m.y * 2 + x, second, flying[2 + x])
        third_phase.append(
            (
                send(g, 4, far_y * 2 + m.c, first, m.yn),
                send(g, 5, m.y * 2 + m.other_c, second, m.xn),
            )
        )
    services[2]()
    for g, (first, second) in enumerate(parts):
        receive(g, 4, own_k, first, third_phase[g][0])
        receive(g, 5, own_k, second, third_phase[g][1])
        yield g, slice(g * size, (g + 1) * size)


def forward(b, m, links, shape):
    rows, local, chan, n_dp, block, wide_d = shape
    cap, heads = rows // n_dp, local // chan
    width, all_heads = 8 * wide_d, 2 * heads
    scale = (4 * chan) ** -0.5
    blocks, n_blocks = band(rows)
    low_rows = pl.ds(0, rows)

    b.scatter_copies = []
    partners = m.plane_peers + m.dp_peers
    barrier = pltpu.get_barrier_semaphore()
    for peer in partners:
        pl.semaphore_signal(barrier, inc=1, device_id=peer, device_id_type=MESH)
    own_copies = [
        pltpu.make_async_copy(own, hold.at[m.z], b.local_sem.at[k])
        for k, (own, hold) in enumerate(
            ((b.own_cell, b.up_cell), (b.own_gate, b.up_gate), (b.own_down, b.down))
        )
    ]
    for copy in own_copies:
        copy.start()
    own_place = pl.ds(pl.multiple_of(m.z * cap, 16), cap)

    def slots_of(source):
        return b.permutation[pl.ds(pl.multiple_of(source * rows, rows), rows)].reshape(1, rows)

    b.gains[m.slot] = jnp.broadcast_to(b.ln_gain[...].astype(F32).reshape(1, wide_d), (8, wide_d))
    b.valids[m.z] = jnp.broadcast_to(b.valid[...].astype(F32).reshape(1, rows), (8, rows))
    count = block // 2 if block % 256 == 0 else block
    cells = [
        Ring(links, b.up_cell, pl.ds(at, count), m.ring_next, m.owners)
        for at in range(0, block, count)
    ]
    gate = Ring(links, b.up_gate, pl.ds(0, block), m.ring_next, m.owners)
    down = Ring(links, b.down, pl.ds(0, local), m.ring_next, m.owners)
    if n_dp <= 4:
        mixed_ring = LineGather(links, b.mixed_all, m, n_dp)
    else:
        mixed_ring = Ring(links, b.mixed_all, pl.ds(0, rows), m.ring_next, m.owners)
    own_copies[0].wait()
    pl.semaphore_wait(barrier, len(partners))
    cells[0].start()

    digits = rows.bit_length() - 1
    packs = max(8, n_dp)
    own = slots_of(m.z)
    dest = lax.shift_right_logical(own, digits)
    to_pack = lax.broadcasted_iota(jnp.int32, (packs, rows), 0) == dest
    ahead = prefix_lanes(jnp.where(to_pack, 1.0, 0.0))
    rank = jnp.sum(jnp.where(to_pack, ahead, 0.0), axis=0, keepdims=True).astype(jnp.int32) - 1
    line = lax.broadcasted_iota(jnp.int32, (rows, rows), 0)
    b.send_map[...] = jnp.where(line == dest * cap + rank, 1.0, 0.0).astype(BF)
    b.sent_tokens[...] = mm(b.send_map[...], b.tokens[...]).astype(BF)
    b.full[m.slot, own_place] = b.sent_tokens[own_place]

    def exchange(out, into):
        copies = []
        for d, peer in enumerate(m.dp_peers):
            place = pl.ds(pl.multiple_of(lax.rem(m.z + d + 1, n_dp) * cap, 16), cap)
            copies.append(links.go(out.at[place], into.at[own_place], peer))
        return copies

    b.exchange = exchange
    a2a = exchange(b.sent_tokens, b.full.at[m.slot])
    b.token_copies = a2a
    for ring in cells[1:]:
        ring.start()
    one = pl.ds(0, 1)
    gain_copies = [
        links.go(b.gains.at[m.slot], b.gains.at[m.slot], peer) for peer in m.plane_peers
    ]
    valid_copies = [
        links.go(b.valids.at[m.z, one], b.valids.at[m.z, one], peer) for peer in m.dp_peers
    ]
    for copy in own_copies[1:]:
        copy.wait()

    b.wide_f[...] = jnp.zeros((rows, rows), F32)

    def place_source(s, carry):
        perm = slots_of(s)
        mine = lax.shift_right_logical(perm, digits) == m.z
        ahead = prefix_lanes(jnp.broadcast_to(jnp.where(mine, 1.0, 0.0), (8, rows)))[:1]
        at = jnp.where(mine, s * cap + ahead.astype(jnp.int32) - 1, -1)
        slot = perm - m.z * rows
        slots = jnp.where(line == slot, 1.0, 0.0).astype(BF)
        places = jnp.where(line == at, 1.0, 0.0).astype(BF)
        b.wide_f[...] += mm_nt(slots, places)
        return carry

    lax.fori_loop(0, n_dp, place_source, 0)
    b.recv_map[...] = b.wide_f[...].astype(BF)
    for copy in a2a:
        copy.wait_recv()
    cells[0].step()

    b.sums[...] = jnp.zeros((rows, 128), F32)
    b.squares[...] = jnp.zeros((rows, 128), F32)
    arrivals = 0
    for slot in plane_gather(links, m, b.full, rows):
        columns = pl.ds(pl.multiple_of(slot * wide_d, 128), wide_d)

        def place_rows(r, carry, slot=slot, columns=columns):
            at = pl.ds(pl.multiple_of(r * LINE, LINE), LINE)
            x = mm(b.recv_map[at], b.full[slot])
            b.normed[at, columns] = x.astype(BF)
            b.sums[at] += jnp.sum(x, axis=1, keepdims=True)
            b.squares[at] += jnp.sum(x * x, axis=1, keepdims=True)
            return carry

        lax.fori_loop(0, rows // LINE, place_rows, 0)
        arrivals += 1
        if arrivals in (3, 8):
            cells[-1].step()
        if arrivals == 6:
            cells[0].step()
    own_columns = pl.ds(pl.multiple_of(m.slot * wide_d, 128), wide_d)
    b.x_own[...] = b.normed[:, own_columns]
    b.sent_goal[...] = mm(b.send_map[...], b.targets[...]).astype(BF)
    b.goal_places[own_place] = b.sent_goal[own_place]
    for copy in gain_copies:
        copy.wait_recv()

    def normalise(r, carry):
        at = pl.ds(pl.multiple_of(r * 64, 64), 64)
        mean = b.sums[at][:, :1] / width
        var = b.squares[at][:, :1] / width - mean * mean
        rstd = root_inverse(var + EPSILON)
        b.sums[at] = jnp.broadcast_to(mean, (64, 128))
        b.squares[at] = jnp.broadcast_to(rstd, (64, 128))
        for i in range(8):
            x = b.normed[at, i * wide_d : (i + 1) * wide_d].astype(F32)
            x = (x - mean) * rstd * b.gains[i, :1]
            b.normed[at, i * wide_d : (i + 1) * wide_d] = x.astype(BF)
        return carry

    lax.fori_loop(0, rows // 64, normalise, 0)

    def project(hold, rings, target):
        count = block // len(rings)
        for s in range(n_dp):
            owner = m.owners[s]
            for r, ring in enumerate(rings):
                while ring.at < s:
                    ring.step()
                columns = pl.ds(pl.multiple_of(owner * block + r * count, 128), count)
                product = mm(b.normed[:, columns], hold[owner, r * count : (r + 1) * count])
                target[...] = product if s + r == 0 else target[...] + product

    for ring in cells:
        ring.last_leg()
    gate.start()
    down.start()
    project(b.up_cell, cells, b.wide_f)

    for h in range(heads):
        at = slice(h * chan, (h + 1) * chan)
        for j in range(4):
            b.chan_params[j : j + 1, at] = b.conv_weight[j].astype(F32)[h : h + 1]
        for j, ref in ((4, b.conv_bias), (5, b.group_gain), (6, b.skip_gain)):
            b.chan_params[j : j + 1, at] = ref[...].astype(F32)[h : h + 1]
        for s in range(3):
            for i in range(4):
                tap = b.qkv_weight[s, i].astype(F32)[h : h + 1]
                b.maps8[s, h, i : i + 1] = tap
                b.maps8[s, h, i + 4 : i + 5] = tap
            for g in range(2 * all_heads):
                row = b.gate_weight[g // all_heads, g % all_heads, s].astype(F32)[h : h + 1]
                b.gates_f[g : g + 1, s * local + h * chan : s * local + (h + 1) * chan] = row
    b.gates_f[8:] = jnp.zeros((8, 3 * local), F32)
    b.gates_w[...] = b.gates_f[...].astype(BF)
    place = lax.broadcasted_iota(jnp.int32, (rows, 1), 0)
    ends, total = [], 0
    for k in range(b.lengths.shape[1]):
        total = total + b.lengths[m.z, k]
        ends.append(total)
    begin = jnp.zeros((rows, 1), jnp.int32)
    for end in ends:
        begin = jnp.where(place >= end, end, begin)
    b.begin[...] = jnp.broadcast_to(begin, (rows, 128))

    def convolve(i, carry):
        at = pl.ds(pl.multiple_of(i * 128, 128), 128)
        low = b.wide_f[:, at].astype(BF)
        b.branch[:, at] = low
        x = low.astype(F32)
        since = lax.broadcasted_iota(jnp.int32, (rows, 128), 0) - b.begin[...]
        conv = b.chan_params[4:5, at] + b.chan_params[0:1, at] * x
        for j in range(1, 4):
            back = b.chan_params[j : j + 1, at] * pltpu.roll(x, j, 0)
            conv = conv + jnp.where(since >= j, back, 0.0)
        sig = sigmoid(conv)
        act = conv * sig
        b.act[:, at] = act
        b.slope[:, at] = sig + act * (1.0 - sig)
        return carry

    lax.fori_loop(0, local // 128, convolve, 0)
    r_map = lax.broadcasted_iota(jnp.int32, (chan, chan), 0) // 4
    c_map = lax.broadcasted_iota(jnp.int32, (chan, chan), 1) // 4
    same = r_map == c_map
    for s in range(3):
        for h in range(heads):
            base = b.maps8[s, h]
            dense = jnp.broadcast_to(base[None], (chan // 8, 8, chan)).reshape(chan, chan)
            b.maps[s, h] = jnp.where(same, dense, 0.0).astype(BF)
    for h in range(heads):
        at = slice(h * chan, (h + 1) * chan)
        act = b.act[:, at]
        high, rest = split(act)
        least = ((act - high.astype(F32)) - rest.astype(F32)).astype(BF)
        for s in range(2):
            b.qkv[:, s * local + h * chan : s * local + (h + 1) * chan] = (
                mm(high, b.maps[s, h]) + (mm(rest, b.maps[s, h]) + mm(least, b.maps[s, h]))
            ).astype(BF)
        b.qkv[:, 2 * local + h * chan : 2 * local + (h + 1) * chan] = mm(
            b.branch[:, at], b.maps[2, h]
        ).astype(BF)

    pre_part = mm_nt(b.gates_w[...], b.qkv[...])[:8]
    pre_sum = push_sum(links, m, pre_part, b.pre_box, m.plane_peers, m.slot, 8)

    def q_of(h, i):
        return b.qkv[i * LINE : (i + 1) * LINE, h * chan : (h + 1) * chan]

    def k_of(h, low, n):
        return b.qkv[
            low * LINE : (low + n) * LINE, local + h * chan : local + (h + 1) * chan
        ]

    def v_of(h, low, n):
        return b.qkv[
            low * LINE : (low + n) * LINE, 2 * local + h * chan : 2 * local + (h + 1) * chan
        ]

    b.of = (q_of, k_of, v_of)
    for h in range(heads):
        for i, low, at, n in blocks:
            tile = mm_nt(q_of(h, i), k_of(h, low, n))
            for k in range(n):
                b.score_part[h, at + k] = tile[:, k * LINE : (k + 1) * LINE]
    other = links.go(b.score_part.at[1 - m.core], b.score_in.at[0], m.sib)
    b.score_copy = other
    other.wait_recv()
    b.score_sum[...] = b.score_part[m.core] + b.score_in[0]
    far = links.go(b.score_sum, b.score_in.at[1], m.yn)

    line81 = lax.broadcasted_iota(jnp.int32, (8, 1), 0)
    given = b.gate_bias[...].astype(F32)
    bias = jnp.zeros((8, 1), F32)
    for g in range(2):
        for o in range(all_heads):
            bias = jnp.where(line81 == g * all_heads + o, given[g : g + 1, o : o + 1], bias)
    pre = pre_sum() + bias
    b.pre[...] = pre
    line8 = lax.broadcasted_iota(jnp.int32, (8, rows), 0)
    head = m.c * heads + m.core
    in_gate = jnp.sum(jnp.where(line8 == head, pre, 0.0), axis=0, keepdims=True)
    forget = jnp.sum(jnp.where(line8 == head + all_heads, pre, 0.0), axis=0, keepdims=True)
    log_forget = jnp.minimum(forget, 0.0) - jnp.log(1.0 + jnp.exp(-jnp.abs(forget)))
    rising = prefix_lanes(jnp.broadcast_to(log_forget, (8, rows)))
    rise_col = to_columns(rising)
    gate_line = in_gate - rising[:1]
    gate.step()
    for copy in valid_copies:
        copy.wait_recv()
    b.keep[...] = jnp.zeros((rows, 128), F32)

    def take_source(s, carry):
        perm = slots_of(s)
        valid = b.valids[s][:1]
        pack = lax.shift_right_logical(perm, digits)
        lasts = jnp.zeros((1, rows), jnp.int32)
        for p in range(n_dp):
            last = sum(b.lengths[p, k] for k in range(b.lengths.shape[1]))
            lasts = jnp.where(pack == p, last, lasts)
        counted = jnp.where(perm - pack * rows < lasts, valid, 0.0)
        hits = jnp.where(line == perm - m.z * rows, counted, 0.0)
        b.keep[...] += jnp.sum(hits, axis=1, keepdims=True)
        return carry + jnp.sum(counted, axis=1, keepdims=True)

    valid_count = lax.fori_loop(0, n_dp, take_source, jnp.zeros((1, 1), F32))
    keep = b.keep[:, :1]
    far.wait_recv()
    b.score_part[m.core] = b.score_sum[...] + b.score_in[1]
    for i, low, at, n in blocks:
        lines = slice(i * LINE, (i + 1) * LINE)
        t_at = i * LINE + lax.broadcasted_iota(jnp.int32, (LINE, n * LINE), 0)
        s_at = low * LINE + lax.broadcasted_iota(jnp.int32, (LINE, n * LINE), 1)
        allowed = (s_at <= t_at) & (s_at >= b.begin[lines][:, :1])
        logit = jnp.where(
            allowed, rise_col[lines][:, :1] + gate_line[:, low * LINE : (low + n) * LINE], NEG_FILL
        )
        top = jnp.max(logit, axis=1, keepdims=True)
        decay = jnp.where(allowed, jnp.exp(logit - top), 0.0) * scale
        weight = wide(b.score_part, m.core, at, n) * decay
        den = jnp.sum(weight, axis=1, keepdims=True)
        floor = jnp.exp(-top)
        inv = 1.0 / jnp.maximum(jnp.abs(den), floor)
        shares = (weight * inv).astype(BF)
        b.inv[lines] = jnp.broadcast_to(inv, (LINE, 128))
        sign = jnp.where(jnp.abs(den) > floor, jnp.where(den > 0.0, 1.0, -1.0), 0.0)
        b.sign[lines] = jnp.broadcast_to(sign, (LINE, 128))
        for k in range(n):
            b.decay[at + k] = decay[:, k * LINE : (k + 1) * LINE]
            b.weight[at + k] = weight[:, k * LINE : (k + 1) * LINE]
            b.share[m.core, at + k] = shares[:, k * LINE : (k + 1) * LINE]
    shared = links.go(b.share.at[m.core], b.share.at[m.core], m.sib)
    gate.step()
    shared.wait_recv()
    columns = []
    for h in range(heads):
        for i, low, at, n in blocks:
            lines = slice(i * LINE, (i + 1) * LINE)
            b.hidden[lines, h * chan : (h + 1) * chan] = mm(
                wide(b.share, h, at, n), v_of(h, low, n)
            )
        hid = b.hidden[:, h * chan : (h + 1) * chan]
        columns.append(jnp.sum(hid, axis=1, keepdims=True))
        columns.append(jnp.sum(hid * hid, axis=1, keepdims=True))
    moment_sum = push_sum(
        links, m, to_lanes(columns, rows), b.moment_box, m.tensor_peers, m.t, 4
    )
    gate.finish()
    down.step()
    project(b.up_gate, (gate,), b.wide_f)
    moments = to_columns(moment_sum()) / (4 * chan)
    for h in range(heads):
        mean = moments[:, 2 * h : 2 * h + 1]
        rstd = root_inverse(moments[:, 2 * h + 1 : 2 * h + 2] - mean * mean + EPSILON)
        b.head_rstd[h] = jnp.broadcast_to(rstd, (rows, 128))
        b.head_mean[h] = jnp.broadcast_to(mean, (rows, 128))
    down.step()

    def mix(i, carry):
        at = pl.ds(pl.multiple_of(i * 128, 128), 128)
        h = lax.div(i, chan // 128)
        hat = (b.hidden[:, at] - b.head_mean[h]) * b.head_rstd[h]
        b.hidden[:, at] = hat
        low = b.wide_f[:, at].astype(BF)
        b.gate_low[:, at] = low
        g = low.astype(F32)
        inner = hat * b.chan_params[5:6, at] + b.chan_params[6:7, at] * b.act[:, at]
        b.mixed_all[m.z, :, at] = (inner * (g * sigmoid(g))).astype(BF)
        return carry

    lax.fori_loop(0, local // 128, mix, 0)
    down.last_leg()
    goal_copies = exchange(b.sent_goal, b.goal_places)
    mixed_ring.start()
    down.finish()
    piece = min(block, wide_d)

    def down_part(y, core, x):
        slot = (y * 2 + core) * 2 + x
        parts = []
        for k in range(wide_d // piece):
            if block >= 2 * wide_d:
                owner = lax.div((y * 2 + core) * 2 * wide_d, block)
                parts.append(mm(b.mixed_all[m.z], b.down[owner, :, x * wide_d : (x + 1) * wide_d]))
            else:
                owner = lax.div(slot * wide_d, block) + k
                parts.append(mm(b.mixed_all[m.z], b.down[owner]))
        return jnp.concatenate(parts, axis=1)

    own_k = m.y * 2 + m.c
    summed = plane_scatter(links, m, down_part, b, rows, (idle, mixed_ring.step, idle))
    loss_sum = jnp.zeros((1, 1), F32)
    b.arriving = []
    size = rows // GROUPS
    for copy in goal_copies:
        copy.wait_recv()
    b.goal[...] = mm(b.recv_map[...], b.goal_places[...]).astype(BF)
    for g, at in summed:
        result = (b.x_own[at].astype(F32) + b.acc[own_k, at]).astype(BF)
        b.result[at] = result
        difference = result.astype(F32) - b.goal[at].astype(F32)
        own_gradient = ((rows * n_dp) / valid_count * keep[at] * difference).astype(BF)
        b.full[m.slot, at] = own_gradient
        arriving = plane_gather(links, m, b.full, size, g * size)
        slot = next(arriving)
        b.arriving.append(itertools.chain([slot], arriving))
        b.own_gradient[at] = own_gradient
        per_row = jnp.sum(difference * difference, axis=1, keepdims=True)
        loss_sum = loss_sum + jnp.sum(keep[at] * 0.5 * per_row, axis=0, keepdims=True)
    b.loss_part[...] = jnp.broadcast_to(loss_sum / valid_count, (8, 128))
    b.mixed_ring = mixed_ring

    b.sent_out[...] = mm_tn(b.recv_map[...], b.result[...]).astype(BF)
    b.home_out[own_place] = b.sent_out[own_place]
    b.home_copies = exchange(b.sent_out, b.home_out)


def backward(b, m, links, shape):
    rows, local, chan, n_dp, block, wide_d = shape
    cap, heads = rows // n_dp, local // chan
    all_heads = 2 * heads
    width, head_width = 8 * wide_d, 4 * chan
    blocks, n_blocks = band(rows)
    q_of, k_of, v_of = b.of
    line8 = lax.broadcasted_iota(jnp.int32, (8, rows), 0)
    head = m.c * heads + m.core

    size = rows // GROUPS
    for turn, slots in enumerate(zip(*b.arriving)):
        for g, slot in enumerate(slots):
            lines = slice(g * size, (g + 1) * size)
            grads = b.full[slot, lines]
            if block >= wide_d:
                ratio = block // wide_d
                at = pl.ds(pl.multiple_of(lax.rem(slot, ratio) * wide_d, 128), wide_d)
                product = mm_nt(grads, b.down[lax.div(slot, ratio), :, at])
            else:
                ratio = wide_d // block
                product = sum(
                    mm_nt(grads[:, k * block : (k + 1) * block], b.down[slot * ratio + k])
                    for k in range(ratio)
                )
            b.wide_f[lines] = product if turn == 0 else b.wide_f[lines] + product
        if turn == 5:
            b.mixed_ring.step()
    for arriving in b.arriving:
        for _ in arriving:
            pass

    per = rows // 8
    own_rows = pl.ds(pl.multiple_of(m.slot * per, 16), per)
    for d in range(n_dp):
        to = m.z if d == 0 else m.dp_peers[d - 1][0]
        if block >= wide_d:
            ratio = block // wide_d
            for k in range(ratio):
                b.cols_out[to, :, k * wide_d : (k + 1) * wide_d] = b.full[to * ratio + k, own_rows]
        else:
            ratio = wide_d // block
            at = pl.ds(pl.multiple_of(lax.rem(to, ratio) * block, 128), block)
            b.cols_out[to] = b.full[lax.div(to, ratio), own_rows, at]
    from_here = pl.ds(pl.multiple_of(m.z * per, 16), per)
    b.cols[m.slot, from_here] = b.cols_out[m.z]
    cols_copies = [
        links.go(b.cols_out.at[peer[0]], b.cols.at[m.slot, from_here], peer)
        for peer in m.dp_peers
    ]

    def sum_down():
        for copy in cols_copies:
            copy.wait_recv()
        b.mixed_ring.finish()
        b.grad_down[...] = jnp.zeros((local, block), F32)
        for slot in plane_gather(links, m, b.cols, n_dp * per):
            at = pl.ds(pl.multiple_of(slot * per, 16), per)
            for p in range(0, n_dp, 4):
                left = jnp.concatenate([b.mixed_all[p + k, at] for k in range(4)], axis=0)
                b.grad_down[...] += mm_tn(left, b.cols[slot, p * per : (p + 4) * per])
            yield

    down_sum = sum_down()

    def advance(steps):
        for _ in range(steps):
            next(down_sum, None)

    def up_ring(grads, hold, g, h):
        at_h = slice(h * chan, (h + 1) * chan)

        def part(owner):
            at = pl.ds(pl.multiple_of(owner * block, 128), block)
            return mm_tn(b.normed[:, at], grads[:, at_h])

        def keep(total):
            b.grad_up[:, g, h] = total

        return (LineSum if n_dp <= 4 else RingSum)(links, part, hold.at[h], keep, m, n_dp)

    gates = [up_ring(b.g_gate, b.ring_gate, 1, h) for h in range(heads)]
    cells = [up_ring(b.g_cell, b.ring_cell, 0, h) for h in range(heads)]

    def ticks(rings):
        for _ in range(n_dp):
            for ring in rings:
                yield ring.step()

    gate_ticks, cell_ticks = ticks(gates), ticks(cells)

    def tick(source):
        return lambda: next(source, None)

    def unmix(i, carry):
        at = pl.ds(pl.multiple_of(i * 128, 128), 128)
        gm = b.wide_f[:, at]
        g = b.gate_low[:, at].astype(F32)
        sig = sigmoid(g)
        silu = g * sig
        hat, act = b.hidden[:, at], b.act[:, at]
        group, skip = b.chan_params[5:6, at], b.chan_params[6:7, at]
        inner = hat * group + skip * act
        b.g_gate[:, at] = (gm * inner * (sig + silu * (1.0 - sig))).astype(BF)
        gi = gm * silu
        b.small[5:6, at] = jnp.sum(gi * hat, axis=0, keepdims=True)
        b.small[6:7, at] = jnp.sum(gi * act, axis=0, keepdims=True)
        b.g_act[:, at] = gi * skip
        b.wide_f[:, at] = gi * group
        return carry

    lax.fori_loop(0, local // 128, unmix, 0)
    b.mixed_ring.last_leg()
    next(gate_ticks)
    next(gate_ticks)
    columns = []
    for h in range(heads):
        u = b.wide_f[:, h * chan : (h + 1) * chan]
        columns.append(jnp.sum(u, axis=1, keepdims=True))
        columns.append(
            jnp.sum(u * b.hidden[:, h * chan : (h + 1) * chan], axis=1, keepdims=True)
        )
    u_sum = push_sum(links, m, to_lanes(columns, rows), b.u_box, m.tensor_peers, m.t, 4)
    u_moments = to_columns(u_sum())
    rhos = []
    for h in range(heads):
        at = slice(h * chan, (h + 1) * chan)
        rstd = b.head_rstd[h][:, :1]
        mean_u = u_moments[:, 2 * h : 2 * h + 1] / head_width
        sum_ux = u_moments[:, 2 * h + 1 : 2 * h + 2]
        d_hidden = rstd * (b.wide_f[:, at] - mean_u - b.hidden[:, at] * (sum_ux / head_width))
        b.d_hidden[:, at] = d_hidden.astype(BF)
        rhos.append(sum_ux * (EPSILON * rstd * rstd))
    rho = jnp.where(m.core == 0, rhos[0], rhos[1])
    links.settle([b.score_copy])
    for h in range(heads):
        for i, low, at, n in blocks:
            tile = mm_nt(
                b.d_hidden[i * LINE : (i + 1) * LINE, h * chan : (h + 1) * chan], v_of(h, low, n)
            )
            for k in range(n):
                b.score_part[h, at + k] = tile[:, k * LINE : (k + 1) * LINE]
    other = links.go(b.score_part.at[1 - m.core], b.score_in.at[0], m.sib)
    other.wait_recv()
    b.share_out[...] = (b.score_part[m.core] + b.score_in[0]).astype(BF)
    far = links.go(b.share_out, b.share_in, m.yn)
    far.wait_recv()
    b.lines[...] = jnp.zeros((8, rows), F32)
    for i, low, at, n in blocks:
        lines = slice(i * LINE, (i + 1) * LINE)
        across = slice(low * LINE, (low + n) * LINE)

        def spread(ref):
            return jnp.concatenate([ref[at + k].astype(F32) for k in range(n)], axis=1)

        inv, sign, radial = b.inv[lines][:, :1], b.sign[lines][:, :1], rho[lines]
        weight = spread(b.weight)
        full = (spread(b.share_out) + spread(b.share_in)) * inv - sign * radial * inv
        exact = jnp.where(sign == 0.0, radial, 0.0)
        noisy = jnp.sum(full * weight, axis=1, keepdims=True)
        square = jnp.sum(weight * weight, axis=1, keepdims=True)
        full = full - weight * ((noisy - exact) / jnp.where(square > 0.0, square, 1.0))
        d_score = (full * spread(b.decay)).astype(BF)
        for k in range(n):
            b.d_score[m.core, at + k] = d_score[:, k * LINE : (k + 1) * LINE]
        b.lines[0:1, across] += jnp.sum(full * weight, axis=0, keepdims=True)
        b.keep[lines] = jnp.broadcast_to(exact, (LINE, 128))
    next(gate_ticks)
    scored = links.go(b.d_score.at[m.core], b.d_score.at[m.core], m.sib)
    over_cols = b.lines[0:1]
    over_rows = b.keep[...].T[0:1]
    delta = jnp.broadcast_to(over_rows - over_cols, (8, rows))
    after = jnp.sum(delta, axis=1, keepdims=True) - prefix_lanes(delta) + delta
    forget = jnp.sum(jnp.where(line8 == head + all_heads, b.pre[...], 0.0), axis=0, keepdims=True)
    d_forget = after[:1] / (1.0 + jnp.exp(forget))
    own_lines = jnp.where(line8 == head, over_cols, 0.0) + jnp.where(
        line8 == head + all_heads, d_forget, 0.0
    )
    head_peers = [
        m.sib,
        m.xn,
        (m.z, m.sib_t, m.other_c),
    ]
    pre_sum = push_sum(links, m, own_lines, b.grad_box, head_peers, m.c * 2 + m.core, 4)

    for h in range(heads):
        at = slice(2 * local + h * chan, 2 * local + (h + 1) * chan)
        b.g_proj[:, at] = jnp.zeros((rows, chan), F32)
        for i, low, place, n in blocks:
            d_hid = b.d_hidden[i * LINE : (i + 1) * LINE, h * chan : (h + 1) * chan]
            b.g_proj[low * LINE : (low + n) * LINE, at] += mm_tn(wide(b.share, h, place, n), d_hid)
    next(gate_ticks)
    scored.wait_recv()
    for h in range(heads):
        at = slice(h * chan, (h + 1) * chan)
        k_at = slice(local + h * chan, local + (h + 1) * chan)
        b.g_proj[:, k_at] = jnp.zeros((rows, chan), F32)
        for i, low, place, n in blocks:
            tile = wide(b.d_score, h, place, n)
            b.g_proj[i * LINE : (i + 1) * LINE, at] = mm(tile, k_of(h, low, n))
            b.g_proj[low * LINE : (low + n) * LINE, k_at] += mm_tn(tile, q_of(h, i))
    pre_grad = pre_sum()
    next(gate_ticks)
    advance(1)
    pre16 = jnp.concatenate([pre_grad, jnp.zeros((8, rows), F32)], axis=0)
    high, rest = split(pre16)
    b.g_proj[...] += mm_tn(high, b.gates_w[...]) + mm_tn(rest, b.gates_w[...])
    gate_grad = (mm(high, b.qkv[...]) + mm(rest, b.qkv[...]))[:8]
    for s in range(3):
        b.low_sum[8 * s : 8 * (s + 1)] = gate_grad[:, s * local : (s + 1) * local]
    bias_grad = jnp.sum(pre_grad, axis=1, keepdims=True)
    b.small[7:8, wide_d : wide_d + 128] = to_lanes_one(bias_grad)
    advance(2)

    r_map = lax.broadcasted_iota(jnp.int32, (chan, chan), 0) // 4
    c_map = lax.broadcasted_iota(jnp.int32, (chan, chan), 1) // 4
    same = r_map == c_map
    for h in range(heads):
        at = slice(h * chan, (h + 1) * chan)
        act_low = b.act[:, at].astype(BF)
        extra = None
        for s in range(3):
            low = b.g_proj[:, s * local + h * chan : s * local + (h + 1) * chan].astype(BF)
            left = act_low if s < 2 else b.branch[:, at]
            dense = jnp.where(same, mm_tn(left, low), 0.0)
            folded = jnp.sum(dense.reshape(chan // 8, 8, chan), axis=0)
            b.low_sum[24 + 4 * s : 28 + 4 * s, at] = folded[:4] + folded[4:]
            back = mm_nt(low, b.maps[s, h])
            if s == 0:
                extra = back
            elif s == 1:
                b.g_act[:, at] += extra + back
            else:
                b.wide_f[:, at] = back

    def unconvolve(i, carry):
        at = pl.ds(pl.multiple_of(i * 128, 128), 128)
        since = lax.broadcasted_iota(jnp.int32, (rows, 128), 0) - b.begin[...]
        x = b.branch[:, at].astype(F32)
        gc = b.g_act[:, at] * b.slope[:, at]
        gb = b.wide_f[:, at] + b.chan_params[0:1, at] * gc
        b.small[0:1, at] = jnp.sum(gc * x, axis=0, keepdims=True)
        b.small[4:5, at] = jnp.sum(gc, axis=0, keepdims=True)
        for j in range(1, 4):
            kept = jnp.where(since >= j, gc, 0.0)
            gb = gb + b.chan_params[j : j + 1, at] * pltpu.roll(kept, rows - j, 0)
            b.small[j : j + 1, at] = jnp.sum(kept * pltpu.roll(x, j, 0), axis=0, keepdims=True)
        b.g_cell[:, at] = gb.astype(BF)
        return carry

    lax.fori_loop(0, local // 128, unconvolve, 0)
    next(gate_ticks)
    next(cell_ticks)
    next(cell_ticks)
    b.low_sum[36:] = jnp.zeros((12, local), F32)
    b.low_box[m.z] = b.low_sum[...].astype(BF)
    low_copies = [links.go(b.low_box.at[m.z], b.low_box.at[m.z], peer) for peer in m.dp_peers]
    advance(4)

    def up_part(y, core, x):
        slot = (y * 2 + core) * 2 + x
        if block >= wide_d:
            ratio = block // wide_d
            at = pl.ds(pl.multiple_of(lax.rem(slot, ratio) * wide_d, 16), wide_d)
            owner = lax.div(slot, ratio)
            return mm_nt(b.g_cell[...], b.up_cell[owner, at]) + mm_nt(
                b.g_gate[...], b.up_gate[owner, at]
            )
        ratio = wide_d // block
        return jnp.concatenate(
            [
                mm_nt(b.g_cell[...], b.up_cell[slot * ratio + k])
                + mm_nt(b.g_gate[...], b.up_gate[slot * ratio + k])
                for k in range(ratio)
            ],
            axis=1,
        )

    own_k = m.y * 2 + m.c
    services = (lambda: advance(2), tick(gate_ticks), tick(gate_ticks))
    for _ in plane_scatter(links, m, up_part, b, rows, services):
        pass
    for _ in gate_ticks:
        pass
    grad_normed = b.acc[own_k]
    x_hat = (b.x_own[...].astype(F32) - b.sums[:, :1]) * b.squares[:, :1]
    grad_scaled = grad_normed * b.gains[m.slot, :1]
    line_sum = push_sum(
        links,
        m,
        to_lanes(
            [
                jnp.sum(grad_scaled, axis=1, keepdims=True),
                jnp.sum(grad_scaled * x_hat, axis=1, keepdims=True),
            ],
            rows,
        ),
        b.line_box,
        m.plane_peers,
        m.slot,
        8,
    )
    loss_sum = push_sum(links, m, b.loss_part[...], b.loss_box, m.plane_peers, m.slot, 8)
    b.small[7:8, :wide_d] = jnp.sum(grad_normed * x_hat, axis=0, keepdims=True)
    b.small[7:8, wide_d + 128 :] = loss_sum()[:1]
    b.small_box[m.z] = b.small[...]
    small_copies = [
        links.go(b.small_box.at[m.z], b.small_box.at[m.z], peer) for peer in m.dp_peers
    ]
    next(cell_ticks)
    lines = to_columns(line_sum()) / width
    grad_x = b.squares[:, :1] * (grad_scaled - lines[:, :1] - x_hat * lines[:, 1:2])
    own_grad = b.own_gradient[...].astype(F32)
    grad_slot = (own_grad + grad_x).astype(BF)
    links.settle(b.token_copies)
    b.sent_tokens[...] = mm_tn(b.recv_map[...], grad_slot).astype(BF)
    own_place = pl.ds(pl.multiple_of(m.z * cap, 16), cap)
    b.home_grad[own_place] = b.sent_tokens[own_place]
    copies = b.exchange(b.sent_tokens, b.home_grad)
    next(cell_ticks)
    for copy in b.home_copies:
        copy.wait_recv()
    b.output[...] = mm_tn(b.send_map[...], b.home_out[...]).astype(BF)
    next(cell_ticks)
    advance(3)
    for copy in small_copies + low_copies:
        copy.wait_recv()
    lows = b.low_box[0].astype(F32)
    for k in range(1, n_dp):
        lows = lows + b.low_box[k].astype(F32)
    b.low_sum[...] = lows
    total = b.small_box[0]
    for k in range(1, n_dp):
        total = total + b.small_box[k]
    b.small[...] = total
    b.loss[...] = total[7:8, wide_d + 128 : wide_d + 129]
    b.grad_ln[...] = total[7:8, :wide_d]
    for h in range(heads):
        at = slice(h * chan, (h + 1) * chan)
        for j in range(4):
            b.grad_conv_weight[j, h : h + 1] = b.small[j : j + 1, at]
        for j, ref in ((4, b.grad_conv_bias), (5, b.grad_group), (6, b.grad_skip)):
            ref[h : h + 1] = b.small[j : j + 1, at]
        for s in range(3):
            for i in range(4):
                k = 24 + 4 * s + i
                b.grad_qkv[s, i, h : h + 1] = b.low_sum[k : k + 1, at]
            for g in range(2 * all_heads):
                k = 8 * s + g
                b.grad_gate_weight[g // all_heads, g % all_heads, s, h : h + 1] = b.low_sum[
                    k : k + 1, at
                ]
    for g in range(2):
        at = wide_d + g * all_heads
        b.grad_gate_bias[g : g + 1] = total[7:8, at : at + all_heads]
    for _ in cell_ticks:
        pass
    for copy in copies:
        copy.wait_recv()
    b.grad_input[...] = mm_tn(b.send_map[...], b.home_grad[...]).astype(BF)
    for line in [b.mixed_ring] + gates + cells:
        line.settle()


def kernel(names, shape, limit, *refs):
    b = types.SimpleNamespace(**dict(zip(names, refs)))
    m = coordinates(shape[3])
    links = Links(b.send_sem, b.recv_sem, limit)
    forward(b, m, links, shape)
    backward(b, m, links, shape)
    links.close()


def carry_out(*refs):
    *ends, sems = refs
    half = len(ends) // 2
    copies = [
        pltpu.make_async_copy(ends[k], ends[half + k], sems.at[k]) for k in range(half)
    ]
    for copy in copies:
        copy.start()
    for copy in copies:
        copy.wait()


def shards(
    tokens,
    targets,
    ln_gain,
    up_weight,
    conv_weight,
    conv_bias,
    qkv_weight,
    gate_weight,
    gate_bias,
    group_gain,
    skip_gain,
    down_weight,
    lengths,
    permutation,
    valid,
):
    rows, wide_d = tokens.shape
    n_dp = lax.axis_size("dp")
    heads, chan = up_weight.shape[2], up_weight.shape[3]
    local = heads * chan
    block = up_weight.shape[0]
    width = 8 * wide_d
    up_halves = up_weight.transpose(1, 0, 2, 3).reshape(2, block, local)
    inputs = dict(
        tokens=tokens,
        targets=targets,
        permutation=permutation,
        valid=valid,
        own_cell=up_halves[0],
        own_gate=up_halves[1],
        own_down=down_weight.reshape(local, block),
        ln_gain=ln_gain,
        conv_weight=conv_weight,
        conv_bias=conv_bias,
        qkv_weight=qkv_weight,
        gate_weight=gate_weight,
        gate_bias=gate_bias,
        group_gain=group_gain,
        skip_gain=skip_gain,
        lengths=lengths,
    )
    outputs = dict(
        output=((rows, wide_d), BF),
        loss=((1, 1), F32),
        grad_input=((rows, wide_d), BF),
        grad_ln=((1, wide_d), F32),
        grad_up=(up_weight.shape, F32),
        grad_conv_weight=(conv_weight.shape, F32),
        grad_conv_bias=(conv_bias.shape, F32),
        grad_qkv=(qkv_weight.shape, F32),
        grad_gate_weight=(gate_weight.shape, F32),
        grad_gate_bias=(gate_bias.shape, F32),
        grad_group=(group_gain.shape, F32),
        grad_skip=(skip_gain.shape, F32),
        grad_down=((local, block), F32),
    )
    n_blocks = band(rows)[1]
    half = rows // 2
    limit = 180 + 18 * n_dp
    turns = (2 if n_dp <= 4 else 1, n_dp)
    scratch = dict(
        send_map=((rows, rows), BF),
        recv_map=((rows, rows), BF),
        chan_params=((8, local), F32),
        maps8=((3, heads, 8, chan), F32),
        gates_f=((16, 3 * local), F32),
        gates_w=((16, 3 * local), BF),
        sent_tokens=((rows, wide_d), BF),
        sent_goal=((rows, wide_d), BF),
        goal_places=((rows, wide_d), BF),
        valids=((n_dp, 8, rows), F32),
        keep=((rows, 128), F32),
        full=((8, rows, wide_d), BF),
        gains=((8, 8, wide_d), F32),
        up_cell=((n_dp, block, local), BF),
        up_gate=((n_dp, block, local), BF),
        down=((n_dp, local, block), BF),
        sums=((rows, 128), F32),
        squares=((rows, 128), F32),
        x_own=((rows, wide_d), BF),
        normed=((rows, width), BF),
        wide_f=((rows, local), F32),
        begin=((rows, 128), jnp.int32),
        branch=((rows, local), BF),
        act=((rows, local), F32),
        slope=((rows, local), F32),
        maps=((3, heads, chan, chan), BF),
        qkv=((rows, 3 * local), BF),
        pre_box=((8, 8, rows), F32),
        pre=((8, rows), F32),
        score_part=((heads, n_blocks, LINE, LINE), F32),
        score_in=((2, n_blocks, LINE, LINE), F32),
        score_sum=((n_blocks, LINE, LINE), F32),
        decay=((n_blocks, LINE, LINE), F32),
        weight=((n_blocks, LINE, LINE), F32),
        share=((heads, n_blocks, LINE, LINE), BF),
        inv=((rows, 128), F32),
        sign=((rows, 128), F32),
        hidden=((rows, local), F32),
        moment_box=((4, 8, rows), F32),
        head_rstd=((heads, rows, 128), F32),
        head_mean=((heads, rows, 128), F32),
        gate_low=((rows, local), BF),
        out=((4, rows, wide_d), BF),
        into=((4, rows, wide_d), BF),
        acc=((4, rows, wide_d), F32),
        small_out=((6 * GROUPS, half // GROUPS, wide_d), BF),
        small_in=((6 * GROUPS, half // GROUPS, wide_d), BF),
        loss_part=((8, 128), F32),
        goal=((rows, wide_d), BF),
        result=((rows, wide_d), BF),
        own_gradient=((rows, wide_d), BF),
        sent_out=((rows, wide_d), BF),
        home_out=((rows, wide_d), BF),
        home_grad=((rows, wide_d), BF),
        mixed_all=((n_dp, rows, local), BF),
        cols_out=((n_dp, rows // 8, block), BF),
        cols=((8, n_dp * rows // 8, block), BF),
        low_sum=((48, local), F32),
        low_box=((n_dp, 48, local), BF),
        ring_gate=((heads,) + turns + (block, chan), BF),
        ring_cell=((heads,) + turns + (block, chan), BF),
        g_gate=((rows, local), BF),
        g_cell=((rows, local), BF),
        small=((8, local), F32),
        small_box=((n_dp, 8, local), F32),
        g_act=((rows, local), F32),
        u_box=((4, 8, rows), F32),
        d_hidden=((rows, local), BF),
        share_out=((n_blocks, LINE, LINE), BF),
        share_in=((n_blocks, LINE, LINE), BF),
        lines=((8, rows), F32),
        d_score=((heads, n_blocks, LINE, LINE), BF),
        grad_box=((4, 8, rows), F32),
        g_proj=((rows, 3 * local), F32),
        line_box=((8, 8, rows), F32),
        loss_box=((8, 8, 128), F32),
    )
    vmem = pl.BlockSpec(memory_space=pltpu.VMEM)
    spaces = {name: pl.BlockSpec(memory_space=pl.ANY) for name in inputs if name[:4] == "own_"}
    spaces["lengths"] = pl.BlockSpec(memory_space=pltpu.SMEM)
    names = list(inputs) + list(outputs) + list(scratch) + ["send_sem", "recv_sem", "local_sem"]
    results = pl.pallas_call(
        lambda *refs: kernel(names, (rows, local, chan, n_dp, block, wide_d), limit, *refs),
        out_shape=[jax.ShapeDtypeStruct(*spec) for spec in outputs.values()],
        in_specs=[spaces.get(name, vmem) for name in inputs],
        out_specs=[vmem] * len(outputs),
        scratch_shapes=[pltpu.VMEM(*spec) for spec in scratch.values()]
        + [pltpu.SemaphoreType.DMA((limit,)), pltpu.SemaphoreType.DMA((limit,))]
        + [pltpu.SemaphoreType.DMA((3,))],
        compiler_params=pltpu.CompilerParams(
            collective_id=0, has_side_effects=True, vmem_limit_bytes=VMEM_LIMIT
        ),
    )(*inputs.values())
    results = pl.pallas_call(
        carry_out,
        out_shape=[jax.ShapeDtypeStruct(*spec) for spec in outputs.values()],
        in_specs=[pl.BlockSpec(memory_space=pl.ANY)] * len(outputs),
        out_specs=[vmem] * len(outputs),
        scratch_shapes=[pltpu.SemaphoreType.DMA((len(outputs),))],
    )(*results)
    o = types.SimpleNamespace(**dict(zip(outputs, results)))
    return (
        o.output,
        o.loss.reshape(()),
        o.grad_input,
        o.grad_ln.reshape(-1),
        o.grad_up,
        o.grad_conv_weight,
        o.grad_conv_bias,
        o.grad_qkv,
        o.grad_gate_weight,
        o.grad_gate_bias,
        o.grad_group,
        o.grad_skip,
        o.grad_down.reshape(down_weight.shape),
    )


def solution(mesh):
    return jax.shard_map(
        shards,
        mesh=mesh,
        in_specs=(
            P("dp", ("tensor", "ctx")),
            P("dp", ("tensor", "ctx")),
            P(("tensor", "ctx")),
            P("dp", None, "ctx", "tensor"),
            P(None, "ctx", "tensor"),
            P("ctx", "tensor"),
            P(None, None, "ctx", "tensor"),
            P(None, None, None, "ctx", "tensor"),
            P(),
            P("ctx", "tensor"),
            P("ctx", "tensor"),
            P("ctx", "tensor", "dp"),
            P(),
            P(),
            P("dp"),
        ),
        out_specs=(
            P("dp", ("tensor", "ctx")),
            P(),
            P("dp", ("tensor", "ctx")),
            P(("tensor", "ctx")),
            P("dp", None, "ctx", "tensor"),
            P(None, "ctx", "tensor"),
            P("ctx", "tensor"),
            P(None, None, "ctx", "tensor"),
            P(None, None, None, "ctx", "tensor"),
            P(),
            P("ctx", "tensor"),
            P("ctx", "tensor"),
            P("ctx", "tensor", "dp"),
        ),
        check_vma=False,
    )
```

```python
import itertools
import types

import jax
import jax.numpy as jnp
from jax import lax
from jax.experimental import pallas as pl
from jax.experimental.pallas import tpu as pltpu
from jax.sharding import PartitionSpec as P

NEG_FILL = -1e30
EPSILON = 1e-05
BF = jnp.bfloat16
F32 = jnp.float32
MESH = pl.DeviceIdType.MESH
VMEM_LIMIT = 62 * 1024 * 1024
LINE = 128
GROUPS = 2
BAND = 2


def mm(a, b):
    return jnp.dot(a, b, preferred_element_type=F32)


def mm_nt(a, b):
    return lax.dot_general(a, b, (((1,), (1,)), ((), ())), preferred_element_type=F32)


def mm_tn(a, b):
    return lax.dot_general(a, b, (((0,), (0,)), ((), ())), preferred_element_type=F32)


def split(v):
    high = v.astype(BF)
    return high, (v - high.astype(F32)).astype(BF)


def root_inverse(v):
    guess = lax.rsqrt(v)
    return guess * (1.5 - 0.5 * v * guess * guess)


def sigmoid(v):
    return 1.0 / (1.0 + jnp.exp(-v))


class Links:
    def __init__(self, send, recv, limit):
        self.send, self.recv, self.limit = send, recv, limit
        self.used, self.open = 0, []

    def make(self, src, dst, peer):
        k = self.used
        self.used += 1
        assert k < self.limit
        copy = pltpu.make_async_remote_copy(
            src_ref=src,
            dst_ref=dst,
            send_sem=self.send.at[k],
            recv_sem=self.recv.at[k],
            device_id=peer,
            device_id_type=MESH,
        )
        return copy

    def go(self, src, dst, peer):
        copy = self.make(src, dst, peer)
        copy.start()
        self.open.append(copy)
        return copy

    def settle(self, copies):
        for copy in copies:
            copy.wait_send()
        self.open = [c for c in self.open if all(c is not done for done in copies)]

    def close(self):
        self.settle(list(self.open))


class Ring:
    def __init__(self, links, hold, part, next_peer, owners):
        self.links, self.hold, self.part = links, hold, part
        self.peer, self.owners = next_peer, owners
        self.flying, self.at = None, 0

    def start(self):
        block = self.hold.at[self.owners[self.at], self.part]
        self.flying = self.links.go(block, block, self.peer)

    def step(self):
        if self.at >= len(self.owners) - 1:
            return False
        if self.flying is None:
            self.start()
        self.flying.wait_recv()
        self.at += 1
        self.flying = None
        if self.at < len(self.owners) - 1:
            self.start()
            return True
        return False

    def last_leg(self):
        while self.at < len(self.owners) - 2:
            self.step()

    def finish(self):
        while self.step():
            pass

    def settle(self):
        self.links.close()


def when(condition, *actions):
    @pl.when(condition)
    def _():
        for action in actions:
            action()


class LineGather:
    def __init__(self, links, hold, m, count):
        self.z, self.count, self.at = m.z, count, 0
        z, last = m.z, count - 1
        self.ways = []
        for d in range(1, count):
            to_right = jnp.maximum(z - (d - 1), 0)
            to_left = jnp.minimum(z + (d - 1), last)
            self.ways.append(
                (
                    (
                        links.make(hold.at[to_right], hold.at[to_right], m.right),
                        (z < last) & (z >= d - 1),
                        z >= d,
                    ),
                    (
                        links.make(hold.at[to_left], hold.at[to_left], m.left),
                        (z > 0) & (z + d - 1 <= last),
                        z + d <= last,
                    ),
                )
            )

    def start(self):
        for copy, sends, _ in self.ways[self.at]:
            when(sends, copy.start)

    def step(self):
        if self.at >= self.count - 1:
            return
        for copy, _, receives in self.ways[self.at]:
            when(receives, copy.wait_recv)
        self.at += 1
        if self.at < self.count - 1:
            self.start()

    def last_leg(self):
        while self.at < self.count - 2:
            self.step()

    def finish(self):
        while self.at < self.count - 1:
            self.step()

    def settle(self):
        for pair in self.ways:
            for copy, sends, _ in pair:
                when(sends, copy.wait_send)


class LineSum:
    def __init__(self, links, part, hold, target, m, count, size):
        self.part, self.hold, self.target = part, hold, target
        self.z, self.count, self.at, self.size = m.z, count, 0, size
        places = (m.z, count - 1 - m.z)
        self.ways = [
            (
                places[way],
                [
                    links.make(hold.at[way, t], hold.at[way, t + 1], peer)
                    for t in range(count - 1)
                ],
            )
            for way, peer in enumerate((m.right, m.left))
        ]

    def step(self):
        t, count = self.at, self.count
        if t > count - 1:
            return
        self.at += 1
        size = self.size
        pieces = self.hold.shape[-2] // size

        def arrive(place, copies):
            if t:
                when((place > 0) & (place <= t), copies[t - 1].wait_recv)

        def lines(j):
            return pl.ds(pl.multiple_of(j * size, size), size)

        def add(way, place, own, j):
            if t:
                own = own + jnp.where(place > 0, self.hold[way, t, lines(j)].astype(F32), 0.0)
            return own

        if t == count - 1:
            for place, copies in self.ways:
                arrive(place, copies)

            def last(j, carry):
                total = self.part(self.z, j)
                for way, (place, _) in enumerate(self.ways):
                    total = add(way, place, total, j)
                self.target(total, lines(j))
                return carry

            lax.fori_loop(0, pieces, last, 0)
            return
        for way, (place, copies) in enumerate(self.ways):
            arrive(place, copies)

            def send(way=way, place=place, copies=copies):
                ahead = count - 1 - t
                owner = self.z + ahead if way == 0 else self.z - ahead

                def piece(j, carry):
                    self.hold[way, t, lines(j)] = add(
                        way, place, self.part(owner, j), j
                    ).astype(BF)
                    return carry

                lax.fori_loop(0, pieces, piece, 0)
                copies[t].start()

            when(place <= t, send)

    def settle(self):
        for place, copies in self.ways:
            for t, copy in enumerate(copies):
                when(place <= t, copy.wait_send)


class RingSum:
    def __init__(self, links, part, hold, target, m, count, size):
        self.links, self.part, self.hold, self.target = links, part, hold, target
        self.m, self.count, self.at = m, count, -1
        self.sent = []

    def step(self):
        if self.at >= self.count - 1:
            return
        self.at += 1
        own = self.part(self.m.owners[(self.at + 1) % self.count])
        if self.at:
            self.sent[-1].wait_recv()
            own = own + self.hold[0, self.at].astype(F32)
        if self.at == self.count - 1:
            self.target(own, pl.ds(0, own.shape[0]))
            return
        self.hold[0, self.at] = own.astype(BF)
        self.sent.append(
            self.links.go(
                self.hold.at[0, self.at], self.hold.at[0, self.at + 1], self.m.ring_next
            )
        )

    def settle(self):
        self.links.settle(self.sent)


def coordinates(dp_count):
    z, t, c = lax.axis_index("dp"), lax.axis_index("tensor"), lax.axis_index("ctx")
    core = lax.rem(t, 2)
    m = types.SimpleNamespace(z=z, t=t, c=c, core=core, y=lax.div(t, 2))
    m.sib_t, m.far_t, m.other_c = t + 1 - 2 * core, lax.rem(t + 2, 4), 1 - c
    m.sib, m.yn, m.xn = (z, m.sib_t, c), (z, m.far_t, c), (z, t, m.other_c)
    m.slot = t * 2 + c
    m.slot_x, m.slot_y, m.slot_d = t * 2 + m.other_c, m.far_t * 2 + c, m.far_t * 2 + m.other_c
    m.to_sib = 2 - 4 * core
    if dp_count == 4:
        def after(v):
            return lax.rem(2 * v + 1, 5)

        def before(v):
            return lax.rem(3 * v + 2, 5)
    else:
        def after(v):
            return lax.rem(v + 1, dp_count)

        def before(v):
            return lax.rem(v + dp_count - 1, dp_count)

    m.ring_next = (after(z), t, c)
    m.owners = [z]
    for _ in range(dp_count - 1):
        m.owners.append(before(m.owners[-1]))
    m.right = (lax.rem(z + 1, dp_count), t, c)
    m.left = (lax.rem(z + dp_count - 1, dp_count), t, c)
    m.dp_peers = [(lax.rem(z + d, dp_count), t, c) for d in range(1, dp_count)]
    m.plane_peers = [
        (z, lax.rem(t + dt, 4), lax.rem(c + dc, 2))
        for dt in range(4)
        for dc in range(2)
        if dt or dc
    ]
    m.tensor_peers = [(z, lax.rem(t + dt, 4), c) for dt in range(1, 4)]
    return m


def plane_gather(links, m, full, rows, base=0):
    half = rows // 2
    first, second, whole = pl.ds(base, half), pl.ds(base + half, half), pl.ds(base, rows)
    sent = []

    def send(slot, part, peer):
        sent.append(links.go(full.at[slot, part], full.at[slot, part], peer))
        return sent[-1]

    x_first = send(m.slot, first, m.xn)
    y_second = send(m.slot, second, m.yn)
    to_sib = send(m.slot, whole, m.sib)
    x_second = send(m.slot, second, m.xn)
    y_first = send(m.slot, first, m.yn)
    yield m.slot
    to_sib.wait_recv()
    yield m.slot + m.to_sib
    x_first.wait_recv()
    d_first = send(m.slot_x, first, m.yn)
    y_second.wait_recv()
    d_second = send(m.slot_y, second, m.xn)
    x_second.wait_recv()
    sib_x = send(m.slot_x, whole, m.sib)
    yield m.slot_x
    y_first.wait_recv()
    sib_y = send(m.slot_y, whole, m.sib)
    yield m.slot_y
    sib_x.wait_recv()
    yield m.slot_x + m.to_sib
    d_first.wait_recv()
    d_second.wait_recv()
    sib_d = send(m.slot_d, whole, m.sib)
    yield m.slot_d
    sib_y.wait_recv()
    yield m.slot_y + m.to_sib
    sib_d.wait_recv()
    yield m.slot_d + m.to_sib
    links.settle(sent)


def idle():
    pass


def to_lanes(columns, rows):
    lane = lax.broadcasted_iota(jnp.int32, (rows, 128), 1)
    out = jnp.zeros((rows, 128), F32)
    for j, column in enumerate(columns):
        out = jnp.where(lane == j, column, out)
    return out.T[:8]


def to_lanes_one(column):
    line = lax.broadcasted_iota(jnp.int32, (8, 128), 0)
    lane = lax.broadcasted_iota(jnp.int32, (8, 128), 1)
    return jnp.sum(jnp.where(line == lane, column, 0.0), axis=0, keepdims=True)


def to_columns(lines):
    rows = lines.shape[1]
    return jnp.concatenate([lines, jnp.zeros((120, rows), F32)], axis=0).T


def push_sum(links, m, lines, box, peers, own_place, count):
    box[own_place] = lines
    copies = [links.go(box.at[own_place], box.at[own_place], peer) for peer in peers]

    def finish():
        for copy in copies:
            copy.wait_recv()
        total = box[0]
        for k in range(1, count):
            total = total + box[k]
        return total

    return finish


def prefix_lanes(v):
    width = v.shape[1]
    lane = lax.broadcasted_iota(jnp.int32, v.shape, 1)
    step = 1
    while step < width:
        v = v + jnp.where(lane >= step, pltpu.roll(v, step, 1), 0.0)
        step *= 2
    return v


def band(rows):
    out, at = [], 0
    for i in range(rows // LINE):
        low = max(0, i - BAND)
        out.append((i, low, at, i - low + 1))
        at += i - low + 1
    return out, at


def wide(ref, h, at, width):
    return jnp.concatenate([ref[h, at + k] for k in range(width)], axis=1)


def plane_scatter(links, m, part, b, rows, services):
    size = rows // GROUPS
    half = size // 2
    own_k = m.y * 2 + m.c
    far_y = 1 - m.y
    links.settle(b.scatter_copies)
    copies = []
    for k in range(4):
        b.out[k] = part(k // 2, 1 - m.core, k % 2).astype(BF)
        for g in range(GROUPS):
            at = pl.ds(g * size, size)
            copies.append(links.go(b.out.at[k, at], b.into.at[k, at], m.sib))

    def own_part(k, carry):
        b.acc[k] = part(lax.div(k, 2), m.core, lax.rem(k, 2))
        return carry

    lax.fori_loop(0, 4, own_part, 0)
    b.scatter_copies = list(copies)
    services[0]()

    def send(g, place, k, at, peer):
        place += 6 * g
        b.small_out[place] = b.acc[k, at].astype(BF)
        copy = links.go(b.small_out.at[place], b.small_in.at[place], peer)
        b.scatter_copies.append(copy)
        return copy

    def receive(g, place, k, at, copy):
        copy.wait_recv()
        b.acc[k, at] += b.small_in[place + 6 * g].astype(F32)

    parts = [(pl.ds(g * size, half), pl.ds(g * size + half, half)) for g in range(GROUPS)]
    second_phase, third_phase = [], []
    for g, (first, second) in enumerate(parts):
        at = pl.ds(g * size, size)
        for k in range(4):
            copies[k * GROUPS + g].wait_recv()
            b.acc[k, at] += b.into[k, at].astype(F32)
        second_phase.append(
            [send(g, y, y * 2 + m.other_c, first, m.xn) for y in range(2)]
            + [send(g, 2 + x, far_y * 2 + x, second, m.yn) for x in range(2)]
        )
    services[1]()
    for g, (first, second) in enumerate(parts):
        flying = second_phase[g]
        for y in range(2):
            receive(g, y, y * 2 + m.c, first, flying[y])
        for x in range(2):
            receive(g, 2 + x, m.y * 2 + x, second, flying[2 + x])
        third_phase.append(
            (
                send(g, 4, far_y * 2 + m.c, first, m.yn),
                send(g, 5, m.y * 2 + m.other_c, second, m.xn),
            )
        )
    services[2]()
    for g, (first, second) in enumerate(parts):
        receive(g, 4, own_k, first, third_phase[g][0])
        receive(g, 5, own_k, second, third_phase[g][1])
        yield g, slice(g * size, (g + 1) * size)


def forward(b, m, links, shape):
    rows, local, chan, n_dp, block, wide_d = shape
    cap, heads = rows // n_dp, local // chan
    width, all_heads = 8 * wide_d, 2 * heads
    scale = (4 * chan) ** -0.5
    blocks, n_blocks = band(rows)
    low_rows = pl.ds(0, rows)

    b.scatter_copies = []
    partners = m.plane_peers + m.dp_peers
    barrier = pltpu.get_barrier_semaphore()
    for peer in partners:
        pl.semaphore_signal(barrier, inc=1, device_id=peer, device_id_type=MESH)
    own_copies = [
        pltpu.make_async_copy(own, hold.at[m.z], b.local_sem.at[k])
        for k, (own, hold) in enumerate(
            ((b.own_cell, b.up_cell), (b.own_gate, b.up_gate), (b.own_down, b.down))
        )
    ]
    for copy in own_copies:
        copy.start()
    own_place = pl.ds(pl.multiple_of(m.z * cap, 16), cap)

    def slots_of(source):
        return b.permutation[pl.ds(pl.multiple_of(source * rows, rows), rows)].reshape(1, rows)

    b.gains[m.slot] = jnp.broadcast_to(b.ln_gain[...].astype(F32).reshape(1, wide_d), (8, wide_d))
    b.valids[m.z] = jnp.broadcast_to(b.valid[...].astype(F32).reshape(1, rows), (8, rows))
    count = block // 2 if block % 256 == 0 else block
    cells = [
        Ring(links, b.up_cell, pl.ds(at, count), m.ring_next, m.owners)
        for at in range(0, block, count)
    ]
    gate = Ring(links, b.up_gate, pl.ds(0, block), m.ring_next, m.owners)
    down = Ring(links, b.down, pl.ds(0, local), m.ring_next, m.owners)
    if n_dp <= 4:
        mixed_ring = LineGather(links, b.mixed_all, m, n_dp)
    else:
        mixed_ring = Ring(links, b.mixed_all, pl.ds(0, rows), m.ring_next, m.owners)
    own_copies[0].wait()
    pl.semaphore_wait(barrier, len(partners))
    cells[0].start()

    digits = rows.bit_length() - 1
    packs = max(8, n_dp)
    own = slots_of(m.z)
    dest = lax.shift_right_logical(own, digits)
    to_pack = lax.broadcasted_iota(jnp.int32, (packs, rows), 0) == dest
    ahead = prefix_lanes(jnp.where(to_pack, 1.0, 0.0))
    rank = jnp.sum(jnp.where(to_pack, ahead, 0.0), axis=0, keepdims=True).astype(jnp.int32) - 1
    line = lax.broadcasted_iota(jnp.int32, (rows, rows), 0)
    b.send_map[...] = jnp.where(line == dest * cap + rank, 1.0, 0.0).astype(BF)
    b.sent_tokens[...] = mm(b.send_map[...], b.tokens[...]).astype(BF)
    b.full[m.slot, own_place] = b.sent_tokens[own_place]

    def exchange(out, into):
        copies = []
        for d, peer in enumerate(m.dp_peers):
            place = pl.ds(pl.multiple_of(lax.rem(m.z + d + 1, n_dp) * cap, 16), cap)
            copies.append(links.go(out.at[place], into.at[own_place], peer))
        return copies

    b.exchange = exchange
    a2a = exchange(b.sent_tokens, b.full.at[m.slot])
    b.token_copies = a2a
    for ring in cells[1:]:
        ring.start()
    one = pl.ds(0, 1)
    gain_copies = [
        links.go(b.gains.at[m.slot], b.gains.at[m.slot], peer) for peer in m.plane_peers
    ]
    valid_copies = [
        links.go(b.valids.at[m.z, one], b.valids.at[m.z, one], peer) for peer in m.dp_peers
    ]
    for copy in own_copies[1:]:
        copy.wait()

    b.wide_f[...] = jnp.zeros((rows, rows), F32)

    def place_source(s, carry):
        perm = slots_of(s)
        mine = lax.shift_right_logical(perm, digits) == m.z
        ahead = prefix_lanes(jnp.broadcast_to(jnp.where(mine, 1.0, 0.0), (8, rows)))[:1]
        at = jnp.where(mine, s * cap + ahead.astype(jnp.int32) - 1, -1)
        slot = perm - m.z * rows
        slots = jnp.where(line == slot, 1.0, 0.0).astype(BF)
        places = jnp.where(line == at, 1.0, 0.0).astype(BF)
        b.wide_f[...] += mm_nt(slots, places)
        return carry

    lax.fori_loop(0, n_dp, place_source, 0)
    b.recv_map[...] = b.wide_f[...].astype(BF)
    for copy in a2a:
        copy.wait_recv()
    cells[0].step()

    b.sums[...] = jnp.zeros((rows, 128), F32)
    b.squares[...] = jnp.zeros((rows, 128), F32)
    arrivals = 0
    for slot in plane_gather(links, m, b.full, rows):
        columns = pl.ds(pl.multiple_of(slot * wide_d, 128), wide_d)

        def place_rows(r, carry, slot=slot, columns=columns):
            at = pl.ds(pl.multiple_of(r * LINE, LINE), LINE)
            x = mm(b.recv_map[at], b.full[slot])
            b.normed[at, columns] = x.astype(BF)
            b.sums[at] += jnp.sum(x, axis=1, keepdims=True)
            b.squares[at] += jnp.sum(x * x, axis=1, keepdims=True)
            return carry

        lax.fori_loop(0, rows // LINE, place_rows, 0)
        arrivals += 1
        if arrivals in (3, 8):
            cells[-1].step()
        if arrivals == 6:
            cells[0].step()
    own_columns = pl.ds(pl.multiple_of(m.slot * wide_d, 128), wide_d)
    b.x_own[...] = b.normed[:, own_columns]
    b.sent_goal[...] = mm(b.send_map[...], b.targets[...]).astype(BF)
    b.goal_places[own_place] = b.sent_goal[own_place]
    for copy in gain_copies:
        copy.wait_recv()

    def normalise(r, carry):
        at = pl.ds(pl.multiple_of(r * 64, 64), 64)
        mean = b.sums[at][:, :1] / width
        var = b.squares[at][:, :1] / width - mean * mean
        rstd = root_inverse(var + EPSILON)
        b.sums[at] = jnp.broadcast_to(mean, (64, 128))
        b.squares[at] = jnp.broadcast_to(rstd, (64, 128))
        for i in range(8):
            x = b.normed[at, i * wide_d : (i + 1) * wide_d].astype(F32)
            x = (x - mean) * rstd * b.gains[i, :1]
            b.normed[at, i * wide_d : (i + 1) * wide_d] = x.astype(BF)
        return carry

    lax.fori_loop(0, rows // 64, normalise, 0)

    def project(hold, rings, target):
        count = block // len(rings)
        for s in range(n_dp):
            owner = m.owners[s]
            for r, ring in enumerate(rings):
                while ring.at < s:
                    ring.step()
                columns = pl.ds(pl.multiple_of(owner * block + r * count, 128), count)
                product = mm(b.normed[:, columns], hold[owner, r * count : (r + 1) * count])
                target[...] = product if s + r == 0 else target[...] + product

    for ring in cells:
        ring.last_leg()
    gate.start()
    down.start()
    project(b.up_cell, cells, b.wide_f)

    for h in range(heads):
        at = slice(h * chan, (h + 1) * chan)
        for j in range(4):
            b.chan_params[j : j + 1, at] = b.conv_weight[j].astype(F32)[h : h + 1]
        for j, ref in ((4, b.conv_bias), (5, b.group_gain), (6, b.skip_gain)):
            b.chan_params[j : j + 1, at] = ref[...].astype(F32)[h : h + 1]
        for s in range(3):
            for i in range(4):
                tap = b.qkv_weight[s, i].astype(F32)[h : h + 1]
                b.maps8[s, h, i : i + 1] = tap
                b.maps8[s, h, i + 4 : i + 5] = tap
            for g in range(2 * all_heads):
                row = b.gate_weight[g // all_heads, g % all_heads, s].astype(F32)[h : h + 1]
                b.gates_f[g : g + 1, s * local + h * chan : s * local + (h + 1) * chan] = row
    b.gates_f[8:] = jnp.zeros((8, 3 * local), F32)
    b.gates_w[...] = b.gates_f[...].astype(BF)
    place = lax.broadcasted_iota(jnp.int32, (rows, 1), 0)
    ends, total = [], 0
    for k in range(b.lengths.shape[1]):
        total = total + b.lengths[m.z, k]
        ends.append(total)
    begin = jnp.zeros((rows, 1), jnp.int32)
    for end in ends:
        begin = jnp.where(place >= end, end, begin)
    b.begin[...] = jnp.broadcast_to(begin, (rows, 128))

    def convolve(i, carry):
        at = pl.ds(pl.multiple_of(i * 128, 128), 128)
        low = b.wide_f[:, at].astype(BF)
        b.branch[:, at] = low
        x = low.astype(F32)
        since = lax.broadcasted_iota(jnp.int32, (rows, 128), 0) - b.begin[...]
        conv = b.chan_params[4:5, at] + b.chan_params[0:1, at] * x
        for j in range(1, 4):
            back = b.chan_params[j : j + 1, at] * pltpu.roll(x, j, 0)
            conv = conv + jnp.where(since >= j, back, 0.0)
        sig = sigmoid(conv)
        act = conv * sig
        b.act[:, at] = act
        b.slope[:, at] = sig + act * (1.0 - sig)
        return carry

    lax.fori_loop(0, local // 128, convolve, 0)
    r_map = lax.broadcasted_iota(jnp.int32, (chan, chan), 0) // 4
    c_map = lax.broadcasted_iota(jnp.int32, (chan, chan), 1) // 4
    same = r_map == c_map
    for s in range(3):
        for h in range(heads):
            base = b.maps8[s, h]
            dense = jnp.broadcast_to(base[None], (chan // 8, 8, chan)).reshape(chan, chan)
            b.maps[s, h] = jnp.where(same, dense, 0.0).astype(BF)
    for h in range(heads):
        at = slice(h * chan, (h + 1) * chan)
        act = b.act[:, at]
        high, rest = split(act)
        least = ((act - high.astype(F32)) - rest.astype(F32)).astype(BF)
        for s in range(2):
            b.qkv[:, s * local + h * chan : s * local + (h + 1) * chan] = (
                mm(high, b.maps[s, h]) + (mm(rest, b.maps[s, h]) + mm(least, b.maps[s, h]))
            ).astype(BF)
        b.qkv[:, 2 * local + h * chan : 2 * local + (h + 1) * chan] = mm(
            b.branch[:, at], b.maps[2, h]
        ).astype(BF)

    pre_part = mm_nt(b.gates_w[...], b.qkv[...])[:8]
    pre_sum = push_sum(links, m, pre_part, b.pre_box, m.plane_peers, m.slot, 8)

    def q_of(h, i):
        return b.qkv[i * LINE : (i + 1) * LINE, h * chan : (h + 1) * chan]

    def k_of(h, low, n):
        return b.qkv[
            low * LINE : (low + n) * LINE, local + h * chan : local + (h + 1) * chan
        ]

    def v_of(h, low, n):
        return b.qkv[
            low * LINE : (low + n) * LINE, 2 * local + h * chan : 2 * local + (h + 1) * chan
        ]

    b.of = (q_of, k_of, v_of)
    for h in range(heads):
        for i, low, at, n in blocks:
            tile = mm_nt(q_of(h, i), k_of(h, low, n))
            for k in range(n):
                b.score_part[h, at + k] = tile[:, k * LINE : (k + 1) * LINE]
    other = links.go(b.score_part.at[1 - m.core], b.score_in.at[0], m.sib)
    b.score_copy = other
    other.wait_recv()
    b.score_sum[...] = b.score_part[m.core] + b.score_in[0]
    far = links.go(b.score_sum, b.score_in.at[1], m.yn)

    line81 = lax.broadcasted_iota(jnp.int32, (8, 1), 0)
    given = b.gate_bias[...].astype(F32)
    bias = jnp.zeros((8, 1), F32)
    for g in range(2):
        for o in range(all_heads):
            bias = jnp.where(line81 == g * all_heads + o, given[g : g + 1, o : o + 1], bias)
    pre = pre_sum() + bias
    b.pre[...] = pre
    line8 = lax.broadcasted_iota(jnp.int32, (8, rows), 0)
    head = m.c * heads + m.core
    in_gate = jnp.sum(jnp.where(line8 == head, pre, 0.0), axis=0, keepdims=True)
    forget = jnp.sum(jnp.where(line8 == head + all_heads, pre, 0.0), axis=0, keepdims=True)
    log_forget = jnp.minimum(forget, 0.0) - jnp.log(1.0 + jnp.exp(-jnp.abs(forget)))
    rising = prefix_lanes(jnp.broadcast_to(log_forget, (8, rows)))
    rise_col = to_columns(rising)
    gate_line = in_gate - rising[:1]
    gate.step()
    for copy in valid_copies:
        copy.wait_recv()
    b.keep[...] = jnp.zeros((rows, 128), F32)

    def take_source(s, carry):
        perm = slots_of(s)
        valid = b.valids[s][:1]
        pack = lax.shift_right_logical(perm, digits)
        lasts = jnp.zeros((1, rows), jnp.int32)
        for p in range(n_dp):
            last = sum(b.lengths[p, k] for k in range(b.lengths.shape[1]))
            lasts = jnp.where(pack == p, last, lasts)
        counted = jnp.where(perm - pack * rows < lasts, valid, 0.0)
        hits = jnp.where(line == perm - m.z * rows, counted, 0.0)
        b.keep[...] += jnp.sum(hits, axis=1, keepdims=True)
        return carry + jnp.sum(counted, axis=1, keepdims=True)

    valid_count = lax.fori_loop(0, n_dp, take_source, jnp.zeros((1, 1), F32))
    keep = b.keep[:, :1]
    far.wait_recv()
    b.score_part[m.core] = b.score_sum[...] + b.score_in[1]
    for i, low, at, n in blocks:
        lines = slice(i * LINE, (i + 1) * LINE)
        t_at = i * LINE + lax.broadcasted_iota(jnp.int32, (LINE, n * LINE), 0)
        s_at = low * LINE + lax.broadcasted_iota(jnp.int32, (LINE, n * LINE), 1)
        allowed = (s_at <= t_at) & (s_at >= b.begin[lines][:, :1])
        logit = jnp.where(
            allowed, rise_col[lines][:, :1] + gate_line[:, low * LINE : (low + n) * LINE], NEG_FILL
        )
        top = jnp.max(logit, axis=1, keepdims=True)
        decay = jnp.where(allowed, jnp.exp(logit - top), 0.0) * scale
        weight = wide(b.score_part, m.core, at, n) * decay
        den = jnp.sum(weight, axis=1, keepdims=True)
        floor = jnp.exp(-top)
        inv = 1.0 / jnp.maximum(jnp.abs(den), floor)
        shares = (weight * inv).astype(BF)
        b.inv[lines] = jnp.broadcast_to(inv, (LINE, 128))
        sign = jnp.where(jnp.abs(den) > floor, jnp.where(den > 0.0, 1.0, -1.0), 0.0)
        b.sign[lines] = jnp.broadcast_to(sign, (LINE, 128))
        for k in range(n):
            b.decay[at + k] = decay[:, k * LINE : (k + 1) * LINE]
            b.weight[at + k] = weight[:, k * LINE : (k + 1) * LINE]
            b.share[m.core, at + k] = shares[:, k * LINE : (k + 1) * LINE]
    shared = links.go(b.share.at[m.core], b.share.at[m.core], m.sib)
    gate.step()
    shared.wait_recv()
    columns = []
    for h in range(heads):
        for i, low, at, n in blocks:
            lines = slice(i * LINE, (i + 1) * LINE)
            b.hidden[lines, h * chan : (h + 1) * chan] = mm(
                wide(b.share, h, at, n), v_of(h, low, n)
            )
        hid = b.hidden[:, h * chan : (h + 1) * chan]
        columns.append(jnp.sum(hid, axis=1, keepdims=True))
        columns.append(jnp.sum(hid * hid, axis=1, keepdims=True))
    moment_sum = push_sum(
        links, m, to_lanes(columns, rows), b.moment_box, m.tensor_peers, m.t, 4
    )
    gate.finish()
    down.step()
    project(b.up_gate, (gate,), b.wide_f)
    moments = to_columns(moment_sum()) / (4 * chan)
    for h in range(heads):
        mean = moments[:, 2 * h : 2 * h + 1]
        rstd = root_inverse(moments[:, 2 * h + 1 : 2 * h + 2] - mean * mean + EPSILON)
        b.head_rstd[h] = jnp.broadcast_to(rstd, (rows, 128))
        b.head_mean[h] = jnp.broadcast_to(mean, (rows, 128))
    down.step()

    def mix(i, carry):
        at = pl.ds(pl.multiple_of(i * 128, 128), 128)
        h = lax.div(i, chan // 128)
        hat = (b.hidden[:, at] - b.head_mean[h]) * b.head_rstd[h]
        b.hidden[:, at] = hat
        low = b.wide_f[:, at].astype(BF)
        b.gate_low[:, at] = low
        g = low.astype(F32)
        inner = hat * b.chan_params[5:6, at] + b.chan_params[6:7, at] * b.act[:, at]
        b.mixed_all[m.z, :, at] = (inner * (g * sigmoid(g))).astype(BF)
        return carry

    lax.fori_loop(0, local // 128, mix, 0)
    down.last_leg()
    goal_copies = exchange(b.sent_goal, b.goal_places)
    mixed_ring.start()
    down.finish()
    piece = min(block, wide_d)

    def down_part(y, core, x):
        slot = (y * 2 + core) * 2 + x
        parts = []
        for k in range(wide_d // piece):
            if block >= 2 * wide_d:
                owner = lax.div((y * 2 + core) * 2 * wide_d, block)
                at = pl.ds(pl.multiple_of(x * wide_d, 128), wide_d)
                parts.append(mm(b.mixed_all[m.z], b.down[owner, :, at]))
            else:
                owner = lax.div(slot * wide_d, block) + k
                parts.append(mm(b.mixed_all[m.z], b.down[owner]))
        return jnp.concatenate(parts, axis=1)

    own_k = m.y * 2 + m.c
    summed = plane_scatter(links, m, down_part, b, rows, (idle, mixed_ring.step, idle))
    loss_sum = jnp.zeros((1, 1), F32)
    b.arriving = []
    size = rows // GROUPS
    for copy in goal_copies:
        copy.wait_recv()
    b.goal[...] = mm(b.recv_map[...], b.goal_places[...]).astype(BF)
    for g, at in summed:
        result = (b.x_own[at].astype(F32) + b.acc[own_k, at]).astype(BF)
        b.result[at] = result
        difference = result.astype(F32) - b.goal[at].astype(F32)
        own_gradient = ((rows * n_dp) / valid_count * keep[at] * difference).astype(BF)
        b.full[m.slot, at] = own_gradient
        arriving = plane_gather(links, m, b.full, size, g * size)
        slot = next(arriving)
        b.arriving.append(itertools.chain([slot], arriving))
        b.own_gradient[at] = own_gradient
        per_row = jnp.sum(difference * difference, axis=1, keepdims=True)
        loss_sum = loss_sum + jnp.sum(keep[at] * 0.5 * per_row, axis=0, keepdims=True)
    b.loss_part[...] = jnp.broadcast_to(loss_sum / valid_count, (8, 128))
    b.mixed_ring = mixed_ring

    b.sent_out[...] = mm_tn(b.recv_map[...], b.result[...]).astype(BF)
    b.home_out[own_place] = b.sent_out[own_place]
    b.home_copies = exchange(b.sent_out, b.home_out)


def backward(b, m, links, shape):
    rows, local, chan, n_dp, block, wide_d = shape
    cap, heads = rows // n_dp, local // chan
    all_heads = 2 * heads
    width, head_width = 8 * wide_d, 4 * chan
    blocks, n_blocks = band(rows)
    q_of, k_of, v_of = b.of
    line8 = lax.broadcasted_iota(jnp.int32, (8, rows), 0)
    head = m.c * heads + m.core

    size = rows // GROUPS
    for turn, slots in enumerate(zip(*b.arriving)):
        for g, slot in enumerate(slots):
            lines = slice(g * size, (g + 1) * size)
            grads = b.full[slot, lines]
            if block >= wide_d:
                ratio = block // wide_d
                at = pl.ds(pl.multiple_of(lax.rem(slot, ratio) * wide_d, 128), wide_d)
                product = mm_nt(grads, b.down[lax.div(slot, ratio), :, at])
            else:
                ratio = wide_d // block
                product = sum(
                    mm_nt(grads[:, k * block : (k + 1) * block], b.down[slot * ratio + k])
                    for k in range(ratio)
                )
            b.wide_f[lines] = product if turn == 0 else b.wide_f[lines] + product
        if turn == 5:
            b.mixed_ring.step()
    for arriving in b.arriving:
        for _ in arriving:
            pass

    per = rows // 8
    own_rows = pl.ds(pl.multiple_of(m.slot * per, 16), per)
    for d in range(n_dp):
        to = m.z if d == 0 else m.dp_peers[d - 1][0]
        if block >= wide_d:
            ratio = block // wide_d
            for k in range(ratio):
                b.cols_out[to, :, k * wide_d : (k + 1) * wide_d] = b.full[to * ratio + k, own_rows]
        else:
            ratio = wide_d // block
            at = pl.ds(pl.multiple_of(lax.rem(to, ratio) * block, 128), block)
            b.cols_out[to] = b.full[lax.div(to, ratio), own_rows, at]
    from_here = pl.ds(pl.multiple_of(m.z * per, 16), per)
    b.cols[m.slot, from_here] = b.cols_out[m.z]
    cols_copies = [
        links.go(b.cols_out.at[peer[0]], b.cols.at[m.slot, from_here], peer)
        for peer in m.dp_peers
    ]

    def sum_down():
        for copy in cols_copies:
            copy.wait_recv()
        b.mixed_ring.finish()
        b.grad_down[...] = jnp.zeros((local, block), F32)
        for slot in plane_gather(links, m, b.cols, n_dp * per):
            at = pl.ds(pl.multiple_of(slot * per, 16), per)
            for p in range(0, n_dp, 4):
                left = jnp.concatenate([b.mixed_all[p + k, at] for k in range(4)], axis=0)
                b.grad_down[...] += mm_tn(left, b.cols[slot, p * per : (p + 4) * per])
            yield

    down_sum = sum_down()

    def advance(steps):
        for _ in range(steps):
            next(down_sum, None)

    def up_ring(grads, hold, g, h):
        at_h = slice(h * chan, (h + 1) * chan)
        size = block // 2 if g else block

        def part(owner, j=None):
            if j is None:
                at = pl.ds(pl.multiple_of(owner * block, 128), block)
            else:
                at = pl.ds(pl.multiple_of(owner * block + j * size, 128), size)
            return mm_tn(b.normed[:, at], grads[:, at_h])

        def keep(total, lines):
            b.grad_up[lines, g, h] = total

        return (LineSum if n_dp <= 4 else RingSum)(
            links, part, hold.at[h], keep, m, n_dp, size
        )

    gates = [up_ring(b.g_gate, b.ring_gate, 1, h) for h in range(heads)]
    cells = [up_ring(b.g_cell, b.ring_cell, 0, h) for h in range(heads)]

    def ticks(rings):
        for _ in range(n_dp):
            for ring in rings:
                yield ring.step()

    gate_ticks, cell_ticks = ticks(gates), ticks(cells)

    def tick(source):
        return lambda: next(source, None)

    def unmix(i, carry):
        at = pl.ds(pl.multiple_of(i * 128, 128), 128)
        gm = b.wide_f[:, at]
        g = b.gate_low[:, at].astype(F32)
        sig = sigmoid(g)
        silu = g * sig
        hat, act = b.hidden[:, at], b.act[:, at]
        group, skip = b.chan_params[5:6, at], b.chan_params[6:7, at]
        inner = hat * group + skip * act
        b.g_gate[:, at] = (gm * inner * (sig + silu * (1.0 - sig))).astype(BF)
        gi = gm * silu
        b.small[5:6, at] = jnp.sum(gi * hat, axis=0, keepdims=True)
        b.small[6:7, at] = jnp.sum(gi * act, axis=0, keepdims=True)
        b.g_act[:, at] = gi * skip
        b.wide_f[:, at] = gi * group
        return carry

    lax.fori_loop(0, local // 128, unmix, 0)
    b.mixed_ring.last_leg()
    next(gate_ticks)
    next(gate_ticks)
    columns = []
    for h in range(heads):
        u = b.wide_f[:, h * chan : (h + 1) * chan]
        columns.append(jnp.sum(u, axis=1, keepdims=True))
        columns.append(
            jnp.sum(u * b.hidden[:, h * chan : (h + 1) * chan], axis=1, keepdims=True)
        )
    u_sum = push_sum(links, m, to_lanes(columns, rows), b.u_box, m.tensor_peers, m.t, 4)
    u_moments = to_columns(u_sum())
    rhos = []
    for h in range(heads):
        at = slice(h * chan, (h + 1) * chan)
        rstd = b.head_rstd[h][:, :1]
        mean_u = u_moments[:, 2 * h : 2 * h + 1] / head_width
        sum_ux = u_moments[:, 2 * h + 1 : 2 * h + 2]
        d_hidden = rstd * (b.wide_f[:, at] - mean_u - b.hidden[:, at] * (sum_ux / head_width))
        b.d_hidden[:, at] = d_hidden.astype(BF)
        rhos.append(sum_ux * (EPSILON * rstd * rstd))
    rho = jnp.where(m.core == 0, rhos[0], rhos[1])
    links.settle([b.score_copy])
    for h in range(heads):
        for i, low, at, n in blocks:
            tile = mm_nt(
                b.d_hidden[i * LINE : (i + 1) * LINE, h * chan : (h + 1) * chan], v_of(h, low, n)
            )
            for k in range(n):
                b.score_part[h, at + k] = tile[:, k * LINE : (k + 1) * LINE]
    other = links.go(b.score_part.at[1 - m.core], b.score_in.at[0], m.sib)
    other.wait_recv()
    b.share_out[...] = (b.score_part[m.core] + b.score_in[0]).astype(BF)
    far = links.go(b.share_out, b.share_in, m.yn)
    far.wait_recv()
    b.lines[...] = jnp.zeros((8, rows), F32)
    for i, low, at, n in blocks:
        lines = slice(i * LINE, (i + 1) * LINE)
        across = slice(low * LINE, (low + n) * LINE)

        def spread(ref):
            return jnp.concatenate([ref[at + k].astype(F32) for k in range(n)], axis=1)

        inv, sign, radial = b.inv[lines][:, :1], b.sign[lines][:, :1], rho[lines]
        weight = spread(b.weight)
        full = (spread(b.share_out) + spread(b.share_in)) * inv - sign * radial * inv
        exact = jnp.where(sign == 0.0, radial, 0.0)
        noisy = jnp.sum(full * weight, axis=1, keepdims=True)
        square = jnp.sum(weight * weight, axis=1, keepdims=True)
        full = full - weight * ((noisy - exact) / jnp.where(square > 0.0, square, 1.0))
        d_score = (full * spread(b.decay)).astype(BF)
        for k in range(n):
            b.d_score[m.core, at + k] = d_score[:, k * LINE : (k + 1) * LINE]
        b.lines[0:1, across] += jnp.sum(full * weight, axis=0, keepdims=True)
        b.keep[lines] = jnp.broadcast_to(exact, (LINE, 128))
    next(gate_ticks)
    scored = links.go(b.d_score.at[m.core], b.d_score.at[m.core], m.sib)
    over_cols = b.lines[0:1]
    over_rows = b.keep[...].T[0:1]
    delta = jnp.broadcast_to(over_rows - over_cols, (8, rows))
    after = jnp.sum(delta, axis=1, keepdims=True) - prefix_lanes(delta) + delta
    forget = jnp.sum(jnp.where(line8 == head + all_heads, b.pre[...], 0.0), axis=0, keepdims=True)
    d_forget = after[:1] / (1.0 + jnp.exp(forget))
    own_lines = jnp.where(line8 == head, over_cols, 0.0) + jnp.where(
        line8 == head + all_heads, d_forget, 0.0
    )
    head_peers = [
        m.sib,
        m.xn,
        (m.z, m.sib_t, m.other_c),
    ]
    pre_sum = push_sum(links, m, own_lines, b.grad_box, head_peers, m.c * 2 + m.core, 4)

    for h in range(heads):
        at = slice(2 * local + h * chan, 2 * local + (h + 1) * chan)
        b.g_proj[:, at] = jnp.zeros((rows, chan), F32)
        for i, low, place, n in blocks:
            d_hid = b.d_hidden[i * LINE : (i + 1) * LINE, h * chan : (h + 1) * chan]
            b.g_proj[low * LINE : (low + n) * LINE, at] += mm_tn(wide(b.share, h, place, n), d_hid)
    next(gate_ticks)
    scored.wait_recv()
    for h in range(heads):
        at = slice(h * chan, (h + 1) * chan)
        k_at = slice(local + h * chan, local + (h + 1) * chan)
        b.g_proj[:, k_at] = jnp.zeros((rows, chan), F32)
        for i, low, place, n in blocks:
            tile = wide(b.d_score, h, place, n)
            b.g_proj[i * LINE : (i + 1) * LINE, at] = mm(tile, k_of(h, low, n))
            b.g_proj[low * LINE : (low + n) * LINE, k_at] += mm_tn(tile, q_of(h, i))
    pre_grad = pre_sum()
    next(gate_ticks)
    advance(1)
    pre16 = jnp.concatenate([pre_grad, jnp.zeros((8, rows), F32)], axis=0)
    high, rest = split(pre16)
    b.g_proj[...] += mm_tn(high, b.gates_w[...]) + mm_tn(rest, b.gates_w[...])
    gate_grad = (mm(high, b.qkv[...]) + mm(rest, b.qkv[...]))[:8]
    for s in range(3):
        b.low_sum[8 * s : 8 * (s + 1)] = gate_grad[:, s * local : (s + 1) * local]
    bias_grad = jnp.sum(pre_grad, axis=1, keepdims=True)
    b.small[7:8, wide_d : wide_d + 128] = to_lanes_one(bias_grad)
    advance(2)

    r_map = lax.broadcasted_iota(jnp.int32, (chan, chan), 0) // 4
    c_map = lax.broadcasted_iota(jnp.int32, (chan, chan), 1) // 4
    same = r_map == c_map
    for h in range(heads):
        at = slice(h * chan, (h + 1) * chan)
        act_low = b.act[:, at].astype(BF)
        extra = None
        for s in range(3):
            low = b.g_proj[:, s * local + h * chan : s * local + (h + 1) * chan].astype(BF)
            left = act_low if s < 2 else b.branch[:, at]
            dense = jnp.where(same, mm_tn(left, low), 0.0)
            folded = jnp.sum(dense.reshape(chan // 8, 8, chan), axis=0)
            b.low_sum[24 + 4 * s : 28 + 4 * s, at] = folded[:4] + folded[4:]
            back = mm_nt(low, b.maps[s, h])
            if s == 0:
                extra = back
            elif s == 1:
                b.g_act[:, at] += extra + back
            else:
                b.wide_f[:, at] = back

    def unconvolve(i, carry):
        at = pl.ds(pl.multiple_of(i * 128, 128), 128)
        since = lax.broadcasted_iota(jnp.int32, (rows, 128), 0) - b.begin[...]
        x = b.branch[:, at].astype(F32)
        gc = b.g_act[:, at] * b.slope[:, at]
        gb = b.wide_f[:, at] + b.chan_params[0:1, at] * gc
        b.small[0:1, at] = jnp.sum(gc * x, axis=0, keepdims=True)
        b.small[4:5, at] = jnp.sum(gc, axis=0, keepdims=True)
        for j in range(1, 4):
            kept = jnp.where(since >= j, gc, 0.0)
            gb = gb + b.chan_params[j : j + 1, at] * pltpu.roll(kept, rows - j, 0)
            b.small[j : j + 1, at] = jnp.sum(kept * pltpu.roll(x, j, 0), axis=0, keepdims=True)
        b.g_cell[:, at] = gb.astype(BF)
        return carry

    lax.fori_loop(0, local // 128, unconvolve, 0)
    next(gate_ticks)
    next(cell_ticks)
    next(cell_ticks)
    b.low_sum[36:] = jnp.zeros((12, local), F32)
    b.low_box[m.z] = b.low_sum[...].astype(BF)
    low_copies = [links.go(b.low_box.at[m.z], b.low_box.at[m.z], peer) for peer in m.dp_peers]
    advance(4)

    def up_part(y, core, x):
        slot = (y * 2 + core) * 2 + x
        if block >= wide_d:
            ratio = block // wide_d
            at = pl.ds(pl.multiple_of(lax.rem(slot, ratio) * wide_d, 16), wide_d)
            owner = lax.div(slot, ratio)
            return mm_nt(b.g_cell[...], b.up_cell[owner, at]) + mm_nt(
                b.g_gate[...], b.up_gate[owner, at]
            )
        ratio = wide_d // block
        return jnp.concatenate(
            [
                mm_nt(b.g_cell[...], b.up_cell[slot * ratio + k])
                + mm_nt(b.g_gate[...], b.up_gate[slot * ratio + k])
                for k in range(ratio)
            ],
            axis=1,
        )

    own_k = m.y * 2 + m.c
    services = (lambda: advance(2), tick(gate_ticks), tick(gate_ticks))
    for _ in plane_scatter(links, m, up_part, b, rows, services):
        pass
    for _ in gate_ticks:
        pass
    grad_normed = b.acc[own_k]
    x_hat = (b.x_own[...].astype(F32) - b.sums[:, :1]) * b.squares[:, :1]
    grad_scaled = grad_normed * b.gains[m.slot, :1]
    line_sum = push_sum(
        links,
        m,
        to_lanes(
            [
                jnp.sum(grad_scaled, axis=1, keepdims=True),
                jnp.sum(grad_scaled * x_hat, axis=1, keepdims=True),
            ],
            rows,
        ),
        b.line_box,
        m.plane_peers,
        m.slot,
        8,
    )
    loss_sum = push_sum(links, m, b.loss_part[...], b.loss_box, m.plane_peers, m.slot, 8)
    b.small[7:8, :wide_d] = jnp.sum(grad_normed * x_hat, axis=0, keepdims=True)
    b.small[7:8, wide_d + 128 :] = loss_sum()[:1]
    b.small_box[m.z] = b.small[...]
    small_copies = [
        links.go(b.small_box.at[m.z], b.small_box.at[m.z], peer) for peer in m.dp_peers
    ]
    next(cell_ticks)
    lines = to_columns(line_sum()) / width
    grad_x = b.squares[:, :1] * (grad_scaled - lines[:, :1] - x_hat * lines[:, 1:2])
    own_grad = b.own_gradient[...].astype(F32)
    grad_slot = (own_grad + grad_x).astype(BF)
    links.settle(b.token_copies)
    b.sent_tokens[...] = mm_tn(b.recv_map[...], grad_slot).astype(BF)
    own_place = pl.ds(pl.multiple_of(m.z * cap, 16), cap)
    b.home_grad[own_place] = b.sent_tokens[own_place]
    copies = b.exchange(b.sent_tokens, b.home_grad)
    next(cell_ticks)
    for copy in b.home_copies:
        copy.wait_recv()
    b.output[...] = mm_tn(b.send_map[...], b.home_out[...]).astype(BF)
    next(cell_ticks)
    advance(3)
    for copy in small_copies + low_copies:
        copy.wait_recv()
    lows = b.low_box[0].astype(F32)
    for k in range(1, n_dp):
        lows = lows + b.low_box[k].astype(F32)
    b.low_sum[...] = lows
    total = b.small_box[0]
    for k in range(1, n_dp):
        total = total + b.small_box[k]
    b.small[...] = total
    b.loss[...] = total[7:8, wide_d + 128 : wide_d + 129]
    b.grad_ln[...] = total[7:8, :wide_d]
    for h in range(heads):
        at = slice(h * chan, (h + 1) * chan)
        for j in range(4):
            b.grad_conv_weight[j, h : h + 1] = b.small[j : j + 1, at]
        for j, ref in ((4, b.grad_conv_bias), (5, b.grad_group), (6, b.grad_skip)):
            ref[h : h + 1] = b.small[j : j + 1, at]
        for s in range(3):
            for i in range(4):
                k = 24 + 4 * s + i
                b.grad_qkv[s, i, h : h + 1] = b.low_sum[k : k + 1, at]
            for g in range(2 * all_heads):
                k = 8 * s + g
                b.grad_gate_weight[g // all_heads, g % all_heads, s, h : h + 1] = b.low_sum[
                    k : k + 1, at
                ]
    for g in range(2):
        at = wide_d + g * all_heads
        b.grad_gate_bias[g : g + 1] = total[7:8, at : at + all_heads]
    for _ in cell_ticks:
        pass
    for copy in copies:
        copy.wait_recv()
    b.grad_input[...] = mm_tn(b.send_map[...], b.home_grad[...]).astype(BF)
    for line in [b.mixed_ring] + gates + cells:
        line.settle()


def kernel(names, shape, limit, *refs):
    b = types.SimpleNamespace(**dict(zip(names, refs)))
    m = coordinates(shape[3])
    links = Links(b.send_sem, b.recv_sem, limit)
    forward(b, m, links, shape)
    backward(b, m, links, shape)
    links.close()


def carry_out(*refs):
    *ends, sems = refs
    half = len(ends) // 2
    copies = [
        pltpu.make_async_copy(ends[k], ends[half + k], sems.at[k]) for k in range(half)
    ]
    for copy in copies:
        copy.start()
    for copy in copies:
        copy.wait()


def shards(
    tokens,
    targets,
    ln_gain,
    up_weight,
    conv_weight,
    conv_bias,
    qkv_weight,
    gate_weight,
    gate_bias,
    group_gain,
    skip_gain,
    down_weight,
    lengths,
    permutation,
    valid,
):
    rows, wide_d = tokens.shape
    n_dp = lax.axis_size("dp")
    heads, chan = up_weight.shape[2], up_weight.shape[3]
    local = heads * chan
    block = up_weight.shape[0]
    width = 8 * wide_d
    up_halves = up_weight.transpose(1, 0, 2, 3).reshape(2, block, local)
    inputs = dict(
        tokens=tokens,
        targets=targets,
        permutation=permutation,
        valid=valid,
        own_cell=up_halves[0],
        own_gate=up_halves[1],
        own_down=down_weight.reshape(local, block),
        ln_gain=ln_gain,
        conv_weight=conv_weight,
        conv_bias=conv_bias,
        qkv_weight=qkv_weight,
        gate_weight=gate_weight,
        gate_bias=gate_bias,
        group_gain=group_gain,
        skip_gain=skip_gain,
        lengths=lengths,
    )
    outputs = dict(
        output=((rows, wide_d), BF),
        loss=((1, 1), F32),
        grad_input=((rows, wide_d), BF),
        grad_ln=((1, wide_d), F32),
        grad_up=(up_weight.shape, F32),
        grad_conv_weight=(conv_weight.shape, F32),
        grad_conv_bias=(conv_bias.shape, F32),
        grad_qkv=(qkv_weight.shape, F32),
        grad_gate_weight=(gate_weight.shape, F32),
        grad_gate_bias=(gate_bias.shape, F32),
        grad_group=(group_gain.shape, F32),
        grad_skip=(skip_gain.shape, F32),
        grad_down=((local, block), F32),
    )
    n_blocks = band(rows)[1]
    half = rows // 2
    limit = 150 + 14 * n_dp
    turns = (2 if n_dp <= 4 else 1, n_dp)
    scratch = dict(
        send_map=((rows, rows), BF),
        recv_map=((rows, rows), BF),
        chan_params=((8, local), F32),
        maps8=((3, heads, 8, chan), F32),
        gates_f=((16, 3 * local), F32),
        gates_w=((16, 3 * local), BF),
        sent_tokens=((rows, wide_d), BF),
        sent_goal=((rows, wide_d), BF),
        goal_places=((rows, wide_d), BF),
        valids=((n_dp, 8, rows), F32),
        keep=((rows, 128), F32),
        full=((8, rows, wide_d), BF),
        gains=((8, 8, wide_d), F32),
        up_cell=((n_dp, block, local), BF),
        up_gate=((n_dp, block, local), BF),
        down=((n_dp, local, block), BF),
        sums=((rows, 128), F32),
        squares=((rows, 128), F32),
        x_own=((rows, wide_d), BF),
        normed=((rows, width), BF),
        wide_f=((rows, local), F32),
        begin=((rows, 128), jnp.int32),
        branch=((rows, local), BF),
        act=((rows, local), F32),
        slope=((rows, local), F32),
        maps=((3, heads, chan, chan), BF),
        qkv=((rows, 3 * local), BF),
        pre_box=((8, 8, rows), F32),
        pre=((8, rows), F32),
        score_part=((heads, n_blocks, LINE, LINE), F32),
        score_in=((2, n_blocks, LINE, LINE), F32),
        score_sum=((n_blocks, LINE, LINE), F32),
        decay=((n_blocks, LINE, LINE), F32),
        weight=((n_blocks, LINE, LINE), F32),
        share=((heads, n_blocks, LINE, LINE), BF),
        inv=((rows, 128), F32),
        sign=((rows, 128), F32),
        hidden=((rows, local), F32),
        moment_box=((4, 8, rows), F32),
        head_rstd=((heads, rows, 128), F32),
        head_mean=((heads, rows, 128), F32),
        gate_low=((rows, local), BF),
        out=((4, rows, wide_d), BF),
        into=((4, rows, wide_d), BF),
        acc=((4, rows, wide_d), F32),
        small_out=((6 * GROUPS, half // GROUPS, wide_d), BF),
        small_in=((6 * GROUPS, half // GROUPS, wide_d), BF),
        loss_part=((8, 128), F32),
        goal=((rows, wide_d), BF),
        result=((rows, wide_d), BF),
        own_gradient=((rows, wide_d), BF),
        sent_out=((rows, wide_d), BF),
        home_out=((rows, wide_d), BF),
        home_grad=((rows, wide_d), BF),
        mixed_all=((n_dp, rows, local), BF),
        cols_out=((n_dp, rows // 8, block), BF),
        cols=((8, n_dp * rows // 8, block), BF),
        low_sum=((48, local), F32),
        low_box=((n_dp, 48, local), BF),
        ring_gate=((heads,) + turns + (block, chan), BF),
        ring_cell=((heads,) + turns + (block, chan), BF),
        g_gate=((rows, local), BF),
        g_cell=((rows, local), BF),
        small=((8, local), F32),
        small_box=((n_dp, 8, local), F32),
        g_act=((rows, local), F32),
        u_box=((4, 8, rows), F32),
        d_hidden=((rows, local), BF),
        share_out=((n_blocks, LINE, LINE), BF),
        share_in=((n_blocks, LINE, LINE), BF),
        lines=((8, rows), F32),
        d_score=((heads, n_blocks, LINE, LINE), BF),
        grad_box=((4, 8, rows), F32),
        g_proj=((rows, 3 * local), F32),
        line_box=((8, 8, rows), F32),
        loss_box=((8, 8, 128), F32),
    )
    vmem = pl.BlockSpec(memory_space=pltpu.VMEM)
    spaces = {name: pl.BlockSpec(memory_space=pl.ANY) for name in inputs if name[:4] == "own_"}
    spaces["lengths"] = pl.BlockSpec(memory_space=pltpu.SMEM)
    names = list(inputs) + list(outputs) + list(scratch) + ["send_sem", "recv_sem", "local_sem"]
    results = pl.pallas_call(
        lambda *refs: kernel(names, (rows, local, chan, n_dp, block, wide_d), limit, *refs),
        out_shape=[jax.ShapeDtypeStruct(*spec) for spec in outputs.values()],
        in_specs=[spaces.get(name, vmem) for name in inputs],
        out_specs=[vmem] * len(outputs),
        scratch_shapes=[pltpu.VMEM(*spec) for spec in scratch.values()]
        + [pltpu.SemaphoreType.DMA((limit,)), pltpu.SemaphoreType.DMA((limit,))]
        + [pltpu.SemaphoreType.DMA((3,))],
        compiler_params=pltpu.CompilerParams(
            collective_id=0, has_side_effects=True, vmem_limit_bytes=VMEM_LIMIT
        ),
    )(*inputs.values())
    results = pl.pallas_call(
        carry_out,
        out_shape=[jax.ShapeDtypeStruct(*spec) for spec in outputs.values()],
        in_specs=[pl.BlockSpec(memory_space=pl.ANY)] * len(outputs),
        out_specs=[vmem] * len(outputs),
        scratch_shapes=[pltpu.SemaphoreType.DMA((len(outputs),))],
    )(*results)
    o = types.SimpleNamespace(**dict(zip(outputs, results)))
    return (
        o.output,
        o.loss.reshape(()),
        o.grad_input,
        o.grad_ln.reshape(-1),
        o.grad_up,
        o.grad_conv_weight,
        o.grad_conv_bias,
        o.grad_qkv,
        o.grad_gate_weight,
        o.grad_gate_bias,
        o.grad_group,
        o.grad_skip,
        o.grad_down.reshape(down_weight.shape),
    )


def solution(mesh):
    return jax.shard_map(
        shards,
        mesh=mesh,
        in_specs=(
            P("dp", ("tensor", "ctx")),
            P("dp", ("tensor", "ctx")),
            P(("tensor", "ctx")),
            P("dp", None, "ctx", "tensor"),
            P(None, "ctx", "tensor"),
            P("ctx", "tensor"),
            P(None, None, "ctx", "tensor"),
            P(None, None, None, "ctx", "tensor"),
            P(),
            P("ctx", "tensor"),
            P("ctx", "tensor"),
            P("ctx", "tensor", "dp"),
            P(),
            P(),
            P("dp"),
        ),
        out_specs=(
            P("dp", ("tensor", "ctx")),
            P(),
            P("dp", ("tensor", "ctx")),
            P(("tensor", "ctx")),
            P("dp", None, "ctx", "tensor"),
            P(None, "ctx", "tensor"),
            P("ctx", "tensor"),
            P(None, None, "ctx", "tensor"),
            P(None, None, None, "ctx", "tensor"),
            P(),
            P("ctx", "tensor"),
            P("ctx", "tensor"),
            P("ctx", "tensor", "dp"),
        ),
        check_vma=False,
    )
```

```python
import itertools
import types

import jax
import jax.numpy as jnp
from jax import lax
from jax.experimental import pallas as pl
from jax.experimental.pallas import tpu as pltpu
from jax.sharding import PartitionSpec as P

NEG_FILL = -1e30
EPSILON = 1e-05
BF = jnp.bfloat16
F32 = jnp.float32
MESH = pl.DeviceIdType.MESH
VMEM_LIMIT = 62 * 1024 * 1024
LINE = 128
GROUPS = 2
BAND = 2


def mm(a, b):
    return jnp.dot(a, b, preferred_element_type=F32)


def mm_nt(a, b):
    return lax.dot_general(a, b, (((1,), (1,)), ((), ())), preferred_element_type=F32)


def mm_tn(a, b):
    return lax.dot_general(a, b, (((0,), (0,)), ((), ())), preferred_element_type=F32)


def split(v):
    high = v.astype(BF)
    return high, (v - high.astype(F32)).astype(BF)


def root_inverse(v):
    guess = lax.rsqrt(v)
    return guess * (1.5 - 0.5 * v * guess * guess)


def sigmoid(v):
    return 1.0 / (1.0 + jnp.exp(-v))


class Links:
    def __init__(self, send, recv, limit):
        self.send, self.recv, self.limit = send, recv, limit
        self.used, self.open = 0, []

    def make(self, src, dst, peer):
        k = self.used
        self.used += 1
        assert k < self.limit
        copy = pltpu.make_async_remote_copy(
            src_ref=src,
            dst_ref=dst,
            send_sem=self.send.at[k],
            recv_sem=self.recv.at[k],
            device_id=peer,
            device_id_type=MESH,
        )
        return copy

    def go(self, src, dst, peer):
        copy = self.make(src, dst, peer)
        copy.start()
        self.open.append(copy)
        return copy

    def settle(self, copies):
        for copy in copies:
            copy.wait_send()
        self.open = [c for c in self.open if all(c is not done for done in copies)]

    def close(self):
        self.settle(list(self.open))


class Ring:
    def __init__(self, links, hold, part, next_peer, owners):
        self.links, self.hold, self.part = links, hold, part
        self.peer, self.owners = next_peer, owners
        self.flying, self.at = None, 0

    def start(self):
        block = self.hold.at[self.owners[self.at], self.part]
        self.flying = self.links.go(block, block, self.peer)

    def step(self):
        if self.at >= len(self.owners) - 1:
            return False
        if self.flying is None:
            self.start()
        self.flying.wait_recv()
        self.at += 1
        self.flying = None
        if self.at < len(self.owners) - 1:
            self.start()
            return True
        return False

    def last_leg(self):
        while self.at < len(self.owners) - 2:
            self.step()

    def finish(self):
        while self.step():
            pass

    def settle(self):
        self.links.close()


def when(condition, *actions):
    @pl.when(condition)
    def _():
        for action in actions:
            action()


class LineGather:
    def __init__(self, links, hold, m, count):
        self.z, self.count, self.at = m.z, count, 0
        z, last = m.z, count - 1
        self.ways = []
        for d in range(1, count):
            to_right = jnp.maximum(z - (d - 1), 0)
            to_left = jnp.minimum(z + (d - 1), last)
            self.ways.append(
                (
                    (
                        links.make(hold.at[to_right], hold.at[to_right], m.right),
                        (z < last) & (z >= d - 1),
                        z >= d,
                    ),
                    (
                        links.make(hold.at[to_left], hold.at[to_left], m.left),
                        (z > 0) & (z + d - 1 <= last),
                        z + d <= last,
                    ),
                )
            )

    def start(self):
        for copy, sends, _ in self.ways[self.at]:
            when(sends, copy.start)

    def step(self):
        if self.at >= self.count - 1:
            return
        for copy, _, receives in self.ways[self.at]:
            when(receives, copy.wait_recv)
        self.at += 1
        if self.at < self.count - 1:
            self.start()

    def last_leg(self):
        while self.at < self.count - 2:
            self.step()

    def finish(self):
        while self.at < self.count - 1:
            self.step()

    def settle(self):
        for pair in self.ways:
            for copy, sends, _ in pair:
                when(sends, copy.wait_send)


class LineSum:
    def __init__(self, links, part, hold, target, m, count, size):
        self.part, self.hold, self.target = part, hold, target
        self.z, self.count, self.at, self.size = m.z, count, 0, size
        places = (m.z, count - 1 - m.z)
        self.ways = [
            (
                places[way],
                [
                    links.make(hold.at[way, t], hold.at[way, t + 1], peer)
                    for t in range(count - 1)
                ],
            )
            for way, peer in enumerate((m.right, m.left))
        ]

    def step(self):
        t, count = self.at, self.count
        if t > count - 1:
            return
        self.at += 1
        size = self.size
        pieces = self.hold.shape[-2] // size

        def arrive(place, copies):
            if t:
                when((place > 0) & (place <= t), copies[t - 1].wait_recv)

        def lines(j):
            return pl.ds(pl.multiple_of(j * size, size), size)

        def add(way, place, own, j):
            if t:
                own = own + jnp.where(place > 0, self.hold[way, t, lines(j)].astype(F32), 0.0)
            return own

        if t == count - 1:
            for place, copies in self.ways:
                arrive(place, copies)

            def last(j, carry):
                total = self.part(self.z, j)
                for way, (place, _) in enumerate(self.ways):
                    total = add(way, place, total, j)
                self.target(total, lines(j))
                return carry

            lax.fori_loop(0, pieces, last, 0)
            return
        for way, (place, copies) in enumerate(self.ways):
            arrive(place, copies)

            def send(way=way, place=place, copies=copies):
                ahead = count - 1 - t
                owner = self.z + ahead if way == 0 else self.z - ahead

                def piece(j, carry):
                    self.hold[way, t, lines(j)] = add(
                        way, place, self.part(owner, j), j
                    ).astype(BF)
                    return carry

                lax.fori_loop(0, pieces, piece, 0)
                copies[t].start()

            when(place <= t, send)

    def settle(self):
        for place, copies in self.ways:
            for t, copy in enumerate(copies):
                when(place <= t, copy.wait_send)


class RingSum:
    def __init__(self, links, part, hold, target, m, count, size):
        self.links, self.part, self.hold, self.target = links, part, hold, target
        self.m, self.count, self.at = m, count, -1
        self.sent = []

    def step(self):
        if self.at >= self.count - 1:
            return
        self.at += 1
        own = self.part(self.m.owners[(self.at + 1) % self.count])
        if self.at:
            self.sent[-1].wait_recv()
            own = own + self.hold[0, self.at].astype(F32)
        if self.at == self.count - 1:
            self.target(own, pl.ds(0, own.shape[0]))
            return
        self.hold[0, self.at] = own.astype(BF)
        self.sent.append(
            self.links.go(
                self.hold.at[0, self.at], self.hold.at[0, self.at + 1], self.m.ring_next
            )
        )

    def settle(self):
        self.links.settle(self.sent)


def coordinates(dp_count):
    z, t, c = lax.axis_index("dp"), lax.axis_index("tensor"), lax.axis_index("ctx")
    core = lax.rem(t, 2)
    m = types.SimpleNamespace(z=z, t=t, c=c, core=core, y=lax.div(t, 2))
    m.sib_t, m.far_t, m.other_c = t + 1 - 2 * core, lax.rem(t + 2, 4), 1 - c
    m.sib, m.yn, m.xn = (z, m.sib_t, c), (z, m.far_t, c), (z, t, m.other_c)
    m.slot = t * 2 + c
    m.slot_x, m.slot_y, m.slot_d = t * 2 + m.other_c, m.far_t * 2 + c, m.far_t * 2 + m.other_c
    m.to_sib = 2 - 4 * core
    if dp_count == 4:
        def after(v):
            return lax.rem(2 * v + 1, 5)

        def before(v):
            return lax.rem(3 * v + 2, 5)
    else:
        def after(v):
            return lax.rem(v + 1, dp_count)

        def before(v):
            return lax.rem(v + dp_count - 1, dp_count)

    m.ring_next = (after(z), t, c)
    m.owners = [z]
    for _ in range(dp_count - 1):
        m.owners.append(before(m.owners[-1]))
    m.right = (lax.rem(z + 1, dp_count), t, c)
    m.left = (lax.rem(z + dp_count - 1, dp_count), t, c)
    m.dp_peers = [(lax.rem(z + d, dp_count), t, c) for d in range(1, dp_count)]
    m.plane_peers = [
        (z, lax.rem(t + dt, 4), lax.rem(c + dc, 2))
        for dt in range(4)
        for dc in range(2)
        if dt or dc
    ]
    m.tensor_peers = [(z, lax.rem(t + dt, 4), c) for dt in range(1, 4)]
    return m


def plane_gather(links, m, full, rows, base=0):
    half = rows // 2
    first, second, whole = pl.ds(base, half), pl.ds(base + half, half), pl.ds(base, rows)
    sent = []

    def send(slot, part, peer):
        sent.append(links.go(full.at[slot, part], full.at[slot, part], peer))
        return sent[-1]

    x_first = send(m.slot, first, m.xn)
    y_second = send(m.slot, second, m.yn)
    to_sib = send(m.slot, whole, m.sib)
    x_second = send(m.slot, second, m.xn)
    y_first = send(m.slot, first, m.yn)
    yield m.slot
    to_sib.wait_recv()
    yield m.slot + m.to_sib
    x_first.wait_recv()
    d_first = send(m.slot_x, first, m.yn)
    y_second.wait_recv()
    d_second = send(m.slot_y, second, m.xn)
    x_second.wait_recv()
    sib_x = send(m.slot_x, whole, m.sib)
    yield m.slot_x
    y_first.wait_recv()
    sib_y = send(m.slot_y, whole, m.sib)
    yield m.slot_y
    sib_x.wait_recv()
    yield m.slot_x + m.to_sib
    d_first.wait_recv()
    d_second.wait_recv()
    sib_d = send(m.slot_d, whole, m.sib)
    yield m.slot_d
    sib_y.wait_recv()
    yield m.slot_y + m.to_sib
    sib_d.wait_recv()
    yield m.slot_d + m.to_sib
    links.settle(sent)


def idle():
    pass


def to_lanes(columns, rows):
    lane = lax.broadcasted_iota(jnp.int32, (rows, 128), 1)
    out = jnp.zeros((rows, 128), F32)
    for j, column in enumerate(columns):
        out = jnp.where(lane == j, column, out)
    return out.T[:8]


def to_lanes_one(column):
    line = lax.broadcasted_iota(jnp.int32, (8, 128), 0)
    lane = lax.broadcasted_iota(jnp.int32, (8, 128), 1)
    return jnp.sum(jnp.where(line == lane, column, 0.0), axis=0, keepdims=True)


def to_columns(lines):
    rows = lines.shape[1]
    return jnp.concatenate([lines, jnp.zeros((120, rows), F32)], axis=0).T


def push_sum(links, m, lines, box, peers, own_place, count):
    box[own_place] = lines
    copies = [links.go(box.at[own_place], box.at[own_place], peer) for peer in peers]

    def finish():
        for copy in copies:
            copy.wait_recv()
        total = box[0]
        for k in range(1, count):
            total = total + box[k]
        return total

    return finish


def prefix_lanes(v):
    width = v.shape[1]
    lane = lax.broadcasted_iota(jnp.int32, v.shape, 1)
    step = 1
    while step < width:
        v = v + jnp.where(lane >= step, pltpu.roll(v, step, 1), 0.0)
        step *= 2
    return v


def band(rows):
    out, at = [], 0
    for i in range(rows // LINE):
        low = max(0, i - BAND)
        out.append((i, low, at, i - low + 1))
        at += i - low + 1
    return out, at


def wide(ref, h, at, width):
    return jnp.concatenate([ref[h, at + k] for k in range(width)], axis=1)


def plane_scatter(links, m, part, b, rows, services):
    size = rows // GROUPS
    half = size // 2
    own_k = m.y * 2 + m.c
    far_y = 1 - m.y
    links.settle(b.scatter_copies)
    copies = []
    for k in range(4):
        b.out[k] = part(k // 2, 1 - m.core, k % 2).astype(BF)
        for g in range(GROUPS):
            at = pl.ds(g * size, size)
            copies.append(links.go(b.out.at[k, at], b.into.at[k, at], m.sib))

    def own_part(k, carry):
        b.acc[k] = part(lax.div(k, 2), m.core, lax.rem(k, 2))
        return carry

    lax.fori_loop(0, 4, own_part, 0)
    b.scatter_copies = list(copies)
    services[0]()

    def send(g, place, k, at, peer):
        place += 6 * g
        b.small_out[place] = b.acc[k, at].astype(BF)
        copy = links.go(b.small_out.at[place], b.small_in.at[place], peer)
        b.scatter_copies.append(copy)
        return copy

    def receive(g, place, k, at, copy):
        copy.wait_recv()
        b.acc[k, at] += b.small_in[place + 6 * g].astype(F32)

    parts = [(pl.ds(g * size, half), pl.ds(g * size + half, half)) for g in range(GROUPS)]
    second_phase, third_phase = [], []
    for g, (first, second) in enumerate(parts):
        at = pl.ds(g * size, size)
        for k in range(4):
            copies[k * GROUPS + g].wait_recv()
            b.acc[k, at] += b.into[k, at].astype(F32)
        second_phase.append(
            [send(g, y, y * 2 + m.other_c, first, m.xn) for y in range(2)]
            + [send(g, 2 + x, far_y * 2 + x, second, m.yn) for x in range(2)]
        )
    services[1]()
    for g, (first, second) in enumerate(parts):
        flying = second_phase[g]
        for y in range(2):
            receive(g, y, y * 2 + m.c, first, flying[y])
        for x in range(2):
            receive(g, 2 + x, m.y * 2 + x, second, flying[2 + x])
        third_phase.append(
            (
                send(g, 4, far_y * 2 + m.c, first, m.yn),
                send(g, 5, m.y * 2 + m.other_c, second, m.xn),
            )
        )
    services[2]()
    for g, (first, second) in enumerate(parts):
        receive(g, 4, own_k, first, third_phase[g][0])
        receive(g, 5, own_k, second, third_phase[g][1])
        yield g, slice(g * size, (g + 1) * size)


def forward(b, m, links, shape):
    rows, local, chan, n_dp, block, wide_d = shape
    cap, heads = rows // n_dp, local // chan
    width, all_heads = 8 * wide_d, 2 * heads
    scale = (4 * chan) ** -0.5
    blocks, n_blocks = band(rows)
    low_rows = pl.ds(0, rows)

    b.scatter_copies = []
    partners = m.plane_peers + m.dp_peers
    barrier = pltpu.get_barrier_semaphore()
    for peer in partners:
        pl.semaphore_signal(barrier, inc=1, device_id=peer, device_id_type=MESH)
    own_copies = [
        pltpu.make_async_copy(own, hold.at[m.z], b.local_sem.at[k])
        for k, (own, hold) in enumerate(
            ((b.own_cell, b.up_cell), (b.own_gate, b.up_gate), (b.own_down, b.down))
        )
    ]
    for copy in own_copies:
        copy.start()
    own_place = pl.ds(pl.multiple_of(m.z * cap, 16), cap)

    def slots_of(source):
        return b.permutation[pl.ds(pl.multiple_of(source * rows, rows), rows)].reshape(1, rows)

    b.gains[m.slot] = jnp.broadcast_to(b.ln_gain[...].astype(F32).reshape(1, wide_d), (8, wide_d))
    b.valids[m.z] = jnp.broadcast_to(b.valid[...].astype(F32).reshape(1, rows), (8, rows))
    count = block // 2 if block % 256 == 0 else block
    cells = [
        Ring(links, b.up_cell, pl.ds(at, count), m.ring_next, m.owners)
        for at in range(0, block, count)
    ]
    gate = Ring(links, b.up_gate, pl.ds(0, block), m.ring_next, m.owners)
    down = Ring(links, b.down, pl.ds(0, local), m.ring_next, m.owners)
    if n_dp <= 4:
        mixed_ring = LineGather(links, b.mixed_all, m, n_dp)
    else:
        mixed_ring = Ring(links, b.mixed_all, pl.ds(0, rows), m.ring_next, m.owners)
    own_copies[0].wait()
    pl.semaphore_wait(barrier, len(partners))
    cells[0].start()

    digits = rows.bit_length() - 1
    packs = max(8, n_dp)
    own = slots_of(m.z)
    dest = lax.shift_right_logical(own, digits)
    to_pack = lax.broadcasted_iota(jnp.int32, (packs, rows), 0) == dest
    ahead = prefix_lanes(jnp.where(to_pack, 1.0, 0.0))
    rank = jnp.sum(jnp.where(to_pack, ahead, 0.0), axis=0, keepdims=True).astype(jnp.int32) - 1
    line = lax.broadcasted_iota(jnp.int32, (rows, rows), 0)
    b.send_map[...] = jnp.where(line == dest * cap + rank, 1.0, 0.0).astype(BF)
    b.sent_tokens[...] = mm(b.send_map[...], b.tokens[...]).astype(BF)
    b.full[m.slot, own_place] = b.sent_tokens[own_place]

    def exchange(out, into):
        copies = []
        for d, peer in enumerate(m.dp_peers):
            place = pl.ds(pl.multiple_of(lax.rem(m.z + d + 1, n_dp) * cap, 16), cap)
            copies.append(links.go(out.at[place], into.at[own_place], peer))
        return copies

    b.exchange = exchange
    a2a = exchange(b.sent_tokens, b.full.at[m.slot])
    b.token_copies = a2a
    for ring in cells[1:]:
        ring.start()
    one = pl.ds(0, 1)
    gain_copies = [
        links.go(b.gains.at[m.slot], b.gains.at[m.slot], peer) for peer in m.plane_peers
    ]
    valid_copies = [
        links.go(b.valids.at[m.z, one], b.valids.at[m.z, one], peer) for peer in m.dp_peers
    ]
    for copy in own_copies[1:]:
        copy.wait()

    b.wide_f[...] = jnp.zeros((rows, rows), F32)

    def place_source(s, carry):
        perm = slots_of(s)
        mine = lax.shift_right_logical(perm, digits) == m.z
        ahead = prefix_lanes(jnp.broadcast_to(jnp.where(mine, 1.0, 0.0), (8, rows)))[:1]
        at = jnp.where(mine, s * cap + ahead.astype(jnp.int32) - 1, -1)
        slot = perm - m.z * rows
        slots = jnp.where(line == slot, 1.0, 0.0).astype(BF)
        places = jnp.where(line == at, 1.0, 0.0).astype(BF)
        b.wide_f[...] += mm_nt(slots, places)
        return carry

    lax.fori_loop(0, n_dp, place_source, 0)
    b.recv_map[...] = b.wide_f[...].astype(BF)
    for copy in a2a:
        copy.wait_recv()
    cells[0].step()

    b.sums[...] = jnp.zeros((rows, 128), F32)
    b.squares[...] = jnp.zeros((rows, 128), F32)
    arrivals = 0
    for slot in plane_gather(links, m, b.full, rows):
        columns = pl.ds(pl.multiple_of(slot * wide_d, 128), wide_d)

        def place_rows(r, carry, slot=slot, columns=columns):
            at = pl.ds(pl.multiple_of(r * LINE, LINE), LINE)
            x = mm(b.recv_map[at], b.full[slot])
            b.normed[at, columns] = x.astype(BF)
            b.sums[at] += jnp.sum(x, axis=1, keepdims=True)
            b.squares[at] += jnp.sum(x * x, axis=1, keepdims=True)
            return carry

        lax.fori_loop(0, rows // LINE, place_rows, 0)
        arrivals += 1
        if arrivals in (3, 8):
            cells[-1].step()
        if arrivals == 6:
            cells[0].step()
    own_columns = pl.ds(pl.multiple_of(m.slot * wide_d, 128), wide_d)
    b.x_own[...] = b.normed[:, own_columns]
    b.sent_goal[...] = mm(b.send_map[...], b.targets[...]).astype(BF)
    b.goal_places[own_place] = b.sent_goal[own_place]
    for copy in gain_copies:
        copy.wait_recv()

    def normalise(r, carry):
        at = pl.ds(pl.multiple_of(r * 64, 64), 64)
        mean = b.sums[at][:, :1] / width
        var = b.squares[at][:, :1] / width - mean * mean
        rstd = root_inverse(var + EPSILON)
        b.sums[at] = jnp.broadcast_to(mean, (64, 128))
        b.squares[at] = jnp.broadcast_to(rstd, (64, 128))
        for i in range(8):
            x = b.normed[at, i * wide_d : (i + 1) * wide_d].astype(F32)
            x = (x - mean) * rstd * b.gains[i, :1]
            b.normed[at, i * wide_d : (i + 1) * wide_d] = x.astype(BF)
        return carry

    lax.fori_loop(0, rows // 64, normalise, 0)

    def project(hold, rings, target):
        count = block // len(rings)
        for s in range(n_dp):
            owner = m.owners[s]
            for r, ring in enumerate(rings):
                while ring.at < s:
                    ring.step()
                columns = pl.ds(pl.multiple_of(owner * block + r * count, 128), count)
                product = mm(b.normed[:, columns], hold[owner, r * count : (r + 1) * count])
                target[...] = product if s + r == 0 else target[...] + product

    for ring in cells:
        ring.last_leg()
    gate.start()
    down.start()
    project(b.up_cell, cells, b.wide_f)

    for h in range(heads):
        at = slice(h * chan, (h + 1) * chan)
        for j in range(4):
            b.chan_params[j : j + 1, at] = b.conv_weight[j].astype(F32)[h : h + 1]
        for j, ref in ((4, b.conv_bias), (5, b.group_gain), (6, b.skip_gain)):
            b.chan_params[j : j + 1, at] = ref[...].astype(F32)[h : h + 1]
        for s in range(3):
            for i in range(4):
                tap = b.qkv_weight[s, i].astype(F32)[h : h + 1]
                b.maps8[s, h, i : i + 1] = tap
                b.maps8[s, h, i + 4 : i + 5] = tap
            for g in range(2 * all_heads):
                row = b.gate_weight[g // all_heads, g % all_heads, s].astype(F32)[h : h + 1]
                b.gates_f[g : g + 1, s * local + h * chan : s * local + (h + 1) * chan] = row
    b.gates_f[8:] = jnp.zeros((8, 3 * local), F32)
    b.gates_w[...] = b.gates_f[...].astype(BF)
    place = lax.broadcasted_iota(jnp.int32, (rows, 1), 0)
    ends, total = [], 0
    for k in range(b.lengths.shape[1]):
        total = total + b.lengths[m.z, k]
        ends.append(total)
    begin = jnp.zeros((rows, 1), jnp.int32)
    for end in ends:
        begin = jnp.where(place >= end, end, begin)
    b.begin[...] = jnp.broadcast_to(begin, (rows, 128))

    def convolve(i, carry):
        at = pl.ds(pl.multiple_of(i * 128, 128), 128)
        low = b.wide_f[:, at].astype(BF)
        b.branch[:, at] = low
        x = low.astype(F32)
        since = lax.broadcasted_iota(jnp.int32, (rows, 128), 0) - b.begin[...]
        conv = b.chan_params[4:5, at] + b.chan_params[0:1, at] * x
        for j in range(1, 4):
            back = b.chan_params[j : j + 1, at] * pltpu.roll(x, j, 0)
            conv = conv + jnp.where(since >= j, back, 0.0)
        sig = sigmoid(conv)
        act = conv * sig
        b.act[:, at] = act
        b.slope[:, at] = sig + act * (1.0 - sig)
        return carry

    lax.fori_loop(0, local // 128, convolve, 0)
    r_map = lax.broadcasted_iota(jnp.int32, (chan, chan), 0) // 4
    c_map = lax.broadcasted_iota(jnp.int32, (chan, chan), 1) // 4
    same = r_map == c_map
    for s in range(3):
        for h in range(heads):
            base = b.maps8[s, h]
            dense = jnp.broadcast_to(base[None], (chan // 8, 8, chan)).reshape(chan, chan)
            b.maps[s, h] = jnp.where(same, dense, 0.0).astype(BF)
    for h in range(heads):
        at = slice(h * chan, (h + 1) * chan)
        act = b.act[:, at]
        high, rest = split(act)
        least = ((act - high.astype(F32)) - rest.astype(F32)).astype(BF)
        for s in range(2):
            b.qkv[:, s * local + h * chan : s * local + (h + 1) * chan] = (
                mm(high, b.maps[s, h]) + (mm(rest, b.maps[s, h]) + mm(least, b.maps[s, h]))
            ).astype(BF)
        b.qkv[:, 2 * local + h * chan : 2 * local + (h + 1) * chan] = mm(
            b.branch[:, at], b.maps[2, h]
        ).astype(BF)

    pre_part = mm_nt(b.gates_w[...], b.qkv[...])[:8]
    pre_sum = push_sum(links, m, pre_part, b.pre_box, m.plane_peers, m.slot, 8)

    def q_of(h, i):
        return b.qkv[i * LINE : (i + 1) * LINE, h * chan : (h + 1) * chan]

    def k_of(h, low, n):
        return b.qkv[
            low * LINE : (low + n) * LINE, local + h * chan : local + (h + 1) * chan
        ]

    def v_of(h, low, n):
        return b.qkv[
            low * LINE : (low + n) * LINE, 2 * local + h * chan : 2 * local + (h + 1) * chan
        ]

    b.of = (q_of, k_of, v_of)
    for h in range(heads):
        for i, low, at, n in blocks:
            tile = mm_nt(q_of(h, i), k_of(h, low, n))
            for k in range(n):
                b.score_part[h, at + k] = tile[:, k * LINE : (k + 1) * LINE]
    other = links.go(b.score_part.at[1 - m.core], b.score_in.at[0], m.sib)
    b.score_copy = other
    other.wait_recv()
    b.score_sum[...] = b.score_part[m.core] + b.score_in[0]
    far = links.go(b.score_sum, b.score_in.at[1], m.yn)

    line81 = lax.broadcasted_iota(jnp.int32, (8, 1), 0)
    given = b.gate_bias[...].astype(F32)
    bias = jnp.zeros((8, 1), F32)
    for g in range(2):
        for o in range(all_heads):
            bias = jnp.where(line81 == g * all_heads + o, given[g : g + 1, o : o + 1], bias)
    pre = pre_sum() + bias
    b.pre[...] = pre
    line8 = lax.broadcasted_iota(jnp.int32, (8, rows), 0)
    head = m.c * heads + m.core
    in_gate = jnp.sum(jnp.where(line8 == head, pre, 0.0), axis=0, keepdims=True)
    forget = jnp.sum(jnp.where(line8 == head + all_heads, pre, 0.0), axis=0, keepdims=True)
    log_forget = jnp.minimum(forget, 0.0) - jnp.log(1.0 + jnp.exp(-jnp.abs(forget)))
    rising = prefix_lanes(jnp.broadcast_to(log_forget, (8, rows)))
    rise_col = to_columns(rising)
    gate_line = in_gate - rising[:1]
    gate.step()
    for copy in valid_copies:
        copy.wait_recv()
    b.keep[...] = jnp.zeros((rows, 128), F32)

    def take_source(s, carry):
        perm = slots_of(s)
        valid = b.valids[s][:1]
        pack = lax.shift_right_logical(perm, digits)
        lasts = jnp.zeros((1, rows), jnp.int32)
        for p in range(n_dp):
            last = sum(b.lengths[p, k] for k in range(b.lengths.shape[1]))
            lasts = jnp.where(pack == p, last, lasts)
        counted = jnp.where(perm - pack * rows < lasts, valid, 0.0)
        hits = jnp.where(line == perm - m.z * rows, counted, 0.0)
        b.keep[...] += jnp.sum(hits, axis=1, keepdims=True)
        return carry + jnp.sum(counted, axis=1, keepdims=True)

    valid_count = lax.fori_loop(0, n_dp, take_source, jnp.zeros((1, 1), F32))
    keep = b.keep[:, :1]
    far.wait_recv()
    b.score_part[m.core] = b.score_sum[...] + b.score_in[1]
    for i, low, at, n in blocks:
        lines = slice(i * LINE, (i + 1) * LINE)
        t_at = i * LINE + lax.broadcasted_iota(jnp.int32, (LINE, n * LINE), 0)
        s_at = low * LINE + lax.broadcasted_iota(jnp.int32, (LINE, n * LINE), 1)
        allowed = (s_at <= t_at) & (s_at >= b.begin[lines][:, :1])
        logit = jnp.where(
            allowed, rise_col[lines][:, :1] + gate_line[:, low * LINE : (low + n) * LINE], NEG_FILL
        )
        top = jnp.max(logit, axis=1, keepdims=True)
        decay = jnp.where(allowed, jnp.exp(logit - top), 0.0) * scale
        weight = wide(b.score_part, m.core, at, n) * decay
        den = jnp.sum(weight, axis=1, keepdims=True)
        floor = jnp.exp(-top)
        inv = 1.0 / jnp.maximum(jnp.abs(den), floor)
        shares = (weight * inv).astype(BF)
        b.inv[lines] = jnp.broadcast_to(inv, (LINE, 128))
        sign = jnp.where(jnp.abs(den) > floor, jnp.where(den > 0.0, 1.0, -1.0), 0.0)
        b.sign[lines] = jnp.broadcast_to(sign, (LINE, 128))
        for k in range(n):
            b.decay[at + k] = decay[:, k * LINE : (k + 1) * LINE]
            b.weight[at + k] = weight[:, k * LINE : (k + 1) * LINE]
            b.share[m.core, at + k] = shares[:, k * LINE : (k + 1) * LINE]
    shared = links.go(b.share.at[m.core], b.share.at[m.core], m.sib)
    gate.step()
    shared.wait_recv()
    columns = []
    for h in range(heads):
        for i, low, at, n in blocks:
            lines = slice(i * LINE, (i + 1) * LINE)
            b.hidden[lines, h * chan : (h + 1) * chan] = mm(
                wide(b.share, h, at, n), v_of(h, low, n)
            )
        hid = b.hidden[:, h * chan : (h + 1) * chan]
        columns.append(jnp.sum(hid, axis=1, keepdims=True))
        columns.append(jnp.sum(hid * hid, axis=1, keepdims=True))
    moment_sum = push_sum(
        links, m, to_lanes(columns, rows), b.moment_box, m.tensor_peers, m.t, 4
    )
    gate.finish()
    down.step()
    project(b.up_gate, (gate,), b.wide_f)
    moments = to_columns(moment_sum()) / (4 * chan)
    for h in range(heads):
        mean = moments[:, 2 * h : 2 * h + 1]
        rstd = root_inverse(moments[:, 2 * h + 1 : 2 * h + 2] - mean * mean + EPSILON)
        b.head_rstd[h] = jnp.broadcast_to(rstd, (rows, 128))
        b.head_mean[h] = jnp.broadcast_to(mean, (rows, 128))
    down.step()

    def mix(i, carry):
        at = pl.ds(pl.multiple_of(i * 128, 128), 128)
        h = lax.div(i, chan // 128)
        hat = (b.hidden[:, at] - b.head_mean[h]) * b.head_rstd[h]
        b.hidden[:, at] = hat
        low = b.wide_f[:, at].astype(BF)
        b.gate_low[:, at] = low
        g = low.astype(F32)
        inner = hat * b.chan_params[5:6, at] + b.chan_params[6:7, at] * b.act[:, at]
        b.mixed_all[m.z, :, at] = (inner * (g * sigmoid(g))).astype(BF)
        return carry

    lax.fori_loop(0, local // 128, mix, 0)
    down.last_leg()
    goal_copies = exchange(b.sent_goal, b.goal_places)
    mixed_ring.start()
    down.finish()
    piece = min(block, wide_d)

    def down_part(y, core, x):
        slot = (y * 2 + core) * 2 + x
        parts = []
        for k in range(wide_d // piece):
            if block >= 2 * wide_d:
                owner = lax.div((y * 2 + core) * 2 * wide_d, block)
                at = pl.ds(pl.multiple_of(x * wide_d, 128), wide_d)
                parts.append(mm(b.mixed_all[m.z], b.down[owner, :, at]))
            else:
                owner = lax.div(slot * wide_d, block) + k
                parts.append(mm(b.mixed_all[m.z], b.down[owner]))
        return jnp.concatenate(parts, axis=1)

    own_k = m.y * 2 + m.c
    summed = plane_scatter(links, m, down_part, b, rows, (idle, mixed_ring.step, idle))
    loss_sum = jnp.zeros((1, 1), F32)
    b.arriving = []
    size = rows // GROUPS
    for copy in goal_copies:
        copy.wait_recv()
    b.goal[...] = mm(b.recv_map[...], b.goal_places[...]).astype(BF)
    for g, at in summed:
        result = (b.x_own[at].astype(F32) + b.acc[own_k, at]).astype(BF)
        b.result[at] = result
        difference = result.astype(F32) - b.goal[at].astype(F32)
        own_gradient = ((rows * n_dp) / valid_count * keep[at] * difference).astype(BF)
        b.full[m.slot, at] = own_gradient
        arriving = plane_gather(links, m, b.full, size, g * size)
        slot = next(arriving)
        b.arriving.append(itertools.chain([slot], arriving))
        b.own_gradient[at] = own_gradient
        per_row = jnp.sum(difference * difference, axis=1, keepdims=True)
        loss_sum = loss_sum + jnp.sum(keep[at] * 0.5 * per_row, axis=0, keepdims=True)
    b.loss_part[...] = jnp.broadcast_to(loss_sum / valid_count, (8, 128))
    b.mixed_ring = mixed_ring

    b.sent_out[...] = mm_tn(b.recv_map[...], b.result[...]).astype(BF)
    b.home_out[own_place] = b.sent_out[own_place]
    b.home_copies = exchange(b.sent_out, b.home_out)


def backward(b, m, links, shape):
    rows, local, chan, n_dp, block, wide_d = shape
    cap, heads = rows // n_dp, local // chan
    all_heads = 2 * heads
    width, head_width = 8 * wide_d, 4 * chan
    blocks, n_blocks = band(rows)
    q_of, k_of, v_of = b.of
    line8 = lax.broadcasted_iota(jnp.int32, (8, rows), 0)
    head = m.c * heads + m.core

    size = rows // GROUPS
    for turn, slots in enumerate(zip(*b.arriving)):
        for g, slot in enumerate(slots):
            lines = slice(g * size, (g + 1) * size)
            grads = b.full[slot, lines]
            if block >= wide_d:
                ratio = block // wide_d
                at = pl.ds(pl.multiple_of(lax.rem(slot, ratio) * wide_d, 128), wide_d)
                product = mm_nt(grads, b.down[lax.div(slot, ratio), :, at])
            else:
                ratio = wide_d // block
                product = sum(
                    mm_nt(grads[:, k * block : (k + 1) * block], b.down[slot * ratio + k])
                    for k in range(ratio)
                )
            b.wide_f[lines] = product if turn == 0 else b.wide_f[lines] + product
        if turn == 5:
            b.mixed_ring.step()
    for arriving in b.arriving:
        for _ in arriving:
            pass

    per = rows // 8
    own_rows = pl.ds(pl.multiple_of(m.slot * per, 16), per)
    for d in range(n_dp):
        to = m.z if d == 0 else m.dp_peers[d - 1][0]
        if block >= wide_d:
            ratio = block // wide_d
            for k in range(ratio):
                b.cols_out[to, :, k * wide_d : (k + 1) * wide_d] = b.full[to * ratio + k, own_rows]
        else:
            ratio = wide_d // block
            at = pl.ds(pl.multiple_of(lax.rem(to, ratio) * block, 128), block)
            b.cols_out[to] = b.full[lax.div(to, ratio), own_rows, at]
    from_here = pl.ds(pl.multiple_of(m.z * per, 16), per)
    b.cols[m.slot, from_here] = b.cols_out[m.z]
    cols_copies = [
        links.go(b.cols_out.at[peer[0]], b.cols.at[m.slot, from_here], peer)
        for peer in m.dp_peers
    ]

    def sum_down():
        for copy in cols_copies:
            copy.wait_recv()
        b.mixed_ring.finish()
        b.grad_down[...] = jnp.zeros((local, block), F32)
        for slot in plane_gather(links, m, b.cols, n_dp * per):
            at = pl.ds(pl.multiple_of(slot * per, 16), per)
            for p in range(0, n_dp, 4):
                left = jnp.concatenate([b.mixed_all[p + k, at] for k in range(4)], axis=0)
                b.grad_down[...] += mm_tn(left, b.cols[slot, p * per : (p + 4) * per])
            yield

    down_sum = sum_down()

    def advance(steps):
        for _ in range(steps):
            next(down_sum, None)

    def up_ring(grads, hold, g, h):
        at_h = slice(h * chan, (h + 1) * chan)
        size = block // 2 if g and h else block

        def part(owner, j=None):
            if j is None:
                at = pl.ds(pl.multiple_of(owner * block, 128), block)
            else:
                at = pl.ds(pl.multiple_of(owner * block + j * size, 128), size)
            return mm_tn(b.normed[:, at], grads[:, at_h])

        def keep(total, lines):
            b.grad_up[lines, g, h] = total

        return (LineSum if n_dp <= 4 else RingSum)(
            links, part, hold.at[h], keep, m, n_dp, size
        )

    gates = [up_ring(b.g_gate, b.ring_gate, 1, h) for h in range(heads)]
    cells = [up_ring(b.g_cell, b.ring_cell, 0, h) for h in range(heads)]

    def ticks(rings):
        for _ in range(n_dp):
            for ring in rings:
                yield ring.step()

    gate_ticks, cell_ticks = ticks(gates), ticks(cells)

    def tick(source):
        return lambda: next(source, None)

    def unmix(i, carry):
        at = pl.ds(pl.multiple_of(i * 128, 128), 128)
        gm = b.wide_f[:, at]
        g = b.gate_low[:, at].astype(F32)
        sig = sigmoid(g)
        silu = g * sig
        hat, act = b.hidden[:, at], b.act[:, at]
        group, skip = b.chan_params[5:6, at], b.chan_params[6:7, at]
        inner = hat * group + skip * act
        b.g_gate[:, at] = (gm * inner * (sig + silu * (1.0 - sig))).astype(BF)
        gi = gm * silu
        b.small[5:6, at] = jnp.sum(gi * hat, axis=0, keepdims=True)
        b.small[6:7, at] = jnp.sum(gi * act, axis=0, keepdims=True)
        b.g_act[:, at] = gi * skip
        b.wide_f[:, at] = gi * group
        return carry

    lax.fori_loop(0, local // 128, unmix, 0)
    b.mixed_ring.last_leg()
    next(gate_ticks)
    next(gate_ticks)
    columns = []
    for h in range(heads):
        u = b.wide_f[:, h * chan : (h + 1) * chan]
        columns.append(jnp.sum(u, axis=1, keepdims=True))
        columns.append(
            jnp.sum(u * b.hidden[:, h * chan : (h + 1) * chan], axis=1, keepdims=True)
        )
    u_sum = push_sum(links, m, to_lanes(columns, rows), b.u_box, m.tensor_peers, m.t, 4)
    u_moments = to_columns(u_sum())
    rhos = []
    for h in range(heads):
        at = slice(h * chan, (h + 1) * chan)
        rstd = b.head_rstd[h][:, :1]
        mean_u = u_moments[:, 2 * h : 2 * h + 1] / head_width
        sum_ux = u_moments[:, 2 * h + 1 : 2 * h + 2]
        d_hidden = rstd * (b.wide_f[:, at] - mean_u - b.hidden[:, at] * (sum_ux / head_width))
        b.d_hidden[:, at] = d_hidden.astype(BF)
        rhos.append(sum_ux * (EPSILON * rstd * rstd))
    rho = jnp.where(m.core == 0, rhos[0], rhos[1])
    links.settle([b.score_copy])
    for h in range(heads):
        for i, low, at, n in blocks:
            tile = mm_nt(
                b.d_hidden[i * LINE : (i + 1) * LINE, h * chan : (h + 1) * chan], v_of(h, low, n)
            )
            for k in range(n):
                b.score_part[h, at + k] = tile[:, k * LINE : (k + 1) * LINE]
    other = links.go(b.score_part.at[1 - m.core], b.score_in.at[0], m.sib)
    other.wait_recv()
    b.share_out[...] = (b.score_part[m.core] + b.score_in[0]).astype(BF)
    far = links.go(b.share_out, b.share_in, m.yn)
    far.wait_recv()
    b.lines[...] = jnp.zeros((8, rows), F32)
    for i, low, at, n in blocks:
        lines = slice(i * LINE, (i + 1) * LINE)
        across = slice(low * LINE, (low + n) * LINE)

        def spread(ref):
            return jnp.concatenate([ref[at + k].astype(F32) for k in range(n)], axis=1)

        inv, sign, radial = b.inv[lines][:, :1], b.sign[lines][:, :1], rho[lines]
        weight = spread(b.weight)
        full = (spread(b.share_out) + spread(b.share_in)) * inv - sign * radial * inv
        exact = jnp.where(sign == 0.0, radial, 0.0)
        noisy = jnp.sum(full * weight, axis=1, keepdims=True)
        square = jnp.sum(weight * weight, axis=1, keepdims=True)
        full = full - weight * ((noisy - exact) / jnp.where(square > 0.0, square, 1.0))
        d_score = (full * spread(b.decay)).astype(BF)
        for k in range(n):
            b.d_score[m.core, at + k] = d_score[:, k * LINE : (k + 1) * LINE]
        b.lines[0:1, across] += jnp.sum(full * weight, axis=0, keepdims=True)
        b.keep[lines] = jnp.broadcast_to(exact, (LINE, 128))
    next(gate_ticks)
    scored = links.go(b.d_score.at[m.core], b.d_score.at[m.core], m.sib)
    over_cols = b.lines[0:1]
    over_rows = b.keep[...].T[0:1]
    delta = jnp.broadcast_to(over_rows - over_cols, (8, rows))
    after = jnp.sum(delta, axis=1, keepdims=True) - prefix_lanes(delta) + delta
    forget = jnp.sum(jnp.where(line8 == head + all_heads, b.pre[...], 0.0), axis=0, keepdims=True)
    d_forget = after[:1] / (1.0 + jnp.exp(forget))
    own_lines = jnp.where(line8 == head, over_cols, 0.0) + jnp.where(
        line8 == head + all_heads, d_forget, 0.0
    )
    head_peers = [
        m.sib,
        m.xn,
        (m.z, m.sib_t, m.other_c),
    ]
    pre_sum = push_sum(links, m, own_lines, b.grad_box, head_peers, m.c * 2 + m.core, 4)

    for h in range(heads):
        at = slice(2 * local + h * chan, 2 * local + (h + 1) * chan)
        b.g_proj[:, at] = jnp.zeros((rows, chan), F32)
        for i, low, place, n in blocks:
            d_hid = b.d_hidden[i * LINE : (i + 1) * LINE, h * chan : (h + 1) * chan]
            b.g_proj[low * LINE : (low + n) * LINE, at] += mm_tn(wide(b.share, h, place, n), d_hid)
    next(gate_ticks)
    scored.wait_recv()
    for h in range(heads):
        at = slice(h * chan, (h + 1) * chan)
        k_at = slice(local + h * chan, local + (h + 1) * chan)
        b.g_proj[:, k_at] = jnp.zeros((rows, chan), F32)
        for i, low, place, n in blocks:
            tile = wide(b.d_score, h, place, n)
            b.g_proj[i * LINE : (i + 1) * LINE, at] = mm(tile, k_of(h, low, n))
            b.g_proj[low * LINE : (low + n) * LINE, k_at] += mm_tn(tile, q_of(h, i))
    pre_grad = pre_sum()
    next(gate_ticks)
    advance(1)
    pre16 = jnp.concatenate([pre_grad, jnp.zeros((8, rows), F32)], axis=0)
    high, rest = split(pre16)
    b.g_proj[...] += mm_tn(high, b.gates_w[...]) + mm_tn(rest, b.gates_w[...])
    gate_grad = (mm(high, b.qkv[...]) + mm(rest, b.qkv[...]))[:8]
    for s in range(3):
        b.low_sum[8 * s : 8 * (s + 1)] = gate_grad[:, s * local : (s + 1) * local]
    bias_grad = jnp.sum(pre_grad, axis=1, keepdims=True)
    b.small[7:8, wide_d : wide_d + 128] = to_lanes_one(bias_grad)
    advance(2)

    r_map = lax.broadcasted_iota(jnp.int32, (chan, chan), 0) // 4
    c_map = lax.broadcasted_iota(jnp.int32, (chan, chan), 1) // 4
    same = r_map == c_map
    for h in range(heads):
        at = slice(h * chan, (h + 1) * chan)
        act_low = b.act[:, at].astype(BF)
        extra = None
        for s in range(3):
            low = b.g_proj[:, s * local + h * chan : s * local + (h + 1) * chan].astype(BF)
            left = act_low if s < 2 else b.branch[:, at]
            dense = jnp.where(same, mm_tn(left, low), 0.0)
            folded = jnp.sum(dense.reshape(chan // 8, 8, chan), axis=0)
            b.low_sum[24 + 4 * s : 28 + 4 * s, at] = folded[:4] + folded[4:]
            back = mm_nt(low, b.maps[s, h])
            if s == 0:
                extra = back
            elif s == 1:
                b.g_act[:, at] += extra + back
            else:
                b.wide_f[:, at] = back

    def unconvolve(i, carry):
        at = pl.ds(pl.multiple_of(i * 128, 128), 128)
        since = lax.broadcasted_iota(jnp.int32, (rows, 128), 0) - b.begin[...]
        x = b.branch[:, at].astype(F32)
        gc = b.g_act[:, at] * b.slope[:, at]
        gb = b.wide_f[:, at] + b.chan_params[0:1, at] * gc
        b.small[0:1, at] = jnp.sum(gc * x, axis=0, keepdims=True)
        b.small[4:5, at] = jnp.sum(gc, axis=0, keepdims=True)
        for j in range(1, 4):
            kept = jnp.where(since >= j, gc, 0.0)
            gb = gb + b.chan_params[j : j + 1, at] * pltpu.roll(kept, rows - j, 0)
            b.small[j : j + 1, at] = jnp.sum(kept * pltpu.roll(x, j, 0), axis=0, keepdims=True)
        b.g_cell[:, at] = gb.astype(BF)
        return carry

    lax.fori_loop(0, local // 128, unconvolve, 0)
    next(gate_ticks)
    next(cell_ticks)
    next(cell_ticks)
    b.low_sum[36:] = jnp.zeros((12, local), F32)
    b.low_box[m.z] = b.low_sum[...].astype(BF)
    low_copies = [links.go(b.low_box.at[m.z], b.low_box.at[m.z], peer) for peer in m.dp_peers]
    advance(4)

    def up_part(y, core, x):
        slot = (y * 2 + core) * 2 + x
        if block >= wide_d:
            ratio = block // wide_d
            at = pl.ds(pl.multiple_of(lax.rem(slot, ratio) * wide_d, 16), wide_d)
            owner = lax.div(slot, ratio)
            return mm_nt(b.g_cell[...], b.up_cell[owner, at]) + mm_nt(
                b.g_gate[...], b.up_gate[owner, at]
            )
        ratio = wide_d // block
        return jnp.concatenate(
            [
                mm_nt(b.g_cell[...], b.up_cell[slot * ratio + k])
                + mm_nt(b.g_gate[...], b.up_gate[slot * ratio + k])
                for k in range(ratio)
            ],
            axis=1,
        )

    own_k = m.y * 2 + m.c
    services = (lambda: advance(2), tick(gate_ticks), tick(gate_ticks))
    for _ in plane_scatter(links, m, up_part, b, rows, services):
        pass
    for _ in gate_ticks:
        pass
    grad_normed = b.acc[own_k]
    x_hat = (b.x_own[...].astype(F32) - b.sums[:, :1]) * b.squares[:, :1]
    grad_scaled = grad_normed * b.gains[m.slot, :1]
    line_sum = push_sum(
        links,
        m,
        to_lanes(
            [
                jnp.sum(grad_scaled, axis=1, keepdims=True),
                jnp.sum(grad_scaled * x_hat, axis=1, keepdims=True),
            ],
            rows,
        ),
        b.line_box,
        m.plane_peers,
        m.slot,
        8,
    )
    loss_sum = push_sum(links, m, b.loss_part[...], b.loss_box, m.plane_peers, m.slot, 8)
    b.small[7:8, :wide_d] = jnp.sum(grad_normed * x_hat, axis=0, keepdims=True)
    b.small[7:8, wide_d + 128 :] = loss_sum()[:1]
    b.small_box[m.z] = b.small[...]
    small_copies = [
        links.go(b.small_box.at[m.z], b.small_box.at[m.z], peer) for peer in m.dp_peers
    ]
    next(cell_ticks)
    lines = to_columns(line_sum()) / width
    grad_x = b.squares[:, :1] * (grad_scaled - lines[:, :1] - x_hat * lines[:, 1:2])
    own_grad = b.own_gradient[...].astype(F32)
    grad_slot = (own_grad + grad_x).astype(BF)
    links.settle(b.token_copies)
    b.sent_tokens[...] = mm_tn(b.recv_map[...], grad_slot).astype(BF)
    own_place = pl.ds(pl.multiple_of(m.z * cap, 16), cap)
    b.home_grad[own_place] = b.sent_tokens[own_place]
    copies = b.exchange(b.sent_tokens, b.home_grad)
    next(cell_ticks)
    for copy in b.home_copies:
        copy.wait_recv()
    b.output[...] = mm_tn(b.send_map[...], b.home_out[...]).astype(BF)
    next(cell_ticks)
    advance(3)
    for copy in small_copies + low_copies:
        copy.wait_recv()
    lows = b.low_box[0].astype(F32)
    for k in range(1, n_dp):
        lows = lows + b.low_box[k].astype(F32)
    b.low_sum[...] = lows
    total = b.small_box[0]
    for k in range(1, n_dp):
        total = total + b.small_box[k]
    b.small[...] = total
    b.loss[...] = total[7:8, wide_d + 128 : wide_d + 129]
    b.grad_ln[...] = total[7:8, :wide_d]
    for h in range(heads):
        at = slice(h * chan, (h + 1) * chan)
        for j in range(4):
            b.grad_conv_weight[j, h : h + 1] = b.small[j : j + 1, at]
        for j, ref in ((4, b.grad_conv_bias), (5, b.grad_group), (6, b.grad_skip)):
            ref[h : h + 1] = b.small[j : j + 1, at]
        for s in range(3):
            for i in range(4):
                k = 24 + 4 * s + i
                b.grad_qkv[s, i, h : h + 1] = b.low_sum[k : k + 1, at]
            for g in range(2 * all_heads):
                k = 8 * s + g
                b.grad_gate_weight[g // all_heads, g % all_heads, s, h : h + 1] = b.low_sum[
                    k : k + 1, at
                ]
    for g in range(2):
        at = wide_d + g * all_heads
        b.grad_gate_bias[g : g + 1] = total[7:8, at : at + all_heads]
    for _ in cell_ticks:
        pass
    for copy in copies:
        copy.wait_recv()
    b.grad_input[...] = mm_tn(b.send_map[...], b.home_grad[...]).astype(BF)
    for line in [b.mixed_ring] + gates + cells:
        line.settle()


def kernel(names, shape, limit, *refs):
    b = types.SimpleNamespace(**dict(zip(names, refs)))
    m = coordinates(shape[3])
    links = Links(b.send_sem, b.recv_sem, limit)
    forward(b, m, links, shape)
    backward(b, m, links, shape)
    links.close()


def carry_out(*refs):
    *ends, sems = refs
    half = len(ends) // 2
    copies = [
        pltpu.make_async_copy(ends[k], ends[half + k], sems.at[k]) for k in range(half)
    ]
    for copy in copies:
        copy.start()
    for copy in copies:
        copy.wait()


def shards(
    tokens,
    targets,
    ln_gain,
    up_weight,
    conv_weight,
    conv_bias,
    qkv_weight,
    gate_weight,
    gate_bias,
    group_gain,
    skip_gain,
    down_weight,
    lengths,
    permutation,
    valid,
):
    rows, wide_d = tokens.shape
    n_dp = lax.axis_size("dp")
    heads, chan = up_weight.shape[2], up_weight.shape[3]
    local = heads * chan
    block = up_weight.shape[0]
    width = 8 * wide_d
    up_halves = up_weight.transpose(1, 0, 2, 3).reshape(2, block, local)
    inputs = dict(
        tokens=tokens,
        targets=targets,
        permutation=permutation,
        valid=valid,
        own_cell=up_halves[0],
        own_gate=up_halves[1],
        own_down=down_weight.reshape(local, block),
        ln_gain=ln_gain,
        conv_weight=conv_weight,
        conv_bias=conv_bias,
        qkv_weight=qkv_weight,
        gate_weight=gate_weight,
        gate_bias=gate_bias,
        group_gain=group_gain,
        skip_gain=skip_gain,
        lengths=lengths,
    )
    outputs = dict(
        output=((rows, wide_d), BF),
        loss=((1, 1), F32),
        grad_input=((rows, wide_d), BF),
        grad_ln=((1, wide_d), F32),
        grad_up=(up_weight.shape, F32),
        grad_conv_weight=(conv_weight.shape, F32),
        grad_conv_bias=(conv_bias.shape, F32),
        grad_qkv=(qkv_weight.shape, F32),
        grad_gate_weight=(gate_weight.shape, F32),
        grad_gate_bias=(gate_bias.shape, F32),
        grad_group=(group_gain.shape, F32),
        grad_skip=(skip_gain.shape, F32),
        grad_down=((local, block), F32),
    )
    n_blocks = band(rows)[1]
    half = rows // 2
    limit = 150 + 14 * n_dp
    turns = (2 if n_dp <= 4 else 1, n_dp)
    scratch = dict(
        send_map=((rows, rows), BF),
        recv_map=((rows, rows), BF),
        chan_params=((8, local), F32),
        maps8=((3, heads, 8, chan), F32),
        gates_f=((16, 3 * local), F32),
        gates_w=((16, 3 * local), BF),
        sent_tokens=((rows, wide_d), BF),
        sent_goal=((rows, wide_d), BF),
        goal_places=((rows, wide_d), BF),
        valids=((n_dp, 8, rows), F32),
        keep=((rows, 128), F32),
        full=((8, rows, wide_d), BF),
        gains=((8, 8, wide_d), F32),
        up_cell=((n_dp, block, local), BF),
        up_gate=((n_dp, block, local), BF),
        down=((n_dp, local, block), BF),
        sums=((rows, 128), F32),
        squares=((rows, 128), F32),
        x_own=((rows, wide_d), BF),
        normed=((rows, width), BF),
        wide_f=((rows, local), F32),
        begin=((rows, 128), jnp.int32),
        branch=((rows, local), BF),
        act=((rows, local), F32),
        slope=((rows, local), F32),
        maps=((3, heads, chan, chan), BF),
        qkv=((rows, 3 * local), BF),
        pre_box=((8, 8, rows), F32),
        pre=((8, rows), F32),
        score_part=((heads, n_blocks, LINE, LINE), F32),
        score_in=((2, n_blocks, LINE, LINE), F32),
        score_sum=((n_blocks, LINE, LINE), F32),
        decay=((n_blocks, LINE, LINE), F32),
        weight=((n_blocks, LINE, LINE), F32),
        share=((heads, n_blocks, LINE, LINE), BF),
        inv=((rows, 128), F32),
        sign=((rows, 128), F32),
        hidden=((rows, local), F32),
        moment_box=((4, 8, rows), F32),
        head_rstd=((heads, rows, 128), F32),
        head_mean=((heads, rows, 128), F32),
        gate_low=((rows, local), BF),
        out=((4, rows, wide_d), BF),
        into=((4, rows, wide_d), BF),
        acc=((4, rows, wide_d), F32),
        small_out=((6 * GROUPS, half // GROUPS, wide_d), BF),
        small_in=((6 * GROUPS, half // GROUPS, wide_d), BF),
        loss_part=((8, 128), F32),
        goal=((rows, wide_d), BF),
        result=((rows, wide_d), BF),
        own_gradient=((rows, wide_d), BF),
        sent_out=((rows, wide_d), BF),
        home_out=((rows, wide_d), BF),
        home_grad=((rows, wide_d), BF),
        mixed_all=((n_dp, rows, local), BF),
        cols_out=((n_dp, rows // 8, block), BF),
        cols=((8, n_dp * rows // 8, block), BF),
        low_sum=((48, local), F32),
        low_box=((n_dp, 48, local), BF),
        ring_gate=((heads,) + turns + (block, chan), BF),
        ring_cell=((heads,) + turns + (block, chan), BF),
        g_gate=((rows, local), BF),
        g_cell=((rows, local), BF),
        small=((8, local), F32),
        small_box=((n_dp, 8, local), F32),
        g_act=((rows, local), F32),
        u_box=((4, 8, rows), F32),
        d_hidden=((rows, local), BF),
        share_out=((n_blocks, LINE, LINE), BF),
        share_in=((n_blocks, LINE, LINE), BF),
        lines=((8, rows), F32),
        d_score=((heads, n_blocks, LINE, LINE), BF),
        grad_box=((4, 8, rows), F32),
        g_proj=((rows, 3 * local), F32),
        line_box=((8, 8, rows), F32),
        loss_box=((8, 8, 128), F32),
    )
    vmem = pl.BlockSpec(memory_space=pltpu.VMEM)
    spaces = {name: pl.BlockSpec(memory_space=pl.ANY) for name in inputs if name[:4] == "own_"}
    spaces["lengths"] = pl.BlockSpec(memory_space=pltpu.SMEM)
    names = list(inputs) + list(outputs) + list(scratch) + ["send_sem", "recv_sem", "local_sem"]
    results = pl.pallas_call(
        lambda *refs: kernel(names, (rows, local, chan, n_dp, block, wide_d), limit, *refs),
        out_shape=[jax.ShapeDtypeStruct(*spec) for spec in outputs.values()],
        in_specs=[spaces.get(name, vmem) for name in inputs],
        out_specs=[vmem] * len(outputs),
        scratch_shapes=[pltpu.VMEM(*spec) for spec in scratch.values()]
        + [pltpu.SemaphoreType.DMA((limit,)), pltpu.SemaphoreType.DMA((limit,))]
        + [pltpu.SemaphoreType.DMA((3,))],
        compiler_params=pltpu.CompilerParams(
            collective_id=0, has_side_effects=True, vmem_limit_bytes=VMEM_LIMIT
        ),
    )(*inputs.values())
    results = pl.pallas_call(
        carry_out,
        out_shape=[jax.ShapeDtypeStruct(*spec) for spec in outputs.values()],
        in_specs=[pl.BlockSpec(memory_space=pl.ANY)] * len(outputs),
        out_specs=[vmem] * len(outputs),
        scratch_shapes=[pltpu.SemaphoreType.DMA((len(outputs),))],
    )(*results)
    o = types.SimpleNamespace(**dict(zip(outputs, results)))
    return (
        o.output,
        o.loss.reshape(()),
        o.grad_input,
        o.grad_ln.reshape(-1),
        o.grad_up,
        o.grad_conv_weight,
        o.grad_conv_bias,
        o.grad_qkv,
        o.grad_gate_weight,
        o.grad_gate_bias,
        o.grad_group,
        o.grad_skip,
        o.grad_down.reshape(down_weight.shape),
    )


def solution(mesh):
    return jax.shard_map(
        shards,
        mesh=mesh,
        in_specs=(
            P("dp", ("tensor", "ctx")),
            P("dp", ("tensor", "ctx")),
            P(("tensor", "ctx")),
            P("dp", None, "ctx", "tensor"),
            P(None, "ctx", "tensor"),
            P("ctx", "tensor"),
            P(None, None, "ctx", "tensor"),
            P(None, None, None, "ctx", "tensor"),
            P(),
            P("ctx", "tensor"),
            P("ctx", "tensor"),
            P("ctx", "tensor", "dp"),
            P(),
            P(),
            P("dp"),
        ),
        out_specs=(
            P("dp", ("tensor", "ctx")),
            P(),
            P("dp", ("tensor", "ctx")),
            P(("tensor", "ctx")),
            P("dp", None, "ctx", "tensor"),
            P(None, "ctx", "tensor"),
            P("ctx", "tensor"),
            P(None, None, "ctx", "tensor"),
            P(None, None, None, "ctx", "tensor"),
            P(),
            P("ctx", "tensor"),
            P("ctx", "tensor"),
            P("ctx", "tensor", "dp"),
        ),
        check_vma=False,
    )
```
